128 devices in a mesh: seq: 32 (over x, y, core), head: 4 (over z).
Axes of the slice: x: 4, y: 4, z: 4, core: 2. Of those that a mesh axis runs over, the one named last changes fastest.
Arguments:
- normed: bfloat16 [8192, 2560], P('seq'), may hold values from -6 to 6
- w_x: bfloat16 [2560, 5120], P(None, 'head'), may hold values from -0.125 to 0.125
- w_bc: bfloat16 [2560, 256], replicated, may hold values from -0.125 to 0.125
- conv_w: float32 [4, 5120], P(None, 'head'), may hold values from -3 to 3
- decay_code: int32 [80], P('head'), may hold values from 0 to 255, as said below
- step: float32 [80, 8192], P('head', 'seq'), may hold values from 0.0001 to 10000
- d_skip: float32 [80], P('head'), may hold values from 0.5 to 2
- grad_y: bfloat16 [8192, 5120], P('seq', 'head'), may hold values from -6 to 6
Outputs:
- grad_u: bfloat16 [2560, 8192], P('head', 'seq')
- grad_wx: float32 [2560, 5120], P('seq', 'head')
- grad_wbc: float32 [2560, 256], P('seq')
- grad_log_step: float32 [80, 8192], P('head', 'seq')
The draws below stay inside these ranges and needn't reach their ends.
Inputs may be any that keep to these rules, and one draw needn't show every extreme that they name: `decay_code`: the same codes are used for every token.
All inputs are finite; a program needn't handle non-finite values.
Results may differ from the reference program's by a relative error of at most 0.0056.
Values may be sent and summed in bfloat16 or wider, within the bound.
No kernel may reach another device: no remote copies, remote signals or barrier semaphores. Data moves between devices by JAX's collectives and lax.ppermute only.
A program may use at most 128 MiB of HBM per device.

```python
import math
import jax
import jax.numpy as jnp
from jax import lax

D = 2560
HEAD_COUNT = 80
HEAD_DIM = 64
STATE = 128
GROUP = 256
CONV = 4
LEVELS = 256
T_DEV = 256
TOKEN_COUNT = 8192


def shared_codes(key):
    return jax.random.randint(jax.random.fold_in(key, 7), (HEAD_COUNT,), 0, LEVELS)


def draw_decay_code(key, part):
    return shared_codes(key).astype(jnp.int32)


def draw_step(key, part):
    codes = shared_codes(key)
    key = jax.random.fold_in(key, 3)
    random_keys = jax.random.split(key, 7)
    low = math.log(0.995)
    high = math.log(0.9999)
    rate = -(low + codes.astype(jnp.float32) / (LEVELS - 1) * (high - low))
    share = 0.5
    fast = jax.random.uniform(random_keys[0], (HEAD_COUNT,)) < share
    fast_rho = jnp.exp(jax.random.uniform(random_keys[1], (HEAD_COUNT,), minval=math.log(1.0 / 50.0), maxval=math.log(1.0 / 30.0)))
    slow_rho = jnp.exp(jax.random.uniform(random_keys[2], (HEAD_COUNT,), minval=math.log(0.2), maxval=math.log(0.6))) / TOKEN_COUNT
    decay_factor = jnp.where(fast, fast_rho, slow_rho)
    jagged_input = jnp.exp(jax.random.uniform(random_keys[3], (HEAD_COUNT, TOKEN_COUNT), minval=math.log(0.7), maxval=math.log(1.4)))
    blocks = TOKEN_COUNT // T_DEV
    block_factor = jnp.exp(jax.random.uniform(random_keys[4], (HEAD_COUNT, blocks), minval=math.log(0.5), maxval=math.log(1.5)))
    block_factor = jnp.repeat(block_factor, T_DEV, axis=1)
    spike_index = jax.random.randint(random_keys[5], (HEAD_COUNT, 2), 0, TOKEN_COUNT)
    spike_length = jax.random.uniform(random_keys[6], (HEAD_COUNT, 2), minval=0.2, maxval=0.5)
    token_positions = jnp.arange(TOKEN_COUNT)
    spike_value = jnp.sum(jnp.where(token_positions[None, None, :] == spike_index[:, :, None], spike_length[:, :, None], 0.0), axis=1)
    dropout_fraction = decay_factor[:, None] * jagged_input * block_factor + spike_value
    return (dropout_fraction / rate[:, None]).astype(jnp.float32)


def with_spikes(drawn, own_key, source, target, parts, factor):
    owner, partner = [(jnp.arange(drawn.shape[dim]) // (drawn.shape[dim] // parts)).reshape([-1 if axis == dim else 1 for axis in range(drawn.ndim)]) for dim in (source, target)]
    chosen = jax.random.permutation(own_key, parts)[partner]
    strong = (owner == chosen) | (owner == (partner + parts // 2) % parts)
    return jnp.where(strong, factor * drawn, drawn)


def block_levels(stream_key, shape, shards, smallest, top_value):
    level, own = 1.0, jax.random.fold_in(stream_key, 6)
    for dim, parts in shards:
        draws = jnp.exp(jax.random.uniform(jax.random.fold_in(own, dim), (parts,), jnp.float32, smallest / len(shards), top_value / len(shards)))
        level = level * jnp.repeat(draws, shape[dim] // parts).reshape([-1 if axis == dim else 1 for axis in range(len(shape))])
    return level


def bell_draw(key, dims, spread, reach, cuts=(), dtype=jnp.bfloat16):
    drawn = spread * jax.random.normal(key, dims, jnp.float32)
    if cuts:
        drawn = drawn * block_levels(key, dims, cuts, -0.22, 0.18)
    return jnp.clip(drawn, -reach, reach).astype(dtype)


def heavy_noise(own_key, dims, deviation, most, shards, heavy, kind=jnp.bfloat16):
    array = deviation * jax.random.normal(own_key, dims, jnp.float32)
    if shards:
        array = array * block_levels(own_key, dims, shards, -0.22, 0.18)
    return jnp.clip(with_spikes(array, jax.random.fold_in(own_key, 3), *heavy), -most, most).astype(kind)


def setup_inputs(seed: int = 0) -> dict:
    key_list = jax.random.split(jax.random.key(seed), 9)
    normed = heavy_noise(key_list[0], (TOKEN_COUNT, D), 1.0, 6.0, ((0, 32),), (0, 1, 32, 2.75))
    w_x = bell_draw(key_list[1], (D, HEAD_COUNT * HEAD_DIM), D ** -0.5, 0.125, ((1, 4),))
    w_bc = bell_draw(key_list[2], (D, 2 * STATE), D ** -0.5, 0.125)
    conv_w = bell_draw(key_list[3], (CONV, HEAD_COUNT * HEAD_DIM), 0.5, 3.0, ((1, 4),), jnp.float32)
    decay_code = draw_decay_code(jax.random.fold_in(key_list[8], 71), 0)
    step = draw_step(jax.random.fold_in(key_list[8], 71), 0)
    d_skip = jnp.clip(jnp.exp(math.log(2.0) - 1.3862944 * jax.random.uniform(key_list[6], (HEAD_COUNT,), jnp.float32) ** block_levels(key_list[6], (HEAD_COUNT,), ((0, 4),), -0.2, 0.2)), 0.5, 2.0)
    grad_y = bell_draw(key_list[7], (TOKEN_COUNT, HEAD_COUNT * HEAD_DIM), 1.0, 6.0, ((0, 32), (1, 4)))
    return dict(normed=normed, w_x=w_x, w_bc=w_bc, conv_w=conv_w, decay_code=decay_code, step=step, d_skip=d_skip, grad_y=grad_y)


HIGH = lax.Precision.HIGHEST

def head_rates(codes):
    low = math.log(0.995)
    high = math.log(0.9999)
    return low + codes.astype(jnp.float32) / (LEVELS - 1) * (high - low)

def group_pass(state, pieces):
    xs, bq, cq, lq, gq = pieces
    scale = STATE ** (-0.5)
    cum = jnp.cumsum(lq, axis=1)
    size = lq.shape[1]
    mask = jnp.arange(size)[:, None] >= jnp.arange(size)[None, :]
    diff = cum[:, :, None] - cum[:, None, :]
    lmat = jnp.where(mask, jnp.exp(jnp.where(mask, diff, 0.0)), 0.0)
    gram = jnp.dot(cq, bq.T, precision=HIGH) * scale
    xg = xs * gq.T[:, :, None]
    y_intra = jnp.einsum('hij,jhp->ihp', lmat * gram[None], xg, precision=HIGH)
    y_inter = jnp.einsum('hpn,in->ihp', state, cq, precision=HIGH) * (jnp.exp(cum).T * scale)[:, :, None]
    tail = jnp.exp(cum[:, -1:] - cum)
    carried = jnp.exp(cum[:, -1])[:, None, None] * state
    fresh = jnp.einsum('jhp,jn->hpn', xg * tail.T[:, :, None], bq, precision=HIGH)
    return (carried + fresh, y_intra + y_inter)

def state_space(x3, bmat, cmat, logd, gain, state):
    length, heads, width = x3.shape
    count = length // GROUP
    xs = x3.reshape(count, GROUP, heads, width)
    bs = bmat.reshape(count, GROUP, STATE)
    cs = cmat.reshape(count, GROUP, STATE)
    ls = logd.reshape(heads, count, GROUP).transpose(1, 0, 2)
    gs = gain.reshape(heads, count, GROUP).transpose(1, 0, 2)
    final, ys = lax.scan(jax.checkpoint(group_pass), state, (xs, bs, cs, ls, gs))
    return (final, ys.reshape(length, heads, width))

def mixer(x_act, shared, step, rates, d_skip, state):
    length = x_act.shape[0]
    heads = step.shape[0]
    x3 = x_act.reshape(length, heads, HEAD_DIM)
    logd = rates[:, None] * step
    gain = jnp.sqrt(-2.0 * logd)
    final, y3 = state_space(x3, shared[:, :STATE], shared[:, STATE:], logd, gain, state)
    y3 = y3 + d_skip[None, :, None] * x3
    return (y3.reshape(length, heads * HEAD_DIM), final)

def conv_forward(x_pre, conv_w, before):
    length = x_pre.shape[0]
    ext = jnp.concatenate([before, x_pre], axis=0).astype(jnp.float32)
    total = conv_w[0] * ext[CONV - 1:CONV - 1 + length]
    for tap in range(1, CONV):
        total = total + conv_w[tap] * ext[CONV - 1 - tap:CONV - 1 - tap + length]
    return total

def conv_backward(dxc, conv_w, after):
    length = dxc.shape[0]
    ext = jnp.concatenate([dxc, after], axis=0)
    total = conv_w[0] * ext[0:length]
    for tap in range(1, CONV):
        total = total + conv_w[tap] * ext[tap:tap + length]
    return total

def silu_grad(xc):
    sig = jax.nn.sigmoid(xc)
    return sig * (1.0 + xc * (1.0 - sig))

def reference(normed, w_x, w_bc, conv_w, decay_code, step, d_skip, grad_y):
    x_pre = jnp.dot(normed, w_x, preferred_element_type=jnp.float32).astype(jnp.bfloat16)
    channels = x_pre.shape[1]
    xc = conv_forward(x_pre, conv_w, jnp.zeros((CONV - 1, channels), jnp.bfloat16))
    x_act = jax.nn.silu(xc)
    shared = jnp.dot(normed, w_bc, preferred_element_type=jnp.float32)
    rates = head_rates(decay_code)
    start = jnp.zeros((HEAD_COUNT, HEAD_DIM, STATE), jnp.float32)

    def forward(x_act, shared, step):
        return mixer(x_act, shared, step, rates, d_skip, start)
    (outputs, final), pull = jax.vjp(forward, x_act, shared, step)
    d_x, d_bc, d_step = pull((grad_y.astype(jnp.float32), jnp.zeros_like(final)))
    d_shared = d_bc.astype(jnp.bfloat16)
    dxc = d_x * silu_grad(xc)
    d_pre = conv_backward(dxc, conv_w, jnp.zeros((CONV - 1, channels), jnp.float32)).astype(jnp.bfloat16)
    contract = (((1,), (1,)), ((), ()))
    grad_u = lax.dot_general(w_x, d_pre, contract, preferred_element_type=jnp.float32)
    grad_u = grad_u + lax.dot_general(w_bc, d_shared, contract, preferred_element_type=jnp.float32)
    norm = TOKEN_COUNT ** (-0.5)
    over_tokens = (((0,), (0,)), ((), ()))
    grad_wx = lax.dot_general(normed, d_pre, over_tokens, preferred_element_type=jnp.float32) * norm
    grad_wbc = lax.dot_general(normed, d_shared, over_tokens, preferred_element_type=jnp.float32) * norm
    grad_log_step = step * d_step
    return (grad_u.astype(jnp.bfloat16), grad_wx, grad_wbc, grad_log_step)
```

```python
import functools
import math

import jax
import jax.numpy as jnp
import numpy as np
from jax import lax
from jax.experimental import pallas as pl
from jax.experimental.pallas import tpu as pltpu
from jax.sharding import PartitionSpec as P

D = 2560
HEAD_DIM = 64
STATE = 128
CONV = 4
LEVELS = 256
T = 256
CH = 1280
HEADS = 20
SEQ = 32
ZS = 4
ROWS = 80
SLICE = 40
MSG = 48
BLK = 256
NBLK = CH // BLK
SCALE = STATE ** (-0.5)
F32 = jnp.float32
BF16 = jnp.bfloat16
HIGH = lax.Precision.HIGHEST
NT = (((1,), (1,)), ((), ()))
VMEM = 56 * 2**20


def nt(a, b):
    return lax.dot_general(a, b, NT, preferred_element_type=F32)


def nn(a, b):
    return jnp.dot(a, b, preferred_element_type=F32)


def split(value):
    high = value.astype(BF16)
    return high, (value - high.astype(F32)).astype(BF16)


def wide(dot, a, b):
    a_high, a_low = split(a)
    b_high, b_low = split(b)
    return dot(a_high, b_high) + (dot(a_low, b_high) + dot(a_high, b_low))


def params():
    return pltpu.CompilerParams(vmem_limit_bytes=VMEM)


def cost(flops, nbytes, trans=0):
    return pl.CostEstimate(flops=flops, bytes_accessed=nbytes, transcendentals=trans)


def whole(*shape):
    return pl.BlockSpec(shape, lambda i: (0,) * len(shape))


def triangle(upper):
    row = lax.broadcasted_iota(jnp.int32, (T, T), 0)
    col = lax.broadcasted_iota(jnp.int32, (T, T), 1)
    return jnp.where(row <= col if upper else row >= col, 1.0, 0.0).astype(F32)


def front_kernel(normed, w_bc, rates, step, grad_y, bmat, cmat, cum, logd, dyt, dywt, msg, pulled, turn):
    shared = nn(normed[...], w_bc[...])
    bmat[...] = shared[:, :STATE]
    cmat[...] = shared[:, STATE:]
    c_high, c_low = split(shared[:, STATE:])
    logs = rates[...] * step[...]
    logd[...] = logs
    cums = jnp.dot(logs, triangle(True), precision=HIGH, preferred_element_type=F32)
    cum[...] = cums
    grown = jnp.exp(cums)
    weight = grown * SCALE
    for pair in range(HEADS // 2):
        rows = slice(128 * pair, 128 * pair + 128)
        tile = grad_y[:, rows].astype(F32).T
        dyt[rows, :] = tile.astype(BF16)
        tile = jnp.concatenate(
            [
                tile[:64] * weight[2 * pair : 2 * pair + 1],
                tile[64:] * weight[2 * pair + 1 : 2 * pair + 2],
            ],
            axis=0,
        )
        high, low = split(tile)
        dywt[rows, :] = high
        pulled[rows, :] = nn(high, c_high) + (nn(low, c_high) + nn(high, c_low))
    turn[...] = jnp.zeros((128, 128), F32)
    turn[:HEADS, :] = grown[:, 128:]
    through = jnp.broadcast_to(turn[...].T[127:, :], (MSG - SLICE, STATE))
    for k in range(SEQ):
        msg[k, :SLICE, :] = pulled[SLICE * k : SLICE * (k + 1), :]
        msg[k, SLICE:, :] = through


def front(normed, w_bc, rates, step, grad_y):
    return pl.pallas_call(
        front_kernel,
        out_shape=(
            jax.ShapeDtypeStruct((T, STATE), F32),
            jax.ShapeDtypeStruct((T, STATE), F32),
            jax.ShapeDtypeStruct((HEADS, T), F32),
            jax.ShapeDtypeStruct((HEADS, T), F32),
            jax.ShapeDtypeStruct((CH, T), BF16),
            jax.ShapeDtypeStruct((CH, T), BF16),
            jax.ShapeDtypeStruct((SEQ, MSG, STATE), F32),
        ),
        scratch_shapes=[pltpu.VMEM((CH, STATE), F32), pltpu.VMEM((128, 128), F32)],
        compiler_params=params(),
        cost_estimate=cost(2 * T * D * 256 + 6 * CH * T * 128, 6 * 2**20),
    )(normed, w_bc, rates, step, grad_y)


def chain_kernel(reverse, table, recv, decays, tie, out, turn):
    del tie
    lanes = jnp.concatenate([decays[:, 0, :], jnp.zeros((128 - SEQ, 128), F32)], axis=0)
    turn[...] = lanes.T
    head = table[32]
    row = lax.broadcasted_iota(jnp.int32, (SLICE, 128), 0)
    cols = jnp.where(row < table[33], turn[pl.ds(head, 1), :], turn[pl.ds(head + 1, 1), :])
    state = jnp.zeros((SLICE, STATE), F32)
    for k in range(SEQ - 1, -1, -1) if reverse else range(SEQ):
        out[k] = state
        state = cols[:, k : k + 1] * state + recv[k]


def chain(table, recv, pulls, tie, reverse):
    return pl.pallas_call(
        functools.partial(chain_kernel, reverse),
        grid=(1,),
        in_specs=[
            pl.BlockSpec(memory_space=pltpu.SMEM),
            whole(SEQ, SLICE, STATE),
            pl.BlockSpec((SEQ, MSG - SLICE, STATE), lambda i: (0, SLICE // 8, 0)),
            pl.BlockSpec(memory_space=pl.ANY),
        ],
        out_specs=whole(SEQ, SLICE, STATE),
        out_shape=jax.ShapeDtypeStruct((SEQ, SLICE, STATE), F32),
        scratch_shapes=[pltpu.VMEM((128, 128), F32)],
        compiler_params=params(),
        cost_estimate=cost(10**6, 2 * 2**20),
    )(table, recv, pulls, tie)


def channel_kernel(before, normed, w_x, conv_w, cum, logd, bmat, xgt, sgt, xwt, own, ext, pre):
    step = pl.program_id(0)

    @pl.when(step == 0)
    def _():
        ext[:16, :] = before[...]
        ext[16:, :] = normed[...]

    now = lax.rem(step, 2)
    past = pre.at[1 - now]
    total = conv_w[0:1, :] * past[16 : 16 + T, :]
    for tap in range(1, CONV):
        total = total + conv_w[tap : tap + 1, :] * past[16 - tap : 16 - tap + T, :]
    sig = 1.0 / (1.0 + jnp.exp(-total))
    xt = (total * sig).T
    sgt[...] = (sig * (1.0 + total * (1.0 - sig))).T
    parts = []
    block = jnp.maximum(step - 1, 0)
    for q in range(BLK // HEAD_DIM):
        head = pl.ds(block * (BLK // HEAD_DIM) + q, 1)
        rows = slice(64 * q, 64 * q + 64)
        gain = jnp.sqrt(-2.0 * logd[head, :])
        cums = cum[head, :]
        tail = jnp.exp(cums[:, T - 1 :] - cums)
        xg = xt[rows] * gain
        xgt[rows, :] = xg.astype(BF16)
        parts.append(xg * tail)
    weighted = jnp.concatenate(parts, axis=0)
    xwt[...] = weighted.astype(BF16)
    own[...] = wide(nn, weighted, bmat[...])
    pre[now] = nn(ext[...], w_x[...]).astype(BF16).astype(F32)


def channels(before, normed, w_x, conv_w, cum, logd, bmat):
    def late(i):
        return jnp.maximum(i - 1, 0)

    rows = pl.BlockSpec((BLK, T), lambda i: (late(i), 0))
    return pl.pallas_call(
        channel_kernel,
        grid=(NBLK + 1,),
        in_specs=[
            whole(16, D),
            whole(T, D),
            pl.BlockSpec((D, BLK), lambda i: (0, jnp.minimum(i, NBLK - 1))),
            pl.BlockSpec((CONV, BLK), lambda i: (0, late(i))),
            whole(HEADS, T),
            whole(HEADS, T),
            whole(T, STATE),
        ],
        out_specs=(rows, rows, rows, pl.BlockSpec((BLK, STATE), lambda i: (late(i), 0))),
        out_shape=(
            jax.ShapeDtypeStruct((CH, T), BF16),
            jax.ShapeDtypeStruct((CH, T), F32),
            jax.ShapeDtypeStruct((CH, T), BF16),
            jax.ShapeDtypeStruct((CH, STATE), F32),
        ),
        scratch_shapes=[pltpu.VMEM((T + 16, D), BF16), pltpu.VMEM((2, T + 16, BLK), F32)],
        compiler_params=params(),
        cost_estimate=cost(2 * T * D * CH, 10 * 2**20, T * CH),
    )(before, normed, w_x, conv_w, cum, logd, bmat)


def intra_kernel(grad_y, dyt, xgt, cum, bmat, cmat, tie, dxg, rc, dbc, gram, dgram):
    del tie
    step = pl.program_id(0)

    @pl.when(step == 0)
    def _():
        gram[...] = wide(nt, cmat[...], bmat[...]) * SCALE
        dgram[...] = jnp.zeros((T, T), F32)

    half = T // 2
    row = lax.broadcasted_iota(jnp.int32, (half, half), 0)
    col = lax.broadcasted_iota(jnp.int32, (half, half), 1)
    keep = row >= col
    blank = jnp.zeros((HEAD_DIM, T), BF16)
    corner = jnp.zeros((half, half), BF16)
    for q in range(BLK // HEAD_DIM):
        head = pl.ds(step * (BLK // HEAD_DIM) + q, 1)
        rows = slice(64 * q, 64 * q + 64)
        cums = cum[head, :]
        column = jnp.broadcast_to(cums, (half, T)).T
        l00 = jnp.exp(jnp.where(keep, column[:half] - cums[:, :half], -1e30))
        l10 = jnp.exp(column[half:] - cums[:, :half])
        l11 = jnp.exp(jnp.where(keep, column[half:] - cums[:, half:], -1e30))
        m00 = (l00 * gram[:half, :half]).astype(BF16)
        m10 = (l10 * gram[half:, :half]).astype(BF16)
        m11 = (l11 * gram[half:, half:]).astype(BF16)
        mat = jnp.concatenate(
            [jnp.concatenate([m00, corner], axis=1), jnp.concatenate([m10, m11], axis=1)], axis=0
        )
        dy = dyt[rows, :]
        xg = xgt[rows, :]
        pair = slice(128 * (q // 2), 128 * (q // 2) + 128)
        right = jnp.concatenate([xg, blank] if q % 2 == 0 else [blank, xg], axis=0)
        dm0 = nn(grad_y[:, pair], right[:, :half])
        dm1 = nn(grad_y[half:, pair], right[:, half:])
        dgram[:half, :half] += l00 * dm0[:half]
        dgram[half:, :half] += l10 * dm0[half:]
        dgram[half:, half:] += l11 * dm1
        back = nn(dy, mat)
        yin = nt(xg, mat)
        dxg[rows, :] = back
        rc[head, :] = jnp.sum(dy.astype(F32) * yin - xg.astype(F32) * back, axis=0, keepdims=True)

    @pl.when(step == NBLK - 1)
    def _():
        dg = (dgram[...] * SCALE).astype(BF16)
        dbc[:STATE, :] = nn(cmat[...].T.astype(BF16), dg)
        dbc[STATE:, :] = nn(dg, bmat[...].astype(BF16)).T


def intra(grad_y, dyt, xgt, cum, bmat, cmat, tie):
    rows = pl.BlockSpec((BLK, T), lambda i: (i, 0))
    return pl.pallas_call(
        intra_kernel,
        grid=(NBLK,),
        in_specs=[
            pl.BlockSpec((T, BLK), lambda i: (0, i)),
            rows,
            rows,
            whole(HEADS, T),
            whole(T, STATE),
            whole(T, STATE),
            pl.BlockSpec(memory_space=pl.ANY),
        ],
        out_specs=(rows, whole(HEADS, T), whole(2 * STATE, T)),
        out_shape=(
            jax.ShapeDtypeStruct((CH, T), F32),
            jax.ShapeDtypeStruct((HEADS, T), F32),
            jax.ShapeDtypeStruct((2 * STATE, T), F32),
        ),
        scratch_shapes=[pltpu.VMEM((T, T), F32), pltpu.VMEM((T, T), F32)],
        compiler_params=params(),
        cost_estimate=cost(HEADS * 2 * T * T * 64 * 8, 4 * 2**20, HEADS * T * T),
    )(grad_y, dyt, xgt, cum, bmat, cmat, tie)


def grad_kernel(
    skip, back, bmat, dxg, dyt, xgt, xwt, sgt, taps, cum, logd, tie, dpre, halo, halves, cross, dbt, ext
):
    del tie
    step = pl.program_id(0)

    @pl.when(step == 0)
    def _():
        dbt[...] = jnp.zeros((STATE, T), F32)

    own = back[...]
    later = wide(nt, own, bmat[...])
    dbt[...] += nn(own.T.astype(BF16), xwt[...])
    parts = []
    for q in range(BLK // HEAD_DIM):
        index = step * (BLK // HEAD_DIM) + q
        head = pl.ds(index, 1)
        rows = slice(64 * q, 64 * q + 64)
        gain = jnp.sqrt(-2.0 * logd[head, :])
        cums = cum[head, :]
        tail = jnp.exp(cums[:, T - 1 :] - cums)
        inter = later[rows] * tail
        whole_dxg = dxg[rows, :] + inter
        xg = xgt[rows, :].astype(F32)
        cross[head, :] = jnp.sum(xg * inter, axis=0, keepdims=True)
        halves[head, :] = 0.5 * jnp.sum(xg * whole_dxg, axis=0, keepdims=True)
        d_x = gain * whole_dxg + skip[index] * dyt[rows, :].astype(F32)
        parts.append(d_x * sgt[rows, :])
    ext[:8, :] = jnp.zeros((8, BLK), F32)
    ext[8 : T + 8, :] = jnp.concatenate(parts, axis=0).T
    ext[T + 8 :, :] = jnp.zeros((8, BLK), F32)
    total = taps[0:1, :] * ext[8 : T + 8, :]
    edge = taps[0:1, :] * ext[:8, :]
    for tap in range(1, CONV):
        weight = taps[tap : tap + 1, :]
        total = total + weight * ext[8 + tap : T + 8 + tap, :]
        edge = edge + weight * ext[tap : 8 + tap, :]
    dpre[...] = total.astype(BF16)
    halo[...] = edge


def gradients(skip, back, bmat, dxg, dyt, xgt, xwt, sgt, taps, cum, logd, tie):
    rows = pl.BlockSpec((BLK, T), lambda i: (i, 0))
    return pl.pallas_call(
        grad_kernel,
        grid=(NBLK,),
        in_specs=[
            pl.BlockSpec(memory_space=pltpu.SMEM),
            pl.BlockSpec((BLK, STATE), lambda i: (i, 0)),
            whole(T, STATE),
            rows,
            rows,
            rows,
            rows,
            rows,
            pl.BlockSpec((CONV, BLK), lambda i: (0, i)),
            whole(HEADS, T),
            whole(HEADS, T),
            pl.BlockSpec(memory_space=pl.ANY),
        ],
        out_specs=(
            pl.BlockSpec((T, BLK), lambda i: (0, i)),
            pl.BlockSpec((8, BLK), lambda i: (0, i)),
            whole(HEADS, T),
            whole(HEADS, T),
            whole(STATE, T),
        ),
        out_shape=(
            jax.ShapeDtypeStruct((T, CH), BF16),
            jax.ShapeDtypeStruct((8, CH), F32),
            jax.ShapeDtypeStruct((HEADS, T), F32),
            jax.ShapeDtypeStruct((HEADS, T), F32),
            jax.ShapeDtypeStruct((STATE, T), F32),
        ),
        scratch_shapes=[pltpu.VMEM((T + 16, BLK), F32)],
        compiler_params=params(),
        cost_estimate=cost(4 * CH * T * 128, 6 * 2**20, T * HEADS),
    )(skip, back, bmat, dxg, dyt, xgt, xwt, sgt, taps, cum, logd, tie)


def state_kernel(
    fore, back, cmat, dyt, dywt, cum, logd, rc, halves, cross, dbt, dbc, gls, shared
):
    state = fore[...]
    before = wide(nt, state, cmat[...])
    dct = nn(state.T.astype(BF16), dywt[...])
    cums = cum[...]
    inner = []
    through = []
    for h in range(HEADS):
        rows = slice(64 * h, 64 * h + 64)
        inner.append(jnp.sum(dyt[rows, :].astype(F32) * before[rows], axis=0, keepdims=True))
        both = jnp.sum(fore[rows, :] * back[rows, :], axis=0, keepdims=True)
        through.append(jnp.sum(both, axis=1, keepdims=True))
    arriving = rc[...] + jnp.exp(cums) * SCALE * jnp.concatenate(inner, axis=0)
    later = jnp.dot(arriving, triangle(False), precision=HIGH, preferred_element_type=F32)
    crossing = cross[...]
    earlier = (
        jnp.dot(crossing, triangle(True), precision=HIGH, preferred_element_type=F32) - crossing
    )
    kept = jnp.exp(cums[:, T - 1 :]) * jnp.concatenate(through, axis=0)
    gls[...] = logd[...] * (later + earlier + kept) + halves[...]
    total = dbc[...] + jnp.concatenate([dbt[...], dct], axis=0)
    shared[...] = total.T.astype(BF16)


def states(fore, back, cmat, dyt, dywt, cum, logd, rc, halves, cross, dbt, dbc):
    vm = pl.BlockSpec(memory_space=pltpu.VMEM)
    return pl.pallas_call(
        state_kernel,
        in_specs=[vm] * 12,
        out_shape=(
            jax.ShapeDtypeStruct((HEADS, T), F32),
            jax.ShapeDtypeStruct((T, 2 * STATE), BF16),
        ),
        compiler_params=params(),
        cost_estimate=cost(4 * CH * T * 128, 4 * 2**20),
    )(fore, back, cmat, dyt, dywt, cum, logd, rc, halves, cross, dbt, dbc)


def select_kernel(order, normed, tie, mine, other, flip):
    del tie
    for k in range(D // 128):
        cols = slice(128 * k, 128 * k + 128)
        flip[cols, :] = normed[:, cols].astype(F32).T.astype(BF16)
    for k in range(16):
        rows = slice(ROWS * k, ROWS * (k + 1))
        mine[rows, :] = flip[pl.ds(pl.multiple_of(order[k] * ROWS, 16), ROWS), :]
        other[rows, :] = flip[pl.ds(pl.multiple_of(order[16 + k] * ROWS, 16), ROWS), :]


def select(order, normed, tie):
    vm = pl.BlockSpec(memory_space=pltpu.VMEM)
    return pl.pallas_call(
        select_kernel,
        in_specs=[pl.BlockSpec(memory_space=pltpu.SMEM), vm, pl.BlockSpec(memory_space=pl.ANY)],
        out_shape=(jax.ShapeDtypeStruct((CH, T), BF16), jax.ShapeDtypeStruct((CH, T), BF16)),
        scratch_shapes=[pltpu.VMEM((D, T), BF16)],
        compiler_params=params(),
        cost_estimate=cost(10**6, 3 * 2**20),
    )(order, normed, tie)


PART = [slice(320 * r, 320 * (r + 1)) for r in range(4)]
WIDE = 640
FULL = WIDE + STATE
MAIN = [slice(0, WIDE), slice(WIDE, 2 * WIDE)]
EXTRA = [slice(0, STATE), slice(STATE, 2 * STATE)]


def mended(grad, halo, cols):
    edge = jnp.concatenate([jnp.zeros((8, WIDE), F32), halo[:, cols]], axis=0)
    return grad[: T - 16, cols], (grad[T - 16 :, cols].astype(F32) + edge).astype(BF16)


def product(refs, side):
    mine, other, grad, grad_other, halo, halo_other, shared, shared_other = refs
    cols = MAIN[side]
    right = jnp.concatenate(
        mended(grad, halo, cols) + mended(grad_other, halo_other, cols), axis=0
    )
    extra = jnp.concatenate([shared[:, EXTRA[side]], shared_other[:, EXTRA[side]]], axis=0)

    def rows(part):
        left = jnp.concatenate([mine[PART[part], :], other[PART[part], :]], axis=1)
        return nn(left, right), nn(left, extra)

    return rows


def up_kernel(*refs):
    up = refs[8]
    for at, (part, side) in enumerate(((2, 0), (1, 1))):
        main, extra = product(refs[:8], side)(part)
        up[PART[at], :WIDE] = main.astype(BF16)
        up[PART[at], WIDE:] = extra.astype(BF16)


def down_kernel(*refs):
    down = refs[9]
    for at, (part, side) in enumerate(((2, 1), (3, 0))):
        main, extra = product(refs[:8], side)(part)
        down[PART[at], :WIDE] = main.astype(BF16)
        down[PART[at], WIDE:] = extra.astype(BF16)


def keep_kernel(*refs):
    for out, (part, side) in zip(refs[9:], ((1, 0), (3, 1), (0, 0), (0, 1))):
        main, extra = product(refs[:8], side)(part)
        out[:, :WIDE] = main
        out[:, WIDE:] = extra


def up_part(args):
    return pl.pallas_call(
        up_kernel,
        out_shape=jax.ShapeDtypeStruct((640, FULL), BF16),
        compiler_params=params(),
        cost_estimate=cost(2 * 512 * FULL * 640, 4 * 2**20),
    )(*args)


def down_part(args, tie):
    vm = pl.BlockSpec(memory_space=pltpu.VMEM)
    return pl.pallas_call(
        down_kernel,
        in_specs=[vm] * 8 + [pl.BlockSpec(memory_space=pl.ANY)],
        out_shape=jax.ShapeDtypeStruct((640, FULL), BF16),
        compiler_params=params(),
        cost_estimate=cost(2 * 512 * FULL * 640, 4 * 2**20),
    )(*args, tie)


def keep_part(args, tie):
    vm = pl.BlockSpec(memory_space=pltpu.VMEM)
    one = jax.ShapeDtypeStruct((320, FULL), F32)
    return pl.pallas_call(
        keep_kernel,
        in_specs=[vm] * 8 + [pl.BlockSpec(memory_space=pl.ANY)],
        out_shape=(one,) * 4,
        compiler_params=params(),
        cost_estimate=cost(2 * 512 * FULL * 1280, 8 * 2**20),
    )(*args, tie)


def input_kernel(w_x, w_bc, grad, halo, shared, tie, out):
    del tie
    edge = jnp.concatenate([jnp.zeros((8, CH), F32), halo[...]], axis=0)
    last = (grad[T - 16 :, :].astype(F32) + edge).astype(BF16)
    right = jnp.concatenate([grad[: T - 16, :], last], axis=0)
    out[...] = (nt(w_x[...], right) + nt(w_bc[...], shared[...])).astype(BF16)


def input_part(w_x, w_bc, grad, halo, shared, tie):
    rows = D // ZS
    return pl.pallas_call(
        input_kernel,
        grid=(ZS,),
        in_specs=[
            pl.BlockSpec((rows, CH), lambda i: (i, 0)),
            pl.BlockSpec((rows, 2 * STATE), lambda i: (i, 0)),
            whole(T, CH),
            whole(8, CH),
            whole(T, 2 * STATE),
            pl.BlockSpec(memory_space=pl.ANY),
        ],
        out_specs=pl.BlockSpec((rows, T), lambda i: (i, 0)),
        out_shape=jax.ShapeDtypeStruct((D, T), BF16),
        compiler_params=params(),
        cost_estimate=cost(2 * D * (CH + 256) * T, 10 * 2**20),
    )(w_x, w_bc, grad, halo, shared, tie)


def device(x, y, core):
    return ((x % 4) * 4 + y % 4) * 2 + core


def ring(first, by):
    pairs = []
    for x in range(4):
        for y in range(4):
            for core in range(2):
                along_x = (core == 0) == first
                goal = device(x + by, y, core) if along_x else device(x, y + by, core)
                pairs.append((device(x, y, core), goal))
    return pairs


def along(first, by):
    return lambda value: lax.ppermute(value, "seq", ring(first, by))


def ring_sum(move, up1, down1, near_up, near_down, here_a, here_b, size):
    from_up = move(1)(up1)
    from_down = move(-1)(down1)
    up2 = (near_up + from_up[:size].astype(F32)).astype(BF16)
    down2 = (near_down + from_down[:size].astype(F32)).astype(BF16)
    last_up = move(1)(up2)
    last_down = move(-1)(down2)
    total_a = here_a + from_down[size:].astype(F32) + last_up.astype(F32)
    total_b = here_b + from_up[size:].astype(F32) + last_down.astype(F32)
    return total_a, total_b


def place_table():
    rows = []
    for place in range(SEQ):
        core, y, x = place % 2, place // 2 % 4, place // 8
        blocks = [
            [device(x + a, y + b, 0) for a in range(4) for b in range(4)],
            [device(x + b, y + a, 1) for a in range(4) for b in range(4)],
        ]
        head = SLICE * place // HEAD_DIM
        bound = HEAD_DIM * (head + 1) - SLICE * place
        rows.append(blocks[core] + blocks[1 - core] + [head, bound])
    return np.array(rows, np.int32)


def body(normed, w_x, w_bc, conv_w, decay_code, step, d_skip, grad_y):
    place = lax.axis_index("seq")
    core = place % 2
    table = lax.dynamic_index_in_dim(jnp.asarray(place_table()), place, 0, keepdims=False)
    swap = [(i, i ^ 1) for i in range(SEQ)]

    low = math.log(0.995)
    high = math.log(0.9999)
    rates = low + decay_code.astype(F32)[:, None] / (LEVELS - 1) * (high - low)
    before = lax.ppermute(normed[T - 16 :], "seq", [(i, i + 1) for i in range(SEQ - 1)])

    bmat, cmat, cum, logd, dyt, dywt, msg = front(normed, w_bc, rates, step, grad_y)
    pulls = lax.all_to_all(msg, "seq", 0, 0)
    xgt, sgt, xwt, own = channels(before, normed, w_x, conv_w, cum, logd, bmat)
    ahead = lax.all_to_all(own.reshape(SEQ, SLICE, STATE), "seq", 0, 0)
    back_parts = chain(table, pulls, pulls, own, True)
    back = lax.all_to_all(back_parts, "seq", 0, 0).reshape(CH, STATE)
    dxg, rc, dbc = intra(grad_y, dyt, xgt, cum, bmat, cmat, back_parts)
    fore_parts = chain(table, ahead, pulls, rc, False)
    fore = lax.all_to_all(fore_parts, "seq", 0, 0).reshape(CH, STATE)

    dpre, halo, halves, cross, dbt = gradients(
        d_skip, back, bmat, dxg, dyt, xgt, xwt, sgt, conv_w, cum, logd, fore_parts
    )
    dpre_other = lax.ppermute(dpre, "seq", swap)
    halo_mine = lax.ppermute(halo, "seq", [(i, i - 1) for i in range(1, SEQ)])
    halo_pair = lax.ppermute(halo, "seq", [(i, i - 2) for i in range(2, SEQ, 2)])
    halo_other = jnp.where(core == 0, halo_pair, halo)
    mine, other = select(table, normed, dpre)
    other = lax.ppermute(other, "seq", swap)
    gls, shared = states(fore, back, cmat, dyt, dywt, cum, logd, rc, halves, cross, dbt, dbc)
    shared_other = lax.ppermute(shared, "seq", swap)

    args = (mine, other, dpre, dpre_other, halo_mine, halo_other, shared, shared_other)
    up1 = up_part(args)
    down1 = down_part(args, up1)
    near_up, near_down, here_a, here_b = keep_part(args, down1)
    part = input_part(w_x, w_bc, dpre, halo_mine, shared, here_a)
    grad_u = lax.psum_scatter(part, "head", scatter_dimension=0, tiled=True)
    sum_a, sum_b = ring_sum(
        lambda by: along(True, by), up1, down1, near_up, near_down, here_a, here_b, 320
    )
    a4 = sum_a.reshape(4, ROWS, FULL)
    b4 = sum_b.reshape(4, ROWS, FULL)
    up1 = jnp.concatenate([a4[2], b4[1]], axis=0).astype(BF16)
    down1 = jnp.concatenate([b4[2], a4[3]], axis=0).astype(BF16)
    sum_a, sum_b = ring_sum(
        lambda by: along(False, by), up1, down1, a4[1], b4[3], a4[0], b4[0], ROWS
    )
    norm = (T * SEQ) ** (-0.5)
    grad_wx = jnp.concatenate([sum_a[:, :WIDE], sum_b[:, :WIDE]], axis=1) * norm
    grad_wbc = jnp.concatenate([sum_a[:, WIDE:], sum_b[:, WIDE:]], axis=1) * norm
    for bit in (1, 2):
        pairs = [(i, i ^ bit) for i in range(ZS)]
        grad_wbc = grad_wbc + lax.ppermute(grad_wbc, "head", pairs)
    return (grad_u, grad_wx, grad_wbc, gls)


def solution(mesh):
    return jax.shard_map(
        body,
        mesh=mesh,
        in_specs=(
            P("seq", None),
            P(None, "head"),
            P(),
            P(None, "head"),
            P("head"),
            P("head", "seq"),
            P("head"),
            P("seq", "head"),
        ),
        out_specs=(P("head", "seq"), P("seq", "head"), P("seq", None), P("head", "seq")),
        check_vma=False,
    )
```

```python
import functools
import math

import jax
import jax.numpy as jnp
import numpy as np
from jax import lax
from jax.experimental import pallas as pl
from jax.experimental.pallas import tpu as pltpu
from jax.sharding import PartitionSpec as P

D = 2560
HEAD_DIM = 64
STATE = 128
CONV = 4
LEVELS = 256
T = 256
CH = 1280
HEADS = 20
SEQ = 32
ZS = 4
ROWS = 80
SLICE = 40
MSG = 88
BLK = 256
NBLK = CH // BLK
SCALE = STATE ** (-0.5)
F32 = jnp.float32
BF16 = jnp.bfloat16
HIGH = lax.Precision.HIGHEST
NT = (((1,), (1,)), ((), ()))
VMEM = 20 * 2**20


def nt(a, b):
    return lax.dot_general(a, b, NT, preferred_element_type=F32)


def nn(a, b):
    return jnp.dot(a, b, preferred_element_type=F32)


def split(value):
    high = value.astype(BF16)
    return high, (value - high.astype(F32)).astype(BF16)


def wide(dot, a, b):
    a_high, a_low = split(a)
    b_high, b_low = split(b)
    return dot(a_high, b_high) + (dot(a_low, b_high) + dot(a_high, b_low))


def params():
    return pltpu.CompilerParams(vmem_limit_bytes=VMEM)


def cost(flops, nbytes, trans=0):
    return pl.CostEstimate(flops=flops, bytes_accessed=nbytes, transcendentals=trans)


def whole(*shape):
    return pl.BlockSpec(shape, lambda i: (0,) * len(shape))


def triangle(upper):
    row = lax.broadcasted_iota(jnp.int32, (T, T), 0)
    col = lax.broadcasted_iota(jnp.int32, (T, T), 1)
    return jnp.where(row <= col if upper else row >= col, 1.0, 0.0).astype(F32)


def front_kernel(normed, w_bc, rates, step, grad_y, bmat, cmat, cum, logd, dyt, dywt, pulled, through, turn):
    shared = nn(normed[...], w_bc[...])
    bmat[...] = shared[:, :STATE]
    cmat[...] = shared[:, STATE:]
    c_high, c_low = split(shared[:, STATE:])
    logs = rates[...] * step[...]
    logd[...] = logs
    cums = jnp.dot(logs, triangle(True), precision=HIGH, preferred_element_type=F32)
    cum[...] = cums
    grown = jnp.exp(cums)
    weight = grown * SCALE
    for pair in range(HEADS // 2):
        rows = slice(128 * pair, 128 * pair + 128)
        tile = grad_y[:, rows].astype(F32).T
        dyt[rows, :] = tile.astype(BF16)
        tile = jnp.concatenate(
            [
                tile[:64] * weight[2 * pair : 2 * pair + 1],
                tile[64:] * weight[2 * pair + 1 : 2 * pair + 2],
            ],
            axis=0,
        )
        high, low = split(tile)
        dywt[rows, :] = high
        pulled[rows, :] = nn(high, c_high) + (nn(low, c_high) + nn(high, c_low))
    turn[...] = jnp.zeros((128, 128), F32)
    turn[:HEADS, :] = grown[:, 128:]
    through[...] = jnp.broadcast_to(turn[...].T[127:, :], (8, STATE))


def front(normed, w_bc, rates, step, grad_y):
    return pl.pallas_call(
        front_kernel,
        out_shape=(
            jax.ShapeDtypeStruct((T, STATE), F32),
            jax.ShapeDtypeStruct((T, STATE), F32),
            jax.ShapeDtypeStruct((HEADS, T), F32),
            jax.ShapeDtypeStruct((HEADS, T), F32),
            jax.ShapeDtypeStruct((CH, T), BF16),
            jax.ShapeDtypeStruct((CH, T), BF16),
            jax.ShapeDtypeStruct((CH, STATE), F32),
            jax.ShapeDtypeStruct((8, STATE), F32),
        ),
        scratch_shapes=[pltpu.VMEM((128, 128), F32)],
        compiler_params=params(),
        cost_estimate=cost(2 * T * D * 256 + 6 * CH * T * 128, 6 * 2**20),
    )(normed, w_bc, rates, step, grad_y)


def chain_kernel(table, recv, tie, out, turn):
    del tie
    lanes = jnp.concatenate([recv[:, 2 * SLICE, :], jnp.zeros((128 - SEQ, 128), F32)], axis=0)
    turn[...] = lanes.T
    head = table[32]
    row = lax.broadcasted_iota(jnp.int32, (SLICE, 128), 0)
    cols = jnp.where(row < table[33], turn[pl.ds(head, 1), :], turn[pl.ds(head + 1, 1), :])
    pulled = jnp.zeros((SLICE, STATE), F32)
    pulls = [None] * SEQ
    for k in range(SEQ - 1, -1, -1):
        pulls[k] = pulled
        pulled = cols[:, k : k + 1] * pulled + recv[k, :SLICE, :]
    state = jnp.zeros((SLICE, STATE), F32)
    for k in range(SEQ):
        out[k] = jnp.concatenate([pulls[k], state], axis=0).astype(BF16)
        state = cols[:, k : k + 1] * state + recv[k, SLICE : 2 * SLICE, :]


def chain(table, recv, tie):
    return pl.pallas_call(
        chain_kernel,
        grid=(1,),
        in_specs=[
            pl.BlockSpec(memory_space=pltpu.SMEM),
            whole(SEQ, MSG, STATE),
            pl.BlockSpec(memory_space=pl.ANY),
        ],
        out_specs=whole(SEQ, 2 * SLICE, STATE),
        out_shape=jax.ShapeDtypeStruct((SEQ, 2 * SLICE, STATE), BF16),
        scratch_shapes=[pltpu.VMEM((128, 128), F32)],
        compiler_params=params(),
        cost_estimate=cost(10**6, 3 * 2**20),
    )(table, recv, tie)


def channel_kernel(
    before, normed, w_x, conv_w, cum, logd, bmat, pulled, through, xgt, slope, xwt, msg, ext, pre, own
):
    step = pl.program_id(0)

    @pl.when(step == 0)
    def _():
        ext[:16, :] = before[...]
        ext[16:, :] = normed[...]

    now = lax.rem(step, 2)
    past = pre.at[1 - now]
    total = conv_w[0:1, :] * past[16 : 16 + T, :]
    for tap in range(1, CONV):
        total = total + conv_w[tap : tap + 1, :] * past[16 - tap : 16 - tap + T, :]
    sig = 0.5 * jnp.tanh(0.5 * total) + 0.5
    xt = (total * sig).T
    slope[...] = sig * (1.0 + total * (1.0 - sig))
    parts = []
    block = jnp.maximum(step - 1, 0)
    for q in range(BLK // HEAD_DIM):
        head = pl.ds(block * (BLK // HEAD_DIM) + q, 1)
        rows = slice(64 * q, 64 * q + 64)
        gain = jnp.sqrt(-2.0 * logd[head, :])
        cums = cum[head, :]
        tail = jnp.exp(cums[:, T - 1 :] - cums)
        xg = xt[rows] * gain
        xgt[rows, :] = xg.astype(BF16)
        parts.append(xg * tail)
    weighted = jnp.concatenate(parts, axis=0)
    xwt[...] = weighted.astype(BF16)
    own[pl.ds(pl.multiple_of(block * BLK, BLK), BLK), :] = wide(nn, weighted, bmat[...])
    pre[now] = nn(ext[...], w_x[...]).astype(BF16).astype(F32)

    @pl.when(step == NBLK)
    def _():
        for k in range(SEQ):
            rows = slice(SLICE * k, SLICE * (k + 1))
            msg[k, :SLICE, :] = pulled[rows, :]
            msg[k, SLICE : 2 * SLICE, :] = own[rows, :]
            msg[k, 2 * SLICE :, :] = through[...]


def channels(before, normed, w_x, conv_w, cum, logd, bmat, pulled, through):
    def late(i):
        return jnp.maximum(i - 1, 0)

    rows = pl.BlockSpec((BLK, T), lambda i: (late(i), 0))
    return pl.pallas_call(
        channel_kernel,
        grid=(NBLK + 1,),
        in_specs=[
            whole(16, D),
            whole(T, D),
            pl.BlockSpec((D, BLK), lambda i: (0, jnp.minimum(i, NBLK - 1))),
            pl.BlockSpec((CONV, BLK), lambda i: (0, late(i))),
            whole(HEADS, T),
            whole(HEADS, T),
            whole(T, STATE),
            whole(CH, STATE),
            whole(8, STATE),
        ],
        out_specs=(
            rows,
            pl.BlockSpec((T, BLK), lambda i: (0, late(i))),
            rows,
            whole(SEQ, MSG, STATE),
        ),
        out_shape=(
            jax.ShapeDtypeStruct((CH, T), BF16),
            jax.ShapeDtypeStruct((T, CH), F32),
            jax.ShapeDtypeStruct((CH, T), BF16),
            jax.ShapeDtypeStruct((SEQ, MSG, STATE), F32),
        ),
        scratch_shapes=[
            pltpu.VMEM((T + 16, D), BF16),
            pltpu.VMEM((2, T + 16, BLK), F32),
            pltpu.VMEM((CH, STATE), F32),
        ],
        compiler_params=params(),
        cost_estimate=cost(2 * T * D * CH, 10 * 2**20, T * CH),
    )(before, normed, w_x, conv_w, cum, logd, bmat, pulled, through)


def intra_kernel(grad_y, dyt, xgt, cum, bmat, cmat, tie, dxg, rc, dbc, gram, dgram):
    del tie
    step = pl.program_id(0)

    @pl.when(step == 0)
    def _():
        gram[...] = wide(nt, cmat[...], bmat[...]) * SCALE
        dgram[...] = jnp.zeros((T, T), F32)

    half = T // 2
    row = lax.broadcasted_iota(jnp.int32, (half, half), 0)
    col = lax.broadcasted_iota(jnp.int32, (half, half), 1)
    keep = row >= col
    blank = jnp.zeros((HEAD_DIM, T), BF16)
    corner = jnp.zeros((half, half), BF16)
    for q in range(BLK // HEAD_DIM):
        head = pl.ds(step * (BLK // HEAD_DIM) + q, 1)
        rows = slice(64 * q, 64 * q + 64)
        cums = cum[head, :]
        column = jnp.broadcast_to(cums, (half, T)).T
        l00 = jnp.exp(jnp.where(keep, column[:half] - cums[:, :half], -1e30))
        l10 = jnp.exp(column[half:] - cums[:, :half])
        l11 = jnp.exp(jnp.where(keep, column[half:] - cums[:, half:], -1e30))
        m00 = (l00 * gram[:half, :half]).astype(BF16)
        m10 = (l10 * gram[half:, :half]).astype(BF16)
        m11 = (l11 * gram[half:, half:]).astype(BF16)
        mat = jnp.concatenate(
            [jnp.concatenate([m00, corner], axis=1), jnp.concatenate([m10, m11], axis=1)], axis=0
        )
        dy = dyt[rows, :]
        xg = xgt[rows, :]
        pair = slice(128 * (q // 2), 128 * (q // 2) + 128)
        right = jnp.concatenate([xg, blank] if q % 2 == 0 else [blank, xg], axis=0)
        dm0 = nn(grad_y[:, pair], right[:, :half])
        dm1 = nn(grad_y[half:, pair], right[:, half:])
        dgram[:half, :half] += l00 * dm0[:half]
        dgram[half:, :half] += l10 * dm0[half:]
        dgram[half:, half:] += l11 * dm1
        back = nn(dy, mat)
        yin = nt(xg, mat)
        dxg[rows, :] = back
        rc[head, :] = jnp.sum(dy.astype(F32) * yin - xg.astype(F32) * back, axis=0, keepdims=True)

    @pl.when(step == NBLK - 1)
    def _():
        dg = (dgram[...] * SCALE).astype(BF16)
        dbc[:STATE, :] = nn(cmat[...].T.astype(BF16), dg)
        dbc[STATE:, :] = nn(dg, bmat[...].astype(BF16)).T


def intra(grad_y, dyt, xgt, cum, bmat, cmat, tie):
    rows = pl.BlockSpec((BLK, T), lambda i: (i, 0))
    return pl.pallas_call(
        intra_kernel,
        grid=(NBLK,),
        in_specs=[
            pl.BlockSpec((T, BLK), lambda i: (0, i)),
            rows,
            rows,
            whole(HEADS, T),
            whole(T, STATE),
            whole(T, STATE),
            pl.BlockSpec(memory_space=pl.ANY),
        ],
        out_specs=(rows, whole(HEADS, T), whole(2 * STATE, T)),
        out_shape=(
            jax.ShapeDtypeStruct((CH, T), F32),
            jax.ShapeDtypeStruct((HEADS, T), F32),
            jax.ShapeDtypeStruct((2 * STATE, T), F32),
        ),
        scratch_shapes=[pltpu.VMEM((T, T), F32), pltpu.VMEM((T, T), F32)],
        compiler_params=params(),
        cost_estimate=cost(HEADS * 2 * T * T * 64 * 8, 4 * 2**20, HEADS * T * T),
    )(grad_y, dyt, xgt, cum, bmat, cmat, tie)


def shared_kernel(back, xwt, dywt, dbc, ds, st, shared):
    for k in range(SEQ):
        rows = slice(SLICE * k, SLICE * (k + 1))
        both = back[k].astype(F32)
        ds[rows, :] = both[:SLICE]
        st[rows, :] = both[SLICE:]
    for at, (state, tokens) in enumerate(((ds, xwt), (st, dywt))):
        turned = state[...].T.astype(BF16)
        part = nn(turned, tokens[...]) + dbc[STATE * at : STATE * (at + 1), :]
        shared[:, STATE * at : STATE * (at + 1)] = part.T


def shared_part(back, xwt, dywt, dbc):
    return pl.pallas_call(
        shared_kernel,
        out_shape=(
            jax.ShapeDtypeStruct((CH, STATE), F32),
            jax.ShapeDtypeStruct((CH, STATE), F32),
            jax.ShapeDtypeStruct((T, 2 * STATE), F32),
        ),
        compiler_params=params(),
        cost_estimate=cost(4 * CH * T * 128, 4 * 2**20),
    )(back, xwt, dywt, dbc)


def grad_kernel(
    skip, back, bmat, dxg, dyt, xgt, slope, taps, cum, logd, tie, dpre, halo, halves, cross, ext
):
    del tie
    step = pl.program_id(0)
    later = wide(nt, back[...], bmat[...])
    parts = []
    for q in range(BLK // HEAD_DIM):
        index = step * (BLK // HEAD_DIM) + q
        head = pl.ds(index, 1)
        rows = slice(64 * q, 64 * q + 64)
        gain = jnp.sqrt(-2.0 * logd[head, :])
        cums = cum[head, :]
        tail = jnp.exp(cums[:, T - 1 :] - cums)
        inter = later[rows] * tail
        whole_dxg = dxg[rows, :] + inter
        xg = xgt[rows, :].astype(F32)
        cross[head, :] = jnp.sum(xg * inter, axis=0, keepdims=True)
        halves[head, :] = 0.5 * jnp.sum(xg * whole_dxg, axis=0, keepdims=True)
        parts.append(gain * whole_dxg + skip[index] * dyt[rows, :].astype(F32))
    ext[:8, :] = jnp.zeros((8, BLK), F32)
    ext[8 : T + 8, :] = jnp.concatenate(parts, axis=0).T * slope[...]
    ext[T + 8 :, :] = jnp.zeros((8, BLK), F32)
    total = taps[0:1, :] * ext[8 : T + 8, :]
    edge = taps[0:1, :] * ext[:8, :]
    for tap in range(1, CONV):
        weight = taps[tap : tap + 1, :]
        total = total + weight * ext[8 + tap : T + 8 + tap, :]
        edge = edge + weight * ext[tap : 8 + tap, :]
    dpre[...] = total.astype(BF16)
    halo[...] = edge


def gradients(skip, back, bmat, dxg, dyt, xgt, slope, taps, cum, logd, tie):
    rows = pl.BlockSpec((BLK, T), lambda i: (i, 0))
    cols = pl.BlockSpec((T, BLK), lambda i: (0, i))
    return pl.pallas_call(
        grad_kernel,
        grid=(NBLK,),
        in_specs=[
            pl.BlockSpec(memory_space=pltpu.SMEM),
            pl.BlockSpec((BLK, STATE), lambda i: (i, 0)),
            whole(T, STATE),
            rows,
            rows,
            rows,
            cols,
            pl.BlockSpec((CONV, BLK), lambda i: (0, i)),
            whole(HEADS, T),
            whole(HEADS, T),
            pl.BlockSpec(memory_space=pl.ANY),
        ],
        out_specs=(
            cols,
            pl.BlockSpec((8, BLK), lambda i: (0, i)),
            whole(HEADS, T),
            whole(HEADS, T),
        ),
        out_shape=(
            jax.ShapeDtypeStruct((T, CH), BF16),
            jax.ShapeDtypeStruct((8, CH), F32),
            jax.ShapeDtypeStruct((HEADS, T), F32),
            jax.ShapeDtypeStruct((HEADS, T), F32),
        ),
        scratch_shapes=[pltpu.VMEM((T + 16, BLK), F32)],
        compiler_params=params(),
        cost_estimate=cost(4 * CH * T * 128, 6 * 2**20, T * HEADS),
    )(skip, back, bmat, dxg, dyt, xgt, slope, taps, cum, logd, tie)


def step_kernel(fore, back, cmat, dyt, cum, logd, rc, halves, cross, tie, gls):
    del tie
    before = wide(nt, fore[...], cmat[...])
    cums = cum[...]
    inner = []
    through = []
    for h in range(HEADS):
        rows = slice(64 * h, 64 * h + 64)
        inner.append(jnp.sum(dyt[rows, :].astype(F32) * before[rows], axis=0, keepdims=True))
        both = jnp.sum(fore[rows, :] * back[rows, :], axis=0, keepdims=True)
        through.append(jnp.sum(both, axis=1, keepdims=True))
    arriving = rc[...] + jnp.exp(cums) * SCALE * jnp.concatenate(inner, axis=0)
    later = jnp.dot(arriving, triangle(False), precision=HIGH, preferred_element_type=F32)
    crossing = cross[...]
    earlier = (
        jnp.dot(crossing, triangle(True), precision=HIGH, preferred_element_type=F32) - crossing
    )
    kept = jnp.exp(cums[:, T - 1 :]) * jnp.concatenate(through, axis=0)
    gls[...] = logd[...] * (later + earlier + kept) + halves[...]


def step_part(fore, back, cmat, dyt, cum, logd, rc, halves, cross, tie):
    vm = pl.BlockSpec(memory_space=pltpu.VMEM)
    return pl.pallas_call(
        step_kernel,
        in_specs=[vm] * 9 + [pl.BlockSpec(memory_space=pl.ANY)],
        out_shape=jax.ShapeDtypeStruct((HEADS, T), F32),
        compiler_params=params(),
        cost_estimate=cost(4 * CH * T * 128, 4 * 2**20),
    )(fore, back, cmat, dyt, cum, logd, rc, halves, cross, tie)


def select_kernel(order, normed, tie, mine, other, flip):
    del tie
    for k in range(D // 128):
        cols = slice(128 * k, 128 * k + 128)
        flip[cols, :] = normed[:, cols].astype(F32).T.astype(BF16)
    for k in range(16):
        rows = slice(ROWS * k, ROWS * (k + 1))
        mine[rows, :] = flip[pl.ds(pl.multiple_of(order[k] * ROWS, 16), ROWS), :]
        other[rows, :] = flip[pl.ds(pl.multiple_of(order[16 + k] * ROWS, 16), ROWS), :]


def select(order, normed, tie):
    vm = pl.BlockSpec(memory_space=pltpu.VMEM)
    return pl.pallas_call(
        select_kernel,
        in_specs=[pl.BlockSpec(memory_space=pltpu.SMEM), vm, pl.BlockSpec(memory_space=pl.ANY)],
        out_shape=(jax.ShapeDtypeStruct((CH, T), BF16), jax.ShapeDtypeStruct((CH, T), BF16)),
        scratch_shapes=[pltpu.VMEM((D, T), BF16)],
        compiler_params=params(),
        cost_estimate=cost(10**6, 3 * 2**20),
    )(order, normed, tie)


PART = [slice(320 * r, 320 * (r + 1)) for r in range(4)]
WIDE = 640
FULL = WIDE + STATE
MAIN = [slice(0, WIDE), slice(WIDE, 2 * WIDE)]
EXTRA = [slice(0, STATE), slice(STATE, 2 * STATE)]


def mended(grad, halo, cols):
    edge = jnp.concatenate([jnp.zeros((8, WIDE), F32), halo[:, cols]], axis=0)
    return grad[: T - 16, cols], (grad[T - 16 :, cols].astype(F32) + edge).astype(BF16)


def product(refs, side):
    mine, other, grad, grad_other, halo, halo_other, shared, shared_other = refs
    cols = MAIN[side]
    right = jnp.concatenate(
        mended(grad, halo, cols) + mended(grad_other, halo_other, cols), axis=0
    )
    extra = jnp.concatenate([shared[:, EXTRA[side]], shared_other[:, EXTRA[side]]], axis=0)

    def rows(part):
        left = jnp.concatenate([mine[PART[part], :], other[PART[part], :]], axis=1)
        return nn(left, right), nn(left, extra)

    return rows


def far_kernel(*refs):
    for out, (part, side) in zip(refs[8:], ((2, 0), (2, 1))):
        main, extra = product(refs[:8], side)(part)
        out[:, :WIDE] = main.astype(BF16)
        out[:, WIDE:] = extra.astype(BF16)


def near_kernel(*refs):
    for out, (part, side) in zip(refs[9:], ((1, 0), (3, 1), (1, 1), (3, 0))):
        main, extra = product(refs[:8], side)(part)
        out[:, :WIDE] = main.astype(out.dtype)
        out[:, WIDE:] = extra.astype(out.dtype)


def here_kernel(*refs):
    for out, (part, side) in zip(refs[9:], ((0, 0), (0, 1))):
        main, extra = product(refs[:8], side)(part)
        out[:, :WIDE] = main
        out[:, WIDE:] = extra


def product_part(kernel, args, ties, types):
    vm = pl.BlockSpec(memory_space=pltpu.VMEM)
    return pl.pallas_call(
        kernel,
        in_specs=[vm] * 8 + [pl.BlockSpec(memory_space=pl.ANY)] * len(ties),
        out_shape=tuple(jax.ShapeDtypeStruct((320, FULL), one) for one in types),
        compiler_params=params(),
        cost_estimate=cost(2 * 512 * FULL * 320 * len(types), (3 + len(types)) * 2**20),
    )(*args, *ties)


def join_kernel(count, *refs):
    ins, outs = refs[: 3 * count], refs[3 * count :]
    for i, out in enumerate(outs):
        near, arrived, direct = ins[3 * i : 3 * i + 3]
        size = near.shape[0]
        out[:size, :] = (near[...] + arrived[...].astype(F32)).astype(BF16)
        out[size:, :] = direct[...]


def join(*triples):
    count = len(triples)
    return pl.pallas_call(
        functools.partial(join_kernel, count),
        out_shape=tuple(
            jax.ShapeDtypeStruct((2 * near.shape[0], near.shape[1]), BF16)
            for near, _, _ in triples
        ),
        compiler_params=params(),
        cost_estimate=cost(10**6, 4 * 2**20),
    )(*[one for triple in triples for one in triple])


def turn_kernel(here_a, here_b, up, down, far_up, far_down, near_up, near_down, dir_up, dir_down, a, b):
    size = 4 * ROWS

    def one(r, side):
        rows = slice(ROWS * r, ROWS * (r + 1))
        direct = slice(size + ROWS * r, size + ROWS * (r + 1))
        if side == 0:
            arrived = up[rows, :].astype(F32) + down[direct, :].astype(F32)
            return here_a[rows, :] + arrived
        arrived = down[rows, :].astype(F32) + up[direct, :].astype(F32)
        return here_b[rows, :] + arrived

    far_up[...] = one(2, 0).astype(BF16)
    far_down[...] = one(2, 1).astype(BF16)
    near_up[...] = one(1, 0)
    near_down[...] = one(3, 1)
    dir_up[...] = one(1, 1).astype(BF16)
    dir_down[...] = one(3, 0).astype(BF16)
    a[...] = one(0, 0)
    b[...] = one(0, 1)


def turn_part(here_a, here_b, up, down):
    return pl.pallas_call(
        turn_kernel,
        out_shape=tuple(
            jax.ShapeDtypeStruct((ROWS, FULL), one)
            for one in (BF16, BF16, F32, F32, BF16, BF16, F32, F32)
        ),
        compiler_params=params(),
        cost_estimate=cost(10**6, 4 * 2**20),
    )(here_a, here_b, up, down)


def last_kernel(a, b, up, down, here_u, up_u, down_u, grad_wx, grad_wbc, grad_u):
    norm = (T * SEQ) ** (-0.5)
    first = a[...] + (up[:ROWS, :].astype(F32) + down[ROWS:, :].astype(F32))
    second = b[...] + (down[:ROWS, :].astype(F32) + up[ROWS:, :].astype(F32))
    grad_wx[:, :WIDE] = first[:, :WIDE] * norm
    grad_wx[:, WIDE:] = second[:, :WIDE] * norm
    grad_wbc[:, :STATE] = first[:, WIDE:] * norm
    grad_wbc[:, STATE:] = second[:, WIDE:] * norm
    size = here_u.shape[0] // 2
    low = here_u[:size, :] + (up_u[:size, :].astype(F32) + down_u[size:, :].astype(F32))
    high = here_u[size:, :] + (down_u[:size, :].astype(F32) + up_u[size:, :].astype(F32))
    grad_u[:size, :] = low.astype(BF16)
    grad_u[size:, :] = high.astype(BF16)


def last_part(*args):
    return pl.pallas_call(
        last_kernel,
        out_shape=(
            jax.ShapeDtypeStruct((ROWS, CH), F32),
            jax.ShapeDtypeStruct((ROWS, 2 * STATE), F32),
            jax.ShapeDtypeStruct((D // ZS, T), BF16),
        ),
        compiler_params=params(),
        cost_estimate=cost(10**6, 3 * 2**20),
    )(*args)


def input_kernel(order, w_x, w_bc, grad, halo, shared, tie, *outs):
    del order, tie
    far_up, far_down, near_up, near_down, dir_up, dir_down, here = outs
    step = pl.program_id(0)
    rows = w_x.shape[0] // 2
    low, high = slice(0, rows), slice(rows, 2 * rows)
    edge = jnp.concatenate([jnp.zeros((8, CH), F32), halo[...]], axis=0)
    last = (grad[T - 16 :, :].astype(F32) + edge).astype(BF16)
    right = jnp.concatenate([grad[: T - 16, :], last], axis=0)
    part = nt(w_x[...], right)

    @pl.when(step == 0)
    def _():
        far_up[...] = part[low].astype(BF16)
        far_down[...] = part[high].astype(BF16)

    @pl.when(step == 1)
    def _():
        near_up[...] = part[low]
        dir_up[...] = part[high].astype(BF16)

    @pl.when(step == 2)
    def _():
        dir_down[...] = part[low].astype(BF16)
        near_down[...] = part[high]

    @pl.when(step == 3)
    def _():
        here[...] = part + nt(w_bc[...], shared[...])


def input_part(order, w_x, w_bc, grad, halo, shared, tie):
    rows = D // ZS
    sizes = (rows // 2,) * 6 + (rows,)
    types = (BF16, BF16, F32, F32, BF16, BF16, F32)
    return pl.pallas_call(
        input_kernel,
        grid_spec=pltpu.PrefetchScalarGridSpec(
            num_scalar_prefetch=1,
            grid=(ZS,),
            in_specs=[
                pl.BlockSpec((rows, CH), lambda i, order: (order[i], 0)),
                pl.BlockSpec((rows, 2 * STATE), lambda i, order: (order[3], 0)),
                pl.BlockSpec((T, CH), lambda i, order: (0, 0)),
                pl.BlockSpec((8, CH), lambda i, order: (0, 0)),
                pl.BlockSpec((T, 2 * STATE), lambda i, order: (0, 0)),
                pl.BlockSpec(memory_space=pl.ANY),
            ],
            out_specs=[pl.BlockSpec((size, T), lambda i, order: (0, 0)) for size in sizes],
        ),
        out_shape=tuple(jax.ShapeDtypeStruct((size, T), one) for size, one in zip(sizes, types)),
        compiler_params=params(),
        cost_estimate=cost(2 * D * (CH + 64) * T, 10 * 2**20),
    )(order, w_x, w_bc, grad, halo, shared, tie)


def device(x, y, core):
    return ((x % 4) * 4 + y % 4) * 2 + core


def ring(first, by):
    pairs = []
    for x in range(4):
        for y in range(4):
            for core in range(2):
                along_x = (core == 0) == first
                goal = device(x + by, y, core) if along_x else device(x, y + by, core)
                pairs.append((device(x, y, core), goal))
    return pairs


def along(first, by):
    return lambda value: lax.ppermute(value, "seq", ring(first, by))


def along_head(by):
    return lambda value: lax.ppermute(value, "head", [(i, (i + by) % ZS) for i in range(ZS)])


def place_table():
    rows = []
    for place in range(SEQ):
        core, y, x = place % 2, place // 2 % 4, place // 8
        blocks = [
            [device(x + a, y + b, 0) for a in range(4) for b in range(4)],
            [device(x + b, y + a, 1) for a in range(4) for b in range(4)],
        ]
        head = SLICE * place // HEAD_DIM
        bound = HEAD_DIM * (head + 1) - SLICE * place
        rows.append(blocks[core] + blocks[1 - core] + [head, bound])
    return np.array(rows, np.int32)


def head_table():
    return np.array([[(z + r) % ZS for r in (2, 1, 3, 0)] for z in range(ZS)], np.int32)


def body(normed, w_x, w_bc, conv_w, decay_code, step, d_skip, grad_y):
    place = lax.axis_index("seq")
    core = place % 2
    z = lax.axis_index("head")
    order_z = jnp.asarray(head_table())[z]
    table = lax.dynamic_index_in_dim(jnp.asarray(place_table()), place, 0, keepdims=False)
    swap = [(i, i ^ 1) for i in range(SEQ)]

    low = math.log(0.995)
    high = math.log(0.9999)
    rates = low + decay_code.astype(F32)[:, None] / (LEVELS - 1) * (high - low)
    before = lax.ppermute(normed[T - 16 :], "seq", [(i, i + 1) for i in range(SEQ - 1)])

    bmat, cmat, cum, logd, dyt, dywt, pulled, through = front(normed, w_bc, rates, step, grad_y)
    xgt, slope, xwt, msg = channels(
        before, normed, w_x, conv_w, cum, logd, bmat, pulled, through
    )
    recv = lax.all_to_all(msg, "seq", 0, 0)
    mine, other = select(table, normed, msg)
    other = lax.ppermute(other, "seq", swap)
    dxg, rc, dbc = intra(grad_y, dyt, xgt, cum, bmat, cmat, mine)
    back = lax.all_to_all(chain(table, recv, rc), "seq", 0, 0)

    ds, st, shared = shared_part(back, xwt, dywt, dbc)
    for bit in (1, 2):
        pairs = [(i, i ^ bit) for i in range(ZS)]
        shared = shared + lax.ppermute(shared, "head", pairs)
    shared = shared.astype(BF16)
    dpre, halo, halves, cross = gradients(
        d_skip, ds, bmat, dxg, dyt, xgt, slope, conv_w, cum, logd, st
    )
    dpre_other = lax.ppermute(dpre, "seq", swap)
    halo_mine = lax.ppermute(halo, "seq", [(i, i - 1) for i in range(1, SEQ)])
    halo_pair = lax.ppermute(halo, "seq", [(i, i - 2) for i in range(2, SEQ, 2)])
    halo_other = jnp.where(core == 0, halo_pair, halo)
    shared_other = lax.ppermute(shared, "seq", swap)

    args = (mine, other, dpre, dpre_other, halo_mine, halo_other, shared, shared_other)
    move = {by: along(True, by) for by in (1, -1)}
    turn = {by: along(False, by) for by in (1, -1)}
    head = {by: along_head(by) for by in (1, -1)}
    far_up, far_down = product_part(far_kernel, args, (), (BF16, BF16))
    ru, rd = move[1](far_up), move[-1](far_down)
    near_up, near_down, dir_up, dir_down = product_part(
        near_kernel, args, (far_up,), (F32, F32, BF16, BF16)
    )
    up, down = join((near_up, ru, dir_up), (near_down, rd, dir_down))
    ru, rd = move[1](up), move[-1](down)
    here_a, here_b = product_part(here_kernel, args, (up,), (F32, F32))
    z_far_up, z_far_down, z_up, z_down, z_dir_up, z_dir_down, z_here = input_part(
        order_z, w_x, w_bc, dpre, halo_mine, shared, here_a
    )
    gls = step_part(st, ds, cmat, dyt, cum, logd, rc, halves, cross, z_here)
    far_up, far_down, near_up, near_down, dir_up, dir_down, here_a, here_b = turn_part(
        here_a, here_b, ru, rd
    )
    ru, rd = turn[1](far_up), turn[-1](far_down)
    zu, zd = head[1](z_far_up), head[-1](z_far_down)
    up, down, z_up, z_down = join(
        (near_up, ru, dir_up),
        (near_down, rd, dir_down),
        (z_up, zu, z_dir_up),
        (z_down, zd, z_dir_down),
    )
    ru, rd = turn[1](up), turn[-1](down)
    zu, zd = head[1](z_up), head[-1](z_down)
    grad_wx, grad_wbc, grad_u = last_part(here_a, here_b, ru, rd, z_here, zu, zd)
    return (grad_u, grad_wx, grad_wbc, gls)


def solution(mesh):
    return jax.shard_map(
        body,
        mesh=mesh,
        in_specs=(
            P("seq", None),
            P(None, "head"),
            P(),
            P(None, "head"),
            P("head"),
            P("head", "seq"),
            P("head"),
            P("seq", "head"),
        ),
        out_specs=(P("head", "seq"), P("seq", "head"), P("seq", None), P("head", "seq")),
        check_vma=False,
    )
```

```python
import functools
import math

import jax
import jax.numpy as jnp
import numpy as np
from jax import lax
from jax.experimental import pallas as pl
from jax.experimental.pallas import tpu as pltpu
from jax.sharding import PartitionSpec as P

D = 2560
HEAD_DIM = 64
STATE = 128
CONV = 4
LEVELS = 256
T = 256
CH = 1280
HEADS = 20
SEQ = 32
ZS = 4
ROWS = 80
SLICE = 40
MSG = 48
BLK = 256
NBLK = CH // BLK
SCALE = STATE ** (-0.5)
F32 = jnp.float32
BF16 = jnp.bfloat16
HIGH = lax.Precision.HIGHEST
NT = (((1,), (1,)), ((), ()))


def nt(a, b):
    return lax.dot_general(a, b, NT, preferred_element_type=F32)


def nn(a, b):
    return jnp.dot(a, b, preferred_element_type=F32)


def split(value):
    high = value.astype(BF16)
    return high, (value - high.astype(F32)).astype(BF16)


def wide(dot, a, b):
    a_high, a_low = split(a)
    b_high, b_low = split(b)
    return dot(a_high, b_high) + (dot(a_low, b_high) + dot(a_high, b_low))


def params(mib=14):
    return pltpu.CompilerParams(vmem_limit_bytes=mib * 2**20)


def cost(flops, nbytes, trans=0):
    return pl.CostEstimate(flops=flops, bytes_accessed=nbytes, transcendentals=trans)


def whole(*shape):
    return pl.BlockSpec(shape, lambda i: (0,) * len(shape))


def triangle(upper):
    row = lax.broadcasted_iota(jnp.int32, (T, T), 0)
    col = lax.broadcasted_iota(jnp.int32, (T, T), 1)
    return jnp.where(row <= col if upper else row >= col, 1.0, 0.0).astype(F32)


def front_kernel(normed, w_bc, rates, step, grad_y, bmat, cmat, cum, logd, dyt, dywt, msg, pulled, turn):
    shared = nn(normed[...], w_bc[...])
    bmat[...] = shared[:, :STATE]
    cmat[...] = shared[:, STATE:]
    c_high, c_low = split(shared[:, STATE:])
    logs = rates[...] * step[...]
    logd[...] = logs
    cums = jnp.dot(logs, triangle(True), precision=HIGH, preferred_element_type=F32)
    cum[...] = cums
    grown = jnp.exp(cums)
    weight = grown * SCALE
    for pair in range(HEADS // 2):
        rows = slice(128 * pair, 128 * pair + 128)
        tile = grad_y[:, rows].astype(F32).T
        dyt[rows, :] = tile.astype(BF16)
        tile = jnp.concatenate(
            [
                tile[:64] * weight[2 * pair : 2 * pair + 1],
                tile[64:] * weight[2 * pair + 1 : 2 * pair + 2],
            ],
            axis=0,
        )
        high, low = split(tile)
        dywt[rows, :] = high
        pulled[rows, :] = nn(high, c_high) + (nn(low, c_high) + nn(high, c_low))
    turn[...] = jnp.zeros((128, 128), F32)
    turn[:HEADS, :] = grown[:, 128:]
    through = jnp.broadcast_to(turn[...].T[127:, :], (MSG - SLICE, STATE))
    for k in range(SEQ):
        msg[k, :SLICE, :] = pulled[SLICE * k : SLICE * (k + 1), :]
        msg[k, SLICE:, :] = through


def front(normed, w_bc, rates, step, grad_y):
    return pl.pallas_call(
        front_kernel,
        out_shape=(
            jax.ShapeDtypeStruct((T, STATE), F32),
            jax.ShapeDtypeStruct((T, STATE), F32),
            jax.ShapeDtypeStruct((HEADS, T), F32),
            jax.ShapeDtypeStruct((HEADS, T), F32),
            jax.ShapeDtypeStruct((CH, T), BF16),
            jax.ShapeDtypeStruct((CH, T), BF16),
            jax.ShapeDtypeStruct((SEQ, MSG, STATE), F32),
        ),
        scratch_shapes=[pltpu.VMEM((CH, STATE), F32), pltpu.VMEM((128, 128), F32)],
        compiler_params=params(),
        cost_estimate=cost(2 * T * D * 256 + 6 * CH * T * 128, 6 * 2**20),
    )(normed, w_bc, rates, step, grad_y)


def chain_kernel(reverse, table, recv, decays, tie, out, turn):
    del tie
    lanes = jnp.concatenate([decays[:, 0, :], jnp.zeros((128 - SEQ, 128), F32)], axis=0)
    turn[...] = lanes.T
    head = table[32]
    row = lax.broadcasted_iota(jnp.int32, (SLICE, 128), 0)
    cols = jnp.where(row < table[33], turn[pl.ds(head, 1), :], turn[pl.ds(head + 1, 1), :])
    state = jnp.zeros((SLICE, STATE), F32)
    for k in range(SEQ - 1, -1, -1) if reverse else range(SEQ):
        out[k] = state.astype(out.dtype)
        state = cols[:, k : k + 1] * state + recv[k]


def chain(table, recv, pulls, tie, reverse):
    return pl.pallas_call(
        functools.partial(chain_kernel, reverse),
        grid=(1,),
        in_specs=[
            pl.BlockSpec(memory_space=pltpu.SMEM),
            whole(SEQ, SLICE, STATE),
            pl.BlockSpec((SEQ, MSG - SLICE, STATE), lambda i: (0, SLICE // 8, 0)),
            pl.BlockSpec(memory_space=pl.ANY),
        ],
        out_specs=whole(SEQ, SLICE, STATE),
        out_shape=jax.ShapeDtypeStruct((SEQ, SLICE, STATE), F32),
        scratch_shapes=[pltpu.VMEM((128, 128), F32)],
        compiler_params=params(),
        cost_estimate=cost(10**6, 2 * 2**20),
    )(table, recv, pulls, tie)


def channel_kernel(
    before, normed, conv_w, cum, logd, w_x, xgt, slope, xwt, xlt, ext, pre, held, sems
):
    copies = [
        pltpu.make_async_copy(w_x.at[:, pl.ds(BLK * i, BLK)], held.at[i], sems.at[i])
        for i in range(NBLK)
    ]
    for one in copies:
        one.start()
    ext[:16, :] = before[...]
    ext[16:, :] = normed[...]
    for i in range(NBLK + 1):
        if i < NBLK:
            copies[i].wait()
            pre[i % 2] = nn(ext[...], held[i]).astype(BF16).astype(F32)
        if i == 0:
            continue
        block = i - 1
        past = pre.at[block % 2]
        cols = slice(BLK * block, BLK * (block + 1))
        total = conv_w[0:1, cols] * past[16 : 16 + T, :]
        for tap in range(1, CONV):
            total = total + conv_w[tap : tap + 1, cols] * past[16 - tap : 16 - tap + T, :]
        sig = 0.5 * jnp.tanh(0.5 * total) + 0.5
        xt = (total * sig).T
        slope[:, cols] = sig * (1.0 + total * (1.0 - sig))
        for q in range(BLK // HEAD_DIM):
            h = block * (BLK // HEAD_DIM) + q
            rows = slice(64 * h, 64 * h + 64)
            gain = jnp.sqrt(-2.0 * logd[h : h + 1, :])
            cums = cum[h : h + 1, :]
            tail = jnp.exp(cums[:, T - 1 :] - cums)
            xg = xt[64 * q : 64 * q + 64] * gain
            xgt[rows, :] = xg.astype(BF16)
            high, low = split(xg * tail)
            xwt[rows, :] = high
            xlt[rows, :] = low


def channels(before, normed, conv_w, cum, logd, w_x):
    vm = pl.BlockSpec(memory_space=pltpu.VMEM)
    return pl.pallas_call(
        channel_kernel,
        in_specs=[vm] * 5 + [pl.BlockSpec(memory_space=pltpu.HBM)],
        out_shape=(
            jax.ShapeDtypeStruct((CH, T), BF16),
            jax.ShapeDtypeStruct((T, CH), F32),
            jax.ShapeDtypeStruct((CH, T), BF16),
            jax.ShapeDtypeStruct((CH, T), BF16),
        ),
        scratch_shapes=[
            pltpu.VMEM((T + 16, D), BF16),
            pltpu.VMEM((2, T + 16, BLK), F32),
            pltpu.VMEM((NBLK, D, BLK), BF16),
            pltpu.SemaphoreType.DMA((NBLK,)),
        ],
        compiler_params=params(24),
        cost_estimate=cost(2 * T * D * CH, 10 * 2**20, T * CH),
    )(before, normed, conv_w, cum, logd, w_x)


def intra_kernel(
    grad_y, dyt, xgt, xwt, xlt, cum, bmat, cmat, tie, dxg, rc, dbc, own, gram, dgram
):
    del tie
    step = pl.program_id(0)

    @pl.when(step == 0)
    def _():
        gram[...] = wide(nt, cmat[...], bmat[...]) * SCALE
        dgram[...] = jnp.zeros((T, T), F32)

    b_high, b_low = split(bmat[...])
    own[...] = nn(xwt[...], b_high) + (nn(xlt[...], b_high) + nn(xwt[...], b_low))
    half = T // 2
    row = lax.broadcasted_iota(jnp.int32, (half, half), 0)
    col = lax.broadcasted_iota(jnp.int32, (half, half), 1)
    keep = row >= col
    blank = jnp.zeros((HEAD_DIM, T), BF16)
    corner = jnp.zeros((half, half), BF16)
    for q in range(BLK // HEAD_DIM):
        head = pl.ds(step * (BLK // HEAD_DIM) + q, 1)
        rows = slice(64 * q, 64 * q + 64)
        cums = cum[head, :]
        column = jnp.broadcast_to(cums, (half, T)).T
        l00 = jnp.exp(jnp.where(keep, column[:half] - cums[:, :half], -1e30))
        l10 = jnp.exp(column[half:] - cums[:, :half])
        l11 = jnp.exp(jnp.where(keep, column[half:] - cums[:, half:], -1e30))
        m00 = (l00 * gram[:half, :half]).astype(BF16)
        m10 = (l10 * gram[half:, :half]).astype(BF16)
        m11 = (l11 * gram[half:, half:]).astype(BF16)
        mat = jnp.concatenate(
            [jnp.concatenate([m00, corner], axis=1), jnp.concatenate([m10, m11], axis=1)], axis=0
        )
        dy = dyt[rows, :]
        xg = xgt[rows, :]
        pair = slice(128 * (q // 2), 128 * (q // 2) + 128)
        right = jnp.concatenate([xg, blank] if q % 2 == 0 else [blank, xg], axis=0)
        dm0 = nn(grad_y[:, pair], right[:, :half])
        dm1 = nn(grad_y[half:, pair], right[:, half:])
        dgram[:half, :half] += l00 * dm0[:half]
        dgram[half:, :half] += l10 * dm0[half:]
        dgram[half:, half:] += l11 * dm1
        back = nn(dy, mat)
        yin = nt(xg, mat)
        dxg[rows, :] = back
        rc[head, :] = jnp.sum(dy.astype(F32) * yin - xg.astype(F32) * back, axis=0, keepdims=True)

    @pl.when(step == NBLK - 1)
    def _():
        dg = (dgram[...] * SCALE).astype(BF16)
        dbc[:STATE, :] = nn(cmat[...].T.astype(BF16), dg)
        dbc[STATE:, :] = nn(dg, bmat[...].astype(BF16)).T


def intra(grad_y, dyt, xgt, xwt, xlt, cum, bmat, cmat, tie):
    rows = pl.BlockSpec((BLK, T), lambda i: (i, 0))
    return pl.pallas_call(
        intra_kernel,
        grid=(NBLK,),
        in_specs=[
            pl.BlockSpec((T, BLK), lambda i: (0, i)),
            rows,
            rows,
            rows,
            rows,
            whole(HEADS, T),
            whole(T, STATE),
            whole(T, STATE),
            pl.BlockSpec(memory_space=pl.ANY),
        ],
        out_specs=(
            rows,
            whole(HEADS, T),
            whole(2 * STATE, T),
            pl.BlockSpec((BLK, STATE), lambda i: (i, 0)),
        ),
        out_shape=(
            jax.ShapeDtypeStruct((CH, T), F32),
            jax.ShapeDtypeStruct((HEADS, T), F32),
            jax.ShapeDtypeStruct((2 * STATE, T), F32),
            jax.ShapeDtypeStruct((CH, STATE), F32),
        ),
        scratch_shapes=[pltpu.VMEM((T, T), F32), pltpu.VMEM((T, T), F32)],
        compiler_params=params(),
        cost_estimate=cost(HEADS * 2 * T * T * 64 * 8, 4 * 2**20, HEADS * T * T),
    )(grad_y, dyt, xgt, xwt, xlt, cum, bmat, cmat, tie)


def shared_kernel(order, ds, st, xwt, dywt, dbc, tie, shared, *outs):
    del tie
    chunks, total = outs[:ZS], outs[ZS]
    for at, (state, tokens) in enumerate(((ds, xwt), (st, dywt))):
        rows = slice(STATE * at, STATE * (at + 1))
        total[rows, :] = nn(state[...].T.astype(BF16), tokens[...]) + dbc[rows, :]
    shared[...] = total[...].astype(BF16)
    for r in range(ZS):
        chunks[r][...] = total[pl.ds(pl.multiple_of(order[r] * 64, 64), 64), :]


def shared_part(order, ds, st, xwt, dywt, dbc, tie):
    vm = pl.BlockSpec(memory_space=pltpu.VMEM)
    return pl.pallas_call(
        shared_kernel,
        in_specs=[pl.BlockSpec(memory_space=pltpu.SMEM)]
        + [vm] * 5
        + [pl.BlockSpec(memory_space=pl.ANY)],
        out_shape=(jax.ShapeDtypeStruct((2 * STATE, T), BF16),)
        + (jax.ShapeDtypeStruct((64, T), F32),) * ZS,
        scratch_shapes=[pltpu.VMEM((2 * STATE, T), F32)],
        compiler_params=params(),
        cost_estimate=cost(4 * CH * T * 128, 4 * 2**20),
    )(order, ds, st, xwt, dywt, dbc, tie)


def small_kernel(table, mine, other, chunk, chunk_other, out):
    part = nt(mine[...], chunk[...]) + nt(other[...], chunk_other[...])
    for k in range(16):
        low = part[ROWS * k : ROWS * k + 40]
        high = part[ROWS * k + 40 : ROWS * (k + 1)]
        out[table[k] // 2] = jnp.concatenate([low, high], axis=1)


def small_part(table, mine, other, chunk, chunk_other):
    vm = pl.BlockSpec(memory_space=pltpu.VMEM)
    return pl.pallas_call(
        small_kernel,
        in_specs=[pl.BlockSpec(memory_space=pltpu.SMEM)] + [vm] * 4,
        out_shape=jax.ShapeDtypeStruct((16, 40, 128), F32),
        compiler_params=params(),
        cost_estimate=cost(2 * CH * 512 * 64, 2 * 2**20),
    )(table, mine, other, chunk, chunk_other)


def grad_kernel(
    skip, back, bmat, dxg, dyt, xgt, slope, taps, cum, logd, tie, dpre, halo, halves, cross, ext
):
    del tie
    step = pl.program_id(0)
    later = wide(nt, back[...], bmat[...])
    parts = []
    for q in range(BLK // HEAD_DIM):
        index = step * (BLK // HEAD_DIM) + q
        head = pl.ds(index, 1)
        rows = slice(64 * q, 64 * q + 64)
        gain = jnp.sqrt(-2.0 * logd[head, :])
        cums = cum[head, :]
        tail = jnp.exp(cums[:, T - 1 :] - cums)
        inter = later[rows] * tail
        whole_dxg = dxg[rows, :] + inter
        xg = xgt[rows, :].astype(F32)
        cross[head, :] = jnp.sum(xg * inter, axis=0, keepdims=True)
        halves[head, :] = 0.5 * jnp.sum(xg * whole_dxg, axis=0, keepdims=True)
        parts.append(gain * whole_dxg + skip[index] * dyt[rows, :].astype(F32))
    ext[:8, :] = jnp.zeros((8, BLK), F32)
    ext[8 : T + 8, :] = jnp.concatenate(parts, axis=0).T * slope[...]
    ext[T + 8 :, :] = jnp.zeros((8, BLK), F32)
    total = taps[0:1, :] * ext[8 : T + 8, :]
    edge = taps[0:1, :] * ext[:8, :]
    for tap in range(1, CONV):
        weight = taps[tap : tap + 1, :]
        total = total + weight * ext[8 + tap : T + 8 + tap, :]
        edge = edge + weight * ext[tap : 8 + tap, :]
    dpre[...] = total.astype(BF16)
    halo[...] = edge


def gradients(skip, back, bmat, dxg, dyt, xgt, slope, taps, cum, logd, tie):
    rows = pl.BlockSpec((BLK, T), lambda i: (i, 0))
    cols = pl.BlockSpec((T, BLK), lambda i: (0, i))
    return pl.pallas_call(
        grad_kernel,
        grid=(NBLK,),
        in_specs=[
            pl.BlockSpec(memory_space=pltpu.SMEM),
            pl.BlockSpec((BLK, STATE), lambda i: (i, 0)),
            whole(T, STATE),
            rows,
            rows,
            rows,
            cols,
            pl.BlockSpec((CONV, BLK), lambda i: (0, i)),
            whole(HEADS, T),
            whole(HEADS, T),
            pl.BlockSpec(memory_space=pl.ANY),
        ],
        out_specs=(
            cols,
            pl.BlockSpec((8, BLK), lambda i: (0, i)),
            whole(HEADS, T),
            whole(HEADS, T),
        ),
        out_shape=(
            jax.ShapeDtypeStruct((T, CH), BF16),
            jax.ShapeDtypeStruct((8, CH), F32),
            jax.ShapeDtypeStruct((HEADS, T), F32),
            jax.ShapeDtypeStruct((HEADS, T), F32),
        ),
        scratch_shapes=[pltpu.VMEM((T + 16, BLK), F32)],
        compiler_params=params(),
        cost_estimate=cost(4 * CH * T * 128, 6 * 2**20, T * HEADS),
    )(skip, back, bmat, dxg, dyt, xgt, slope, taps, cum, logd, tie)


def step_kernel(fore, back, cmat, dyt, cum, logd, rc, halves, cross, tie, gls):
    del tie
    before = wide(nt, fore[...], cmat[...])
    cums = cum[...]
    inner = []
    through = []
    for h in range(HEADS):
        rows = slice(64 * h, 64 * h + 64)
        inner.append(jnp.sum(dyt[rows, :].astype(F32) * before[rows], axis=0, keepdims=True))
        both = jnp.sum(fore[rows, :] * back[rows, :], axis=0, keepdims=True)
        through.append(jnp.sum(both, axis=1, keepdims=True))
    arriving = rc[...] + jnp.exp(cums) * SCALE * jnp.concatenate(inner, axis=0)
    later = jnp.dot(arriving, triangle(False), precision=HIGH, preferred_element_type=F32)
    crossing = cross[...]
    earlier = (
        jnp.dot(crossing, triangle(True), precision=HIGH, preferred_element_type=F32) - crossing
    )
    kept = jnp.exp(cums[:, T - 1 :]) * jnp.concatenate(through, axis=0)
    gls[...] = logd[...] * (later + earlier + kept) + halves[...]


def step_part(fore, back, cmat, dyt, cum, logd, rc, halves, cross, tie):
    vm = pl.BlockSpec(memory_space=pltpu.VMEM)
    return pl.pallas_call(
        step_kernel,
        in_specs=[vm] * 9 + [pl.BlockSpec(memory_space=pl.ANY)],
        out_shape=jax.ShapeDtypeStruct((HEADS, T), F32),
        compiler_params=params(),
        cost_estimate=cost(4 * CH * T * 128, 4 * 2**20),
    )(fore, back, cmat, dyt, cum, logd, rc, halves, cross, tie)


def select_kernel(order, normed, tie, mine, other, flip):
    del tie
    for k in range(D // 128):
        cols = slice(128 * k, 128 * k + 128)
        flip[cols, :] = normed[:, cols].astype(F32).T.astype(BF16)
    for k in range(16):
        rows = slice(ROWS * k, ROWS * (k + 1))
        mine[rows, :] = flip[pl.ds(pl.multiple_of(order[k] * ROWS, 16), ROWS), :]
        other[rows, :] = flip[pl.ds(pl.multiple_of(order[16 + k] * ROWS, 16), ROWS), :]


def select(order, normed, tie):
    vm = pl.BlockSpec(memory_space=pltpu.VMEM)
    return pl.pallas_call(
        select_kernel,
        in_specs=[pl.BlockSpec(memory_space=pltpu.SMEM), vm, pl.BlockSpec(memory_space=pl.ANY)],
        out_shape=(jax.ShapeDtypeStruct((CH, T), BF16), jax.ShapeDtypeStruct((CH, T), BF16)),
        scratch_shapes=[pltpu.VMEM((D, T), BF16)],
        compiler_params=params(),
        cost_estimate=cost(10**6, 3 * 2**20),
    )(order, normed, tie)


PART = [slice(320 * r, 320 * (r + 1)) for r in range(4)]
WIDE = 640
MAIN = [slice(0, WIDE), slice(WIDE, 2 * WIDE)]


def mended(grad, halo, cols):
    edge = jnp.concatenate([jnp.zeros((8, WIDE), F32), halo[:, cols]], axis=0)
    return grad[: T - 16, cols], (grad[T - 16 :, cols].astype(F32) + edge).astype(BF16)


def product(refs, side):
    mine, other, grad, grad_other, halo, halo_other = refs
    cols = MAIN[side]
    right = jnp.concatenate(
        mended(grad, halo, cols) + mended(grad_other, halo_other, cols), axis=0
    )

    def rows(part):
        return nn(jnp.concatenate([mine[PART[part], :], other[PART[part], :]], axis=1), right)

    return rows


def far_kernel(*refs):
    for out, (part, side) in zip(refs[6:], ((2, 0), (2, 1))):
        out[...] = product(refs[:6], side)(part).astype(BF16)


def near_kernel(*refs):
    for out, (part, side) in zip(refs[7:], ((1, 0), (3, 1), (1, 1), (3, 0))):
        out[...] = product(refs[:6], side)(part).astype(out.dtype)


def here_kernel(*refs):
    for out, (part, side) in zip(refs[7:], ((0, 0), (0, 1))):
        out[...] = product(refs[:6], side)(part)


def product_part(kernel, args, ties, types):
    vm = pl.BlockSpec(memory_space=pltpu.VMEM)
    return pl.pallas_call(
        kernel,
        in_specs=[vm] * 6 + [pl.BlockSpec(memory_space=pl.ANY)] * len(ties),
        out_shape=tuple(jax.ShapeDtypeStruct((320, WIDE), one) for one in types),
        compiler_params=params(),
        cost_estimate=cost(2 * 512 * WIDE * 320 * len(types), (3 + len(types)) * 2**20),
    )(*args, *ties)


def join_kernel(count, *refs):
    ins, outs = refs[: 3 * count], refs[3 * count :]
    for i, out in enumerate(outs):
        near, arrived, direct = ins[3 * i : 3 * i + 3]
        size = near.shape[0]
        out[:size, :] = (near[...] + arrived[...].astype(F32)).astype(BF16)
        out[size:, :] = direct[...]


def join(*triples):
    count = len(triples)
    return pl.pallas_call(
        functools.partial(join_kernel, count),
        out_shape=tuple(
            jax.ShapeDtypeStruct((2 * near.shape[0], near.shape[1]), BF16)
            for near, _, _ in triples
        ),
        compiler_params=params(),
        cost_estimate=cost(10**6, 4 * 2**20),
    )(*[one for triple in triples for one in triple])


def turn_kernel(here_a, here_b, up, down, far_up, far_down, near_up, near_down, dir_up, dir_down, a, b):
    size = 4 * ROWS

    def one(r, side):
        rows = slice(ROWS * r, ROWS * (r + 1))
        direct = slice(size + ROWS * r, size + ROWS * (r + 1))
        if side == 0:
            arrived = up[rows, :].astype(F32) + down[direct, :].astype(F32)
            return here_a[rows, :] + arrived
        arrived = down[rows, :].astype(F32) + up[direct, :].astype(F32)
        return here_b[rows, :] + arrived

    far_up[...] = one(2, 0).astype(BF16)
    far_down[...] = one(2, 1).astype(BF16)
    near_up[...] = one(1, 0)
    near_down[...] = one(3, 1)
    dir_up[...] = one(1, 1).astype(BF16)
    dir_down[...] = one(3, 0).astype(BF16)
    a[...] = one(0, 0)
    b[...] = one(0, 1)


def turn_part(here_a, here_b, up, down):
    return pl.pallas_call(
        turn_kernel,
        out_shape=tuple(
            jax.ShapeDtypeStruct((ROWS, WIDE), one)
            for one in (BF16, BF16, F32, F32, BF16, BF16, F32, F32)
        ),
        compiler_params=params(),
        cost_estimate=cost(10**6, 4 * 2**20),
    )(here_a, here_b, up, down)


def last_kernel(
    order, a, b, up, down, here_u, up_u, down_u, c0, c1, c2, c3, grad_wx, grad_wbc, grad_u
):
    norm = (T * SEQ) ** (-0.5)
    first = a[...] + (up[:ROWS, :].astype(F32) + down[ROWS:, :].astype(F32))
    second = b[...] + (down[:ROWS, :].astype(F32) + up[ROWS:, :].astype(F32))
    grad_wx[:, :WIDE] = first * norm
    grad_wx[:, WIDE:] = second * norm
    pieces = []
    for z in range(ZS):
        piece = c0[...]
        for r, one in enumerate((c1, c2, c3)):
            piece = jnp.where(order[r + 1] == z, one[...], piece)
        pieces.append(jnp.concatenate([piece[:, :64], piece[:, 64:]], axis=0) * norm)
    grad_wbc[...] = jnp.concatenate(pieces, axis=1)
    size = here_u.shape[0] // 2
    low = here_u[:size, :] + (up_u[:size, :].astype(F32) + down_u[size:, :].astype(F32))
    high = here_u[size:, :] + (down_u[:size, :].astype(F32) + up_u[size:, :].astype(F32))
    grad_u[:size, :] = low.astype(BF16)
    grad_u[size:, :] = high.astype(BF16)


def last_part(*args):
    vm = pl.BlockSpec(memory_space=pltpu.VMEM)
    return pl.pallas_call(
        last_kernel,
        in_specs=[pl.BlockSpec(memory_space=pltpu.SMEM)] + [vm] * 11,
        out_shape=(
            jax.ShapeDtypeStruct((ROWS, CH), F32),
            jax.ShapeDtypeStruct((ROWS, 2 * STATE), F32),
            jax.ShapeDtypeStruct((D // ZS, T), BF16),
        ),
        compiler_params=params(),
        cost_estimate=cost(10**6, 3 * 2**20),
    )(*args)


def input_kernel(order, w_x, w_bc, grad, halo, shared, tie, *refs):
    del tie
    far_up, far_down, near_up, near_down, dir_up, dir_down, here, held, sems = refs
    size = D // ZS
    half = size // 2
    copies = []
    turn = (2, 1, 3, 0)
    for at, r in enumerate(turn):
        rows = pl.ds(pl.multiple_of(order[r] * size, size), size)
        copies.append(pltpu.make_async_copy(w_x.at[rows, :], held.at[at], sems.at[at]))
        copies[at].start()
    edge = jnp.concatenate([jnp.zeros((8, CH), F32), halo[...]], axis=0)
    last = (grad[T - 16 :, :].astype(F32) + edge).astype(BF16)
    right = jnp.concatenate([grad[: T - 16, :], last], axis=0)
    outs = ((far_up, far_down), (near_up, dir_up), (dir_down, near_down))
    for at, r in enumerate(turn):
        copies[at].wait()
        rows = pl.ds(pl.multiple_of(order[r] * size, size), size)
        part = nt(held[at], right) + nn(w_bc[rows, :], shared[...])
        if r == 0:
            here[...] = part
        else:
            low, high = outs[at]
            low[...] = part[:half].astype(low.dtype)
            high[...] = part[half:].astype(high.dtype)


def input_part(order, w_x, w_bc, grad, halo, shared, tie):
    rows = D // ZS
    vm = pl.BlockSpec(memory_space=pltpu.VMEM)
    sizes = (rows // 2,) * 6 + (rows,)
    types = (BF16, BF16, F32, F32, BF16, BF16, F32)
    return pl.pallas_call(
        input_kernel,
        in_specs=[pl.BlockSpec(memory_space=pltpu.SMEM), pl.BlockSpec(memory_space=pltpu.HBM)]
        + [vm] * 4
        + [pl.BlockSpec(memory_space=pl.ANY)],
        out_shape=tuple(jax.ShapeDtypeStruct((size, T), one) for size, one in zip(sizes, types)),
        scratch_shapes=[pltpu.VMEM((ZS, rows, CH), BF16), pltpu.SemaphoreType.DMA((ZS,))],
        compiler_params=params(20),
        cost_estimate=cost(2 * D * (CH + 256) * T, 10 * 2**20),
    )(order, w_x, w_bc, grad, halo, shared, tie)


def device(x, y, core):
    return ((x % 4) * 4 + y % 4) * 2 + core


def ring(first, by):
    pairs = []
    for x in range(4):
        for y in range(4):
            for core in range(2):
                along_x = (core == 0) == first
                goal = device(x + by, y, core) if along_x else device(x, y + by, core)
                pairs.append((device(x, y, core), goal))
    return pairs


def along(first, by):
    return lambda value: lax.ppermute(value, "seq", ring(first, by))


def along_head(by):
    return lambda value: lax.ppermute(value, "head", [(i, (i + by) % ZS) for i in range(ZS)])


def place_table():
    rows = []
    for place in range(SEQ):
        core, y, x = place % 2, place // 2 % 4, place // 8
        blocks = [
            [device(x + a, y + b, 0) for a in range(4) for b in range(4)],
            [device(x + b, y + a, 1) for a in range(4) for b in range(4)],
        ]
        head = SLICE * place // HEAD_DIM
        bound = HEAD_DIM * (head + 1) - SLICE * place
        rows.append(blocks[core] + blocks[1 - core] + [head, bound])
    return np.array(rows, np.int32)


def head_table():
    return np.array([[(z + r) % ZS for r in range(ZS)] for z in range(ZS)], np.int32)


def body(normed, w_x, w_bc, conv_w, decay_code, step, d_skip, grad_y):
    place = lax.axis_index("seq")
    core = place % 2
    z = lax.axis_index("head")
    order_z = jnp.asarray(head_table())[z]
    table = lax.dynamic_index_in_dim(jnp.asarray(place_table()), place, 0, keepdims=False)
    swap = [(i, i ^ 1) for i in range(SEQ)]

    low = math.log(0.995)
    high = math.log(0.9999)
    rates = low + decay_code.astype(F32)[:, None] / (LEVELS - 1) * (high - low)
    before = lax.ppermute(normed[T - 16 :], "seq", [(i, i + 1) for i in range(SEQ - 1)])

    bmat, cmat, cum, logd, dyt, dywt, msg = front(normed, w_bc, rates, step, grad_y)
    pulls = lax.all_to_all(msg, "seq", 0, 0)
    xgt, slope, xwt, xlt = channels(before, normed, conv_w, cum, logd, w_x)
    back_parts = chain(table, pulls, pulls, xgt, True)
    ds = lax.all_to_all(back_parts, "seq", 0, 0).reshape(CH, STATE)
    dxg, rc, dbc, own = intra(grad_y, dyt, xgt, xwt, xlt, cum, bmat, cmat, back_parts)
    mine, other = select(table, normed, rc)
    other = lax.ppermute(other, "seq", swap)
    ahead = lax.all_to_all(own.reshape(SEQ, SLICE, STATE), "seq", 0, 0)

    dpre, halo, halves, cross = gradients(
        d_skip, ds, bmat, dxg, dyt, xgt, slope, conv_w, cum, logd, mine
    )
    dpre_other = lax.ppermute(dpre, "seq", swap)
    halo_mine = lax.ppermute(halo, "seq", [(i, i - 1) for i in range(1, SEQ)])
    halo_pair = lax.ppermute(halo, "seq", [(i, i - 2) for i in range(2, SEQ, 2)])
    halo_other = jnp.where(core == 0, halo_pair, halo)

    args = (mine, other, dpre, dpre_other, halo_mine, halo_other)
    move = {by: along(True, by) for by in (1, -1)}
    turn = {by: along(False, by) for by in (1, -1)}
    head = {by: along_head(by) for by in (1, -1)}
    far_up, far_down = product_part(far_kernel, args, (), (BF16, BF16))
    ru, rd = move[1](far_up), move[-1](far_down)
    near_up, near_down, dir_up, dir_down = product_part(
        near_kernel, args, (far_up,), (F32, F32, BF16, BF16)
    )
    fore_parts = chain(table, ahead, pulls, near_up, False)
    st = lax.all_to_all(fore_parts, "seq", 0, 0).reshape(CH, STATE)
    up, down = join((near_up, ru, dir_up), (near_down, rd, dir_down))
    ru, rd = move[1](up), move[-1](down)
    here_a, here_b = product_part(here_kernel, args, (up,), (F32, F32))
    shared, *chunks = shared_part(order_z, ds, st, xwt, dywt, dbc, here_a)
    arrived = [along_head(by)(chunks[by]) for by in (1, 2, 3)]
    z_far_up, z_far_down, z_up, z_down, z_dir_up, z_dir_down, z_here = input_part(
        order_z, w_x, w_bc, dpre, halo_mine, shared, here_a
    )
    chunk = (chunks[0] + arrived[0] + arrived[1] + arrived[2]).astype(BF16)
    chunk_other = lax.ppermute(chunk, "seq", swap)
    gls = step_part(st, ds, cmat, dyt, cum, logd, rc, halves, cross, z_here)
    small = small_part(table, mine, other, chunk, chunk_other)
    groups = [[2 * i + c for i in range(16)] for c in range(2)]
    small = lax.all_to_all(small, "seq", 0, 0, axis_index_groups=groups)
    small = jnp.sum(small, axis=0)
    ring = [small] + [along_head(-by)(small) for by in (1, 2, 3)]
    far_up, far_down, near_up, near_down, dir_up, dir_down, here_a, here_b = turn_part(
        here_a, here_b, ru, rd
    )
    ru, rd = turn[1](far_up), turn[-1](far_down)
    zu, zd = head[1](z_far_up), head[-1](z_far_down)
    up, down, z_up, z_down = join(
        (near_up, ru, dir_up),
        (near_down, rd, dir_down),
        (z_up, zu, z_dir_up),
        (z_down, zd, z_dir_down),
    )
    ru, rd = turn[1](up), turn[-1](down)
    zu, zd = head[1](z_up), head[-1](z_down)
    grad_wx, grad_wbc, grad_u = last_part(
        order_z, here_a, here_b, ru, rd, z_here, zu, zd, *ring
    )
    return (grad_u, grad_wx, grad_wbc, gls)


def solution(mesh):
    return jax.shard_map(
        body,
        mesh=mesh,
        in_specs=(
            P("seq", None),
            P(None, "head"),
            P(),
            P(None, "head"),
            P("head"),
            P("head", "seq"),
            P("head"),
            P("seq", "head"),
        ),
        out_specs=(P("head", "seq"), P("seq", "head"), P("seq", None), P("head", "seq")),
        check_vma=False,
    )
```

```python
import functools
import math

import jax
import jax.numpy as jnp
import numpy as np
from jax import lax
from jax.experimental import pallas as pl
from jax.experimental.pallas import tpu as pltpu
from jax.sharding import PartitionSpec as P

D = 2560
HEAD_DIM = 64
STATE = 128
CONV = 4
LEVELS = 256
T = 256
CH = 1280
HEADS = 20
SEQ = 32
ZS = 4
ROWS = 80
SLICE = 40
MSG = 96
BLK = 256
NBLK = CH // BLK
SCALE = STATE ** (-0.5)
F32 = jnp.float32
BF16 = jnp.bfloat16
HIGH = lax.Precision.HIGHEST
NT = (((1,), (1,)), ((), ()))


def nt(a, b):
    return lax.dot_general(a, b, NT, preferred_element_type=F32)


def nn(a, b):
    return jnp.dot(a, b, preferred_element_type=F32)


def split(value):
    high = value.astype(BF16)
    return high, (value - high.astype(F32)).astype(BF16)


def wide(dot, a, b):
    a_high, a_low = split(a)
    b_high, b_low = split(b)
    return dot(a_high, b_high) + (dot(a_low, b_high) + dot(a_high, b_low))


def params(mib=20):
    return pltpu.CompilerParams(vmem_limit_bytes=mib * 2**20)


def cost(flops, nbytes, trans=0):
    return pl.CostEstimate(flops=flops, bytes_accessed=nbytes, transcendentals=trans)


def whole(*shape):
    return pl.BlockSpec(shape, lambda i: (0,) * len(shape))


def triangle(upper):
    row = lax.broadcasted_iota(jnp.int32, (T, T), 0)
    col = lax.broadcasted_iota(jnp.int32, (T, T), 1)
    return jnp.where(row <= col if upper else row >= col, 1.0, 0.0).astype(F32)


def front_part(normed, w_bc, code, step, grad_y, bmat, cmat, cum, logd, dyt, dywt, pulled, turn):
    shared = nn(normed[...], w_bc[...])
    bmat[...] = shared[:, :STATE]
    cmat[...] = shared[:, STATE:]
    c_high, c_low = split(shared[:, STATE:])
    low = math.log(0.995)
    high = math.log(0.9999)
    turn[...] = jnp.zeros((128, 128), F32)
    turn[0:1, :HEADS] = code[...].astype(F32)
    codes = turn[...].T[:HEADS, 0:1]
    logs = (low + codes / (LEVELS - 1) * (high - low)) * step[...]
    logd[...] = logs
    cums = jnp.dot(logs, triangle(True), precision=HIGH, preferred_element_type=F32)
    cum[...] = cums
    grown = jnp.exp(cums)
    weight = grown * SCALE
    for pair in range(HEADS // 2):
        rows = slice(128 * pair, 128 * pair + 128)
        tile = grad_y[:, rows].astype(F32).T
        dyt[rows, :] = tile.astype(BF16)
        tile = jnp.concatenate(
            [
                tile[:64] * weight[2 * pair : 2 * pair + 1],
                tile[64:] * weight[2 * pair + 1 : 2 * pair + 2],
            ],
            axis=0,
        )
        high, low = split(tile)
        dywt[rows, :] = high
        pulled[rows, :] = nn(high, c_high) + (nn(low, c_high) + nn(high, c_low))
    turn[...] = jnp.zeros((128, 128), F32)
    turn[:HEADS, :] = grown[:, 128:]
    through = turn[...].T[127:, :]
    high = through.astype(BF16).astype(F32)
    middle = (through - high).astype(BF16).astype(F32)
    row = lax.broadcasted_iota(jnp.int32, (MSG - 2 * SLICE, STATE), 0)
    rest = jnp.where(row == 2, through - high - middle, 0.0)
    return jnp.where(row == 0, high, jnp.where(row == 1, middle, rest))


def chain_kernel(table, recv, tie, out, turn):
    del tie
    turn[...] = jnp.zeros((128, 128), F32)
    parts = []
    for k in range(SEQ):
        one = recv[k].astype(F32)
        parts.append((one[:SLICE], one[SLICE : 2 * SLICE]))
        turn[k : k + 1, :] = jnp.sum(one[2 * SLICE :], axis=0, keepdims=True)
    turn[...] = turn[...].T
    head = table[32]
    row = lax.broadcasted_iota(jnp.int32, (SLICE, 128), 0)
    cols = jnp.where(row < table[33], turn[pl.ds(head, 1), :], turn[pl.ds(head + 1, 1), :])
    pulled = jnp.zeros((SLICE, STATE), F32)
    pulls = [None] * SEQ
    for k in range(SEQ - 1, -1, -1):
        pulls[k] = pulled
        pulled = cols[:, k : k + 1] * pulled + parts[k][0]
    state = jnp.zeros((SLICE, STATE), F32)
    for k in range(SEQ):
        out[k] = jnp.concatenate([pulls[k], state], axis=0).astype(BF16)
        state = cols[:, k : k + 1] * state + parts[k][1]


def chain(table, recv, tie):
    return pl.pallas_call(
        chain_kernel,
        grid=(1,),
        in_specs=[
            pl.BlockSpec(memory_space=pltpu.SMEM),
            whole(SEQ, MSG, STATE),
            pl.BlockSpec(memory_space=pl.ANY),
        ],
        out_specs=whole(SEQ, 2 * SLICE, STATE),
        out_shape=jax.ShapeDtypeStruct((SEQ, 2 * SLICE, STATE), BF16),
        scratch_shapes=[pltpu.VMEM((128, 128), F32)],
        compiler_params=params(),
        cost_estimate=cost(10**6, 3 * 2**20),
    )(table, recv, tie)


def early_kernel(
    code, before, normed, w_bc, step, grad_y, conv_w, w_x, *refs
):
    bmat, cmat, cum, logd, dyt, dywt, xgt, xlt, slope, xwt, msg = refs[:11]
    pulled, turn, ext, pre, own, held, sems = refs[11:]
    copies = [
        pltpu.make_async_copy(w_x.at[:, pl.ds(BLK * i, BLK)], held.at[i], sems.at[i])
        for i in range(NBLK)
    ]
    for one in copies:
        one.start()
    ext[:16, :] = before[...]
    ext[16:, :] = normed[...]
    through = front_part(
        normed, w_bc, code, step, grad_y, bmat, cmat, cum, logd, dyt, dywt, pulled, turn
    )
    b_high, b_low = split(bmat[...])
    for i in range(NBLK + 1):
        if i < NBLK:
            copies[i].wait()
            pre[i % 2] = nn(ext[...], held[i]).astype(BF16).astype(F32)
        if i == 0:
            continue
        block = i - 1
        past = pre.at[block % 2]
        cols = slice(BLK * block, BLK * (block + 1))
        total = conv_w[0:1, cols] * past[16 : 16 + T, :]
        for tap in range(1, CONV):
            total = total + conv_w[tap : tap + 1, cols] * past[16 - tap : 16 - tap + T, :]
        sig = 0.5 * jnp.tanh(0.5 * total) + 0.5
        xt = (total * sig).T
        slope[:, cols] = sig * (1.0 + total * (1.0 - sig))
        parts = []
        for q in range(BLK // HEAD_DIM):
            h = block * (BLK // HEAD_DIM) + q
            rows = slice(64 * h, 64 * h + 64)
            gain = jnp.sqrt(-2.0 * logd[h : h + 1, :])
            cums = cum[h : h + 1, :]
            tail = jnp.exp(cums[:, T - 1 :] - cums)
            xg = xt[64 * q : 64 * q + 64] * gain
            xgt[rows, :], xlt[rows, :] = split(xg)
            parts.append(xg * tail)
        high, low = split(jnp.concatenate(parts, axis=0))
        xwt[cols, :] = high
        own[cols, :] = nn(high, b_high) + (nn(low, b_high) + nn(high, b_low))
    for k in range(SEQ):
        rows = slice(SLICE * k, SLICE * (k + 1))
        msg[k] = jnp.concatenate([pulled[rows, :], own[rows, :], through], axis=0).astype(BF16)


def early(code, before, normed, w_bc, step, grad_y, conv_w, w_x):
    vm = pl.BlockSpec(memory_space=pltpu.VMEM)
    return pl.pallas_call(
        early_kernel,
        in_specs=[vm] * 7 + [pl.BlockSpec(memory_space=pl.ANY)],
        out_shape=(
            jax.ShapeDtypeStruct((T, STATE), F32),
            jax.ShapeDtypeStruct((T, STATE), F32),
            jax.ShapeDtypeStruct((HEADS, T), F32),
            jax.ShapeDtypeStruct((HEADS, T), F32),
            jax.ShapeDtypeStruct((CH, T), BF16),
            jax.ShapeDtypeStruct((CH, T), BF16),
            jax.ShapeDtypeStruct((CH, T), BF16),
            jax.ShapeDtypeStruct((CH, T), BF16),
            jax.ShapeDtypeStruct((T, CH), F32),
            jax.ShapeDtypeStruct((CH, T), BF16),
            jax.ShapeDtypeStruct((SEQ, MSG, STATE), BF16),
        ),
        scratch_shapes=[
            pltpu.VMEM((CH, STATE), F32),
            pltpu.VMEM((128, 128), F32),
            pltpu.VMEM((T + 16, D), BF16),
            pltpu.VMEM((2, T + 16, BLK), F32),
            pltpu.VMEM((CH, STATE), F32),
            pltpu.VMEM((NBLK, D, BLK), BF16),
            pltpu.SemaphoreType.DMA((NBLK,)),
        ],
        compiler_params=params(56),
        cost_estimate=cost(2 * T * D * (CH + 256), 16 * 2**20, T * CH),
    )(code, before, normed, w_bc, step, grad_y, conv_w, w_x)


def intra_kernel(grad_y, dyt, xgt, cum, bmat, cmat, tie, dxg, rc, dbc, gram, dgram):
    del tie
    step = pl.program_id(0)

    @pl.when(step == 0)
    def _():
        gram[...] = wide(nt, cmat[...], bmat[...]) * SCALE
        dgram[...] = jnp.zeros((T, T), F32)

    half = T // 2
    row = lax.broadcasted_iota(jnp.int32, (half, half), 0)
    col = lax.broadcasted_iota(jnp.int32, (half, half), 1)
    keep = row >= col
    blank = jnp.zeros((HEAD_DIM, T), BF16)
    corner = jnp.zeros((half, half), BF16)
    for q in range(BLK // HEAD_DIM):
        head = pl.ds(step * (BLK // HEAD_DIM) + q, 1)
        rows = slice(64 * q, 64 * q + 64)
        cums = cum[head, :]
        column = jnp.broadcast_to(cums, (half, T)).T
        l00 = jnp.exp(jnp.where(keep, column[:half] - cums[:, :half], -1e30))
        l10 = jnp.exp(column[half:] - cums[:, :half])
        l11 = jnp.exp(jnp.where(keep, column[half:] - cums[:, half:], -1e30))
        m00 = (l00 * gram[:half, :half]).astype(BF16)
        m10 = (l10 * gram[half:, :half]).astype(BF16)
        m11 = (l11 * gram[half:, half:]).astype(BF16)
        mat = jnp.concatenate(
            [jnp.concatenate([m00, corner], axis=1), jnp.concatenate([m10, m11], axis=1)], axis=0
        )
        dy = dyt[rows, :]
        xg = xgt[rows, :]
        pair = slice(128 * (q // 2), 128 * (q // 2) + 128)
        right = jnp.concatenate([xg, blank] if q % 2 == 0 else [blank, xg], axis=0)
        dm0 = nn(grad_y[:, pair], right[:, :half])
        dm1 = nn(grad_y[half:, pair], right[:, half:])
        dgram[:half, :half] += l00 * dm0[:half]
        dgram[half:, :half] += l10 * dm0[half:]
        dgram[half:, half:] += l11 * dm1
        back = nn(dy, mat)
        yin = nt(xg, mat)
        dxg[rows, :] = back
        rc[head, :] = jnp.sum(dy.astype(F32) * yin - xg.astype(F32) * back, axis=0, keepdims=True)

    @pl.when(step == NBLK - 1)
    def _():
        dg = dgram[...] * SCALE
        dbc[:STATE, :] = wide(nn, cmat[...].T, dg)
        dbc[STATE:, :] = wide(nn, dg, bmat[...]).T


def intra(grad_y, dyt, xgt, cum, bmat, cmat, tie):
    rows = pl.BlockSpec((BLK, T), lambda i: (i, 0))
    return pl.pallas_call(
        intra_kernel,
        grid=(NBLK,),
        in_specs=[
            pl.BlockSpec((T, BLK), lambda i: (0, i)),
            rows,
            rows,
            whole(HEADS, T),
            whole(T, STATE),
            whole(T, STATE),
            pl.BlockSpec(memory_space=pl.ANY),
        ],
        out_specs=(rows, whole(HEADS, T), whole(2 * STATE, T)),
        out_shape=(
            jax.ShapeDtypeStruct((CH, T), F32),
            jax.ShapeDtypeStruct((HEADS, T), F32),
            jax.ShapeDtypeStruct((2 * STATE, T), F32),
        ),
        scratch_shapes=[pltpu.VMEM((T, T), F32), pltpu.VMEM((T, T), F32)],
        compiler_params=params(),
        cost_estimate=cost(HEADS * 2 * T * T * 64 * 8, 4 * 2**20, HEADS * T * T),
    )(grad_y, dyt, xgt, cum, bmat, cmat, tie)


def shared_kernel(back, xwt, dywt, dbc, ds, st, shared):
    for k in range(SEQ):
        rows = slice(SLICE * k, SLICE * (k + 1))
        both = back[k].astype(F32)
        ds[rows, :] = both[:SLICE]
        st[rows, :] = both[SLICE:]
    for at, (state, tokens) in enumerate(((ds, xwt), (st, dywt))):
        turned = state[...].T.astype(BF16)
        part = nn(turned, tokens[...]) + dbc[STATE * at : STATE * (at + 1), :]
        shared[:, STATE * at : STATE * (at + 1)] = part.T.astype(BF16)


def shared_part(back, xwt, dywt, dbc):
    return pl.pallas_call(
        shared_kernel,
        out_shape=(
            jax.ShapeDtypeStruct((CH, STATE), F32),
            jax.ShapeDtypeStruct((CH, STATE), F32),
            jax.ShapeDtypeStruct((T, 2 * STATE), BF16),
        ),
        compiler_params=params(),
        cost_estimate=cost(4 * CH * T * 128, 4 * 2**20),
    )(back, xwt, dywt, dbc)


def grad_kernel(
    skip, bmat, taps, cum, logd, tie, back, dxg, dyt, xgt, xlt, slope, dpre, halo, halves, cross, *refs
):
    del tie
    ext, sems, *held = refs
    copies = []
    for i in range(NBLK):
        rows = pl.ds(BLK * i, BLK)
        parts = [one.at[rows, :] for one in (back, dxg, dyt, xgt, xlt)] + [slope.at[:, rows]]
        copies.append(
            [
                pltpu.make_async_copy(part, buffer.at[i], sems.at[i, at])
                for at, (part, buffer) in enumerate(zip(parts, held))
            ]
        )
        for one in copies[i]:
            one.start()
    b_high, b_low = split(bmat[...])
    for i in range(NBLK):
        for one in copies[i]:
            one.wait()
        back_i, dxg_i, dyt_i, xgt_i, xlt_i, slope_i = [buffer.at[i] for buffer in held]
        d_high, d_low = split(back_i[...])
        later = nt(d_high, b_high) + (nt(d_low, b_high) + nt(d_high, b_low))
        parts = []
        for q in range(BLK // HEAD_DIM):
            index = i * (BLK // HEAD_DIM) + q
            head = slice(index, index + 1)
            rows = slice(64 * q, 64 * q + 64)
            gain = jnp.sqrt(-2.0 * logd[head, :])
            cums = cum[head, :]
            tail = jnp.exp(cums[:, T - 1 :] - cums)
            inter = later[rows] * tail
            whole_dxg = dxg_i[rows, :] + inter
            xg = xgt_i[rows, :].astype(F32) + xlt_i[rows, :].astype(F32)
            cross[head, :] = jnp.sum(xg * inter, axis=0, keepdims=True)
            halves[head, :] = 0.5 * jnp.sum(xg * whole_dxg, axis=0, keepdims=True)
            parts.append(gain * whole_dxg + skip[index] * dyt_i[rows, :].astype(F32))
        cols = slice(BLK * i, BLK * (i + 1))
        wide_i = ext.at[i % 2]
        wide_i[:8, :] = jnp.zeros((8, BLK), F32)
        wide_i[8 : T + 8, :] = jnp.concatenate(parts, axis=0).T * slope_i[...]
        wide_i[T + 8 :, :] = jnp.zeros((8, BLK), F32)
        total = taps[0:1, cols] * wide_i[8 : T + 8, :]
        edge = taps[0:1, cols] * wide_i[:8, :]
        for tap in range(1, CONV):
            weight = taps[tap : tap + 1, cols]
            total = total + weight * wide_i[8 + tap : T + 8 + tap, :]
            edge = edge + weight * wide_i[tap : 8 + tap, :]
        dpre[:, cols] = total.astype(BF16)
        halo[:, cols] = edge


def gradients(skip, back, bmat, dxg, dyt, xgt, xlt, slope, taps, cum, logd, tie):
    vm = pl.BlockSpec(memory_space=pltpu.VMEM)
    away = pl.BlockSpec(memory_space=pl.ANY)
    return pl.pallas_call(
        grad_kernel,
        in_specs=[pl.BlockSpec(memory_space=pltpu.SMEM)] + [vm] * 4 + [away] * 7,
        out_shape=(
            jax.ShapeDtypeStruct((T, CH), BF16),
            jax.ShapeDtypeStruct((8, CH), F32),
            jax.ShapeDtypeStruct((HEADS, T), F32),
            jax.ShapeDtypeStruct((HEADS, T), F32),
        ),
        scratch_shapes=[
            pltpu.VMEM((2, T + 16, BLK), F32),
            pltpu.SemaphoreType.DMA((NBLK, 6)),
            pltpu.VMEM((NBLK, BLK, STATE), F32),
            pltpu.VMEM((NBLK, BLK, T), F32),
            pltpu.VMEM((NBLK, BLK, T), BF16),
            pltpu.VMEM((NBLK, BLK, T), BF16),
            pltpu.VMEM((NBLK, BLK, T), BF16),
            pltpu.VMEM((NBLK, T, BLK), F32),
        ],
        compiler_params=params(56),
        cost_estimate=cost(4 * CH * T * 128, 6 * 2**20, T * HEADS),
    )(skip, bmat, taps, cum, logd, tie, back, dxg, dyt, xgt, xlt, slope)


def step_kernel(fore, back, cmat, dyt, cum, logd, rc, halves, cross, tie, gls):
    del tie
    before = wide(nt, fore[...], cmat[...])
    cums = cum[...]
    inner = []
    through = []
    for h in range(HEADS):
        rows = slice(64 * h, 64 * h + 64)
        inner.append(jnp.sum(dyt[rows, :].astype(F32) * before[rows], axis=0, keepdims=True))
        both = jnp.sum(fore[rows, :] * back[rows, :], axis=0, keepdims=True)
        through.append(jnp.sum(both, axis=1, keepdims=True))
    arriving = rc[...] + jnp.exp(cums) * SCALE * jnp.concatenate(inner, axis=0)
    later = jnp.dot(arriving, triangle(False), precision=HIGH, preferred_element_type=F32)
    crossing = cross[...]
    earlier = (
        jnp.dot(crossing, triangle(True), precision=HIGH, preferred_element_type=F32) - crossing
    )
    kept = jnp.exp(cums[:, T - 1 :]) * jnp.concatenate(through, axis=0)
    gls[...] = logd[...] * (later + earlier + kept) + halves[...]


def step_part(fore, back, cmat, dyt, cum, logd, rc, halves, cross, tie):
    vm = pl.BlockSpec(memory_space=pltpu.VMEM)
    return pl.pallas_call(
        step_kernel,
        in_specs=[vm] * 9 + [pl.BlockSpec(memory_space=pl.ANY)],
        out_shape=jax.ShapeDtypeStruct((HEADS, T), F32),
        compiler_params=params(),
        cost_estimate=cost(4 * CH * T * 128, 4 * 2**20),
    )(fore, back, cmat, dyt, cum, logd, rc, halves, cross, tie)


def select_kernel(order, normed, tie, mine, other, flip):
    del tie
    for k in range(D // 128):
        cols = slice(128 * k, 128 * k + 128)
        flip[cols, :] = normed[:, cols].astype(F32).T.astype(BF16)
    for k in range(16):
        rows = slice(ROWS * k, ROWS * (k + 1))
        mine[rows, :] = flip[pl.ds(pl.multiple_of(order[k] * ROWS, 16), ROWS), :]
        other[rows, :] = flip[pl.ds(pl.multiple_of(order[16 + k] * ROWS, 16), ROWS), :]


def select(order, normed, tie):
    vm = pl.BlockSpec(memory_space=pltpu.VMEM)
    return pl.pallas_call(
        select_kernel,
        in_specs=[pl.BlockSpec(memory_space=pltpu.SMEM), vm, pl.BlockSpec(memory_space=pl.ANY)],
        out_shape=(jax.ShapeDtypeStruct((CH, T), BF16), jax.ShapeDtypeStruct((CH, T), BF16)),
        scratch_shapes=[pltpu.VMEM((D, T), BF16)],
        compiler_params=params(),
        cost_estimate=cost(10**6, 3 * 2**20),
    )(order, normed, tie)


PART = [slice(320 * r, 320 * (r + 1)) for r in range(4)]
WIDE = 640
FULL = WIDE + STATE
MAIN = [slice(0, WIDE), slice(WIDE, 2 * WIDE)]
EXTRA = [slice(0, STATE), slice(STATE, 2 * STATE)]


def mended(grad, halo, cols):
    edge = jnp.concatenate([jnp.zeros((8, WIDE), F32), halo[:, cols]], axis=0)
    return grad[: T - 16, cols], (grad[T - 16 :, cols].astype(F32) + edge).astype(BF16)


def product(refs, side):
    mine, other, grad, grad_other, halo, halo_other, shared, shared_other = refs
    cols = MAIN[side]
    right = jnp.concatenate(
        mended(grad, halo, cols) + mended(grad_other, halo_other, cols), axis=0
    )
    extra = jnp.concatenate([shared[:, EXTRA[side]], shared_other[:, EXTRA[side]]], axis=0)

    def rows(part):
        left = jnp.concatenate([mine[PART[part], :], other[PART[part], :]], axis=1)
        return nn(left, right), nn(left, extra)

    return rows


def far_kernel(*refs):
    for out, (part, side) in zip(refs[8:], ((2, 0), (2, 1))):
        main, extra = product(refs[:8], side)(part)
        out[:, :WIDE] = main.astype(BF16)
        out[:, WIDE:] = extra.astype(BF16)


def near_kernel(*refs):
    order = ((1, 0), (3, 1), (1, 1), (3, 0), (0, 0), (0, 1))
    for out, (part, side) in zip(refs[9:], order):
        main, extra = product(refs[:8], side)(part)
        out[:, :WIDE] = main.astype(out.dtype)
        out[:, WIDE:] = extra.astype(out.dtype)


def product_part(kernel, args, ties, types):
    vm = pl.BlockSpec(memory_space=pltpu.VMEM)
    return pl.pallas_call(
        kernel,
        in_specs=[vm] * 8 + [pl.BlockSpec(memory_space=pl.ANY)] * len(ties),
        out_shape=tuple(jax.ShapeDtypeStruct((320, FULL), one) for one in types),
        compiler_params=params(),
        cost_estimate=cost(2 * 512 * FULL * 320 * len(types), (3 + len(types)) * 2**20),
    )(*args, *ties)


def join_kernel(count, *refs):
    ins, outs = refs[: 3 * count], refs[3 * count :]
    for i, out in enumerate(outs):
        near, arrived, direct = ins[3 * i : 3 * i + 3]
        size = near.shape[0]
        out[:size, :] = (near[...] + arrived[...].astype(F32)).astype(BF16)
        out[size:, :] = direct[...]


def join(*triples):
    count = len(triples)
    return pl.pallas_call(
        functools.partial(join_kernel, count),
        out_shape=tuple(
            jax.ShapeDtypeStruct((2 * near.shape[0], near.shape[1]), BF16)
            for near, _, _ in triples
        ),
        compiler_params=params(),
        cost_estimate=cost(10**6, 4 * 2**20),
    )(*[one for triple in triples for one in triple])


def turn_kernel(here_a, here_b, up, down, far_up, far_down, near_up, near_down, dir_up, dir_down, a, b):
    size = 4 * ROWS

    def one(r, side):
        rows = slice(ROWS * r, ROWS * (r + 1))
        direct = slice(size + ROWS * r, size + ROWS * (r + 1))
        if side == 0:
            arrived = up[rows, :].astype(F32) + down[direct, :].astype(F32)
            return here_a[rows, :] + arrived
        arrived = down[rows, :].astype(F32) + up[direct, :].astype(F32)
        return here_b[rows, :] + arrived

    far_up[...] = one(2, 0).astype(BF16)
    far_down[...] = one(2, 1).astype(BF16)
    near_up[...] = one(1, 0)
    near_down[...] = one(3, 1)
    dir_up[...] = one(1, 1).astype(BF16)
    dir_down[...] = one(3, 0).astype(BF16)
    a[...] = one(0, 0)
    b[...] = one(0, 1)


def turn_part(here_a, here_b, up, down):
    return pl.pallas_call(
        turn_kernel,
        out_shape=tuple(
            jax.ShapeDtypeStruct((ROWS, FULL), one)
            for one in (BF16, BF16, F32, F32, BF16, BF16, F32, F32)
        ),
        compiler_params=params(),
        cost_estimate=cost(10**6, 4 * 2**20),
    )(here_a, here_b, up, down)


def last_kernel(a, b, up, down, here_u, up_u, down_u, grad_wx, grad_wbc, grad_u):
    norm = (T * SEQ) ** (-0.5)
    first = a[...] + (up[:ROWS, :].astype(F32) + down[ROWS:, :].astype(F32))
    second = b[...] + (down[:ROWS, :].astype(F32) + up[ROWS:, :].astype(F32))
    grad_wx[:, :WIDE] = first[:, :WIDE] * norm
    grad_wx[:, WIDE:] = second[:, :WIDE] * norm
    grad_wbc[:, :STATE] = first[:, WIDE:] * norm
    grad_wbc[:, STATE:] = second[:, WIDE:] * norm
    size = here_u.shape[0] // 2
    low = here_u[:size, :] + (up_u[:size, :].astype(F32) + down_u[size:, :].astype(F32))
    high = here_u[size:, :] + (down_u[:size, :].astype(F32) + up_u[size:, :].astype(F32))
    grad_u[:size, :] = low.astype(BF16)
    grad_u[size:, :] = high.astype(BF16)


def last_part(*args):
    return pl.pallas_call(
        last_kernel,
        out_shape=(
            jax.ShapeDtypeStruct((ROWS, CH), F32),
            jax.ShapeDtypeStruct((ROWS, 2 * STATE), F32),
            jax.ShapeDtypeStruct((D // ZS, T), BF16),
        ),
        compiler_params=params(),
        cost_estimate=cost(10**6, 3 * 2**20),
    )(*args)


def input_kernel(order, w_x, w_bc, grad, halo, shared, tie, *refs):
    del tie
    far_up, far_down, near_up, near_down, dir_up, dir_down, here, held, small, sems = refs
    size = D // ZS
    half = size // 2
    copies = []
    turn = (2, 1, 3, 0)
    for at, r in enumerate(turn):
        rows = pl.ds(pl.multiple_of(order[r] * size, size), size)
        copies.append(pltpu.make_async_copy(w_x.at[rows, :], held.at[at], sems.at[at]))
        copies[at].start()
    rows = pl.ds(pl.multiple_of(order[0] * size, size), size)
    last_copy = pltpu.make_async_copy(w_bc.at[rows, :], small, sems.at[ZS])
    last_copy.start()
    edge = jnp.concatenate([jnp.zeros((8, CH), F32), halo[...]], axis=0)
    last = (grad[T - 16 :, :].astype(F32) + edge).astype(BF16)
    right = jnp.concatenate([grad[: T - 16, :], last], axis=0)
    outs = ((far_up, far_down), (near_up, dir_up), (dir_down, near_down))
    for at, r in enumerate(turn):
        copies[at].wait()
        part = nt(held[at], right)
        if r == 0:
            last_copy.wait()
            here[...] = part + nt(small[...], shared[...])
        else:
            low, high = outs[at]
            low[...] = part[:half].astype(low.dtype)
            high[...] = part[half:].astype(high.dtype)


def input_part(order, w_x, w_bc, grad, halo, shared, tie):
    rows = D // ZS
    vm = pl.BlockSpec(memory_space=pltpu.VMEM)
    away = pl.BlockSpec(memory_space=pl.ANY)
    sizes = (rows // 2,) * 6 + (rows,)
    types = (BF16, BF16, F32, F32, BF16, BF16, F32)
    return pl.pallas_call(
        input_kernel,
        in_specs=[pl.BlockSpec(memory_space=pltpu.SMEM), away, away, vm, vm, vm, away],
        out_shape=tuple(jax.ShapeDtypeStruct((size, T), one) for size, one in zip(sizes, types)),
        scratch_shapes=[
            pltpu.VMEM((ZS, rows, CH), BF16),
            pltpu.VMEM((rows, 2 * STATE), BF16),
            pltpu.SemaphoreType.DMA((ZS + 1,)),
        ],
        compiler_params=params(48),
        cost_estimate=cost(2 * D * (CH + 64) * T, 10 * 2**20),
    )(order, w_x, w_bc, grad, halo, shared, tie)


def device(x, y, core):
    return ((x % 4) * 4 + y % 4) * 2 + core


def ring(first, by):
    pairs = []
    for x in range(4):
        for y in range(4):
            for core in range(2):
                along_x = (core == 0) == first
                goal = device(x + by, y, core) if along_x else device(x, y + by, core)
                pairs.append((device(x, y, core), goal))
    return pairs


def along(first, by):
    return lambda value: lax.ppermute(value, "seq", ring(first, by))


def along_head(by):
    return lambda value: lax.ppermute(value, "head", [(i, (i + by) % ZS) for i in range(ZS)])


def place_table():
    rows = []
    for place in range(SEQ):
        core, y, x = place % 2, place // 2 % 4, place // 8
        blocks = [
            [device(x + a, y + b, 0) for a in range(4) for b in range(4)],
            [device(x + b, y + a, 1) for a in range(4) for b in range(4)],
        ]
        head = SLICE * place // HEAD_DIM
        bound = HEAD_DIM * (head + 1) - SLICE * place
        rows.append(blocks[core] + blocks[1 - core] + [head, bound])
    return np.array(rows, np.int32)


def full_table():
    order = [[(z + r) % ZS for r in range(ZS)] for z in range(ZS)]
    return np.array([[list(one) + o for o in order] for one in place_table()], np.int32)


def body(normed, w_x, w_bc, conv_w, decay_code, step, d_skip, grad_y):
    place = lax.axis_index("seq")
    core = place % 2
    z = lax.axis_index("head")
    table = jnp.asarray(full_table())[place, z]
    order_z = table[34:]
    swap = [(i, i ^ 1) for i in range(SEQ)]

    before = lax.ppermute(normed[T - 16 :], "seq", [(i, i + 1) for i in range(SEQ - 1)])

    bmat, cmat, cum, logd, dyt, dywt, xgt, xlt, slope, xwt, msg = early(
        decay_code[None, :], before, normed, w_bc, step, grad_y, conv_w, w_x
    )
    recv = lax.all_to_all(msg, "seq", 0, 0)
    mine, other = select(table, normed, msg)
    other = lax.ppermute(other, "seq", swap)
    dxg, rc, dbc = intra(grad_y, dyt, xgt, cum, bmat, cmat, mine)
    back = lax.all_to_all(chain(table, recv, rc), "seq", 0, 0)

    ds, st, shared = shared_part(back, xwt, dywt, dbc)
    others = [along_head(by)(shared) for by in (1, 2, 3)]
    dpre, halo, halves, cross = gradients(
        d_skip, ds, bmat, dxg, dyt, xgt, xlt, slope, conv_w, cum, logd, st
    )
    dpre_other = lax.ppermute(dpre, "seq", swap)
    halo_mine = lax.ppermute(halo, "seq", [(i, i - 1) for i in range(1, SEQ)])
    halo_pair = lax.ppermute(halo, "seq", [(i, i - 2) for i in range(2, SEQ, 2)])
    halo_other = jnp.where(core == 0, halo_pair, halo)
    one, two, three, _ = lax.optimization_barrier((*others, halo))
    near_pair = shared.astype(F32) + two.astype(F32)
    far_pair = one.astype(F32) + three.astype(F32)
    shared = (near_pair + far_pair).astype(BF16)
    shared_other = lax.ppermute(shared, "seq", swap)

    args = (mine, other, dpre, dpre_other, halo_mine, halo_other, shared, shared_other)
    move = {by: along(True, by) for by in (1, -1)}
    turn = {by: along(False, by) for by in (1, -1)}
    head = {by: along_head(by) for by in (1, -1)}
    far_up, far_down = product_part(far_kernel, args, (), (BF16, BF16))
    ru, rd = move[1](far_up), move[-1](far_down)
    near_up, near_down, dir_up, dir_down, here_a, here_b = product_part(
        near_kernel, args, (far_up,), (F32, F32, BF16, BF16, F32, F32)
    )
    up, down = join((near_up, ru, dir_up), (near_down, rd, dir_down))
    ru, rd = move[1](up), move[-1](down)
    z_far_up, z_far_down, z_up, z_down, z_dir_up, z_dir_down, z_here = input_part(
        order_z, w_x, w_bc, dpre, halo_mine, shared, up
    )
    gls = step_part(st, ds, cmat, dyt, cum, logd, rc, halves, cross, z_here)
    far_up, far_down, near_up, near_down, dir_up, dir_down, here_a, here_b = turn_part(
        here_a, here_b, ru, rd
    )
    ru, rd = turn[1](far_up), turn[-1](far_down)
    zu, zd = head[1](z_far_up), head[-1](z_far_down)
    z_up, z_down = join((z_up, zu, z_dir_up), (z_down, zd, z_dir_down))
    zu, zd = head[1](z_up), head[-1](z_down)
    up, down = join((near_up, ru, dir_up), (near_down, rd, dir_down))
    ru, rd = turn[1](up), turn[-1](down)
    grad_wx, grad_wbc, grad_u = last_part(here_a, here_b, ru, rd, z_here, zu, zd)
    return (grad_u, grad_wx, grad_wbc, gls)


def solution(mesh):
    return jax.shard_map(
        body,
        mesh=mesh,
        in_specs=(
            P("seq", None),
            P(None, "head"),
            P(),
            P(None, "head"),
            P("head"),
            P("head", "seq"),
            P("head"),
            P("seq", "head"),
        ),
        out_specs=(P("head", "seq"), P("seq", "head"), P("seq", None), P("head", "seq")),
        check_vma=False,
    )
```

```python
import functools
import math

import jax
import jax.numpy as jnp
import numpy as np
from jax import lax
from jax.experimental import pallas as pl
from jax.experimental.pallas import tpu as pltpu
from jax.sharding import PartitionSpec as P

D = 2560
HEAD_DIM = 64
STATE = 128
CONV = 4
LEVELS = 256
T = 256
CH = 1280
HEADS = 20
SEQ = 32
ZS = 4
ROWS = 80
SLICE = 40
MSG = 96
BLK = 256
NBLK = CH // BLK
SCALE = STATE ** (-0.5)
F32 = jnp.float32
BF16 = jnp.bfloat16
HIGH = lax.Precision.HIGHEST
NT = (((1,), (1,)), ((), ()))


def nt(a, b):
    return lax.dot_general(a, b, NT, preferred_element_type=F32)


def nn(a, b):
    return jnp.dot(a, b, preferred_element_type=F32)


def split(value):
    high = value.astype(BF16)
    return high, (value - high.astype(F32)).astype(BF16)


def wide(dot, a, b):
    a_high, a_low = split(a)
    b_high, b_low = split(b)
    return dot(a_high, b_high) + (dot(a_low, b_high) + dot(a_high, b_low))


def params(mib=20):
    return pltpu.CompilerParams(vmem_limit_bytes=mib * 2**20)


def cost(flops, nbytes, trans=0):
    return pl.CostEstimate(flops=flops, bytes_accessed=nbytes, transcendentals=trans)


def whole(*shape):
    return pl.BlockSpec(shape, lambda i: (0,) * len(shape))


def triangle(upper):
    row = lax.broadcasted_iota(jnp.int32, (T, T), 0)
    col = lax.broadcasted_iota(jnp.int32, (T, T), 1)
    return jnp.where(row <= col if upper else row >= col, 1.0, 0.0).astype(F32)


def front_part(normed, w_bc, code, step, grad_y, bmat, cmat, cum, logd, dyt, dywt, pulled, turn):
    shared = nn(normed[...], w_bc[...])
    bmat[...] = shared[:, :STATE]
    cmat[...] = shared[:, STATE:]
    c_high, c_low = split(shared[:, STATE:])
    low = math.log(0.995)
    high = math.log(0.9999)
    turn[...] = jnp.zeros((128, 128), F32)
    turn[0:1, :HEADS] = code[...].astype(F32)
    codes = turn[...].T[:HEADS, 0:1]
    logs = (low + codes / (LEVELS - 1) * (high - low)) * step[...]
    logd[...] = logs
    cums = jnp.dot(logs, triangle(True), precision=HIGH, preferred_element_type=F32)
    cum[...] = cums
    grown = jnp.exp(cums)
    weight = grown * SCALE
    for pair in range(HEADS // 2):
        rows = slice(128 * pair, 128 * pair + 128)
        tile = grad_y[:, rows].astype(F32).T
        dyt[rows, :] = tile.astype(BF16)
        tile = jnp.concatenate(
            [
                tile[:64] * weight[2 * pair : 2 * pair + 1],
                tile[64:] * weight[2 * pair + 1 : 2 * pair + 2],
            ],
            axis=0,
        )
        high, low = split(tile)
        dywt[rows, :] = high
        pulled[rows, :] = nn(high, c_high) + (nn(low, c_high) + nn(high, c_low))
    turn[...] = jnp.zeros((128, 128), F32)
    turn[:HEADS, :] = grown[:, 128:]
    through = turn[...].T[127:, :]
    high = through.astype(BF16).astype(F32)
    middle = (through - high).astype(BF16).astype(F32)
    row = lax.broadcasted_iota(jnp.int32, (MSG - 2 * SLICE, STATE), 0)
    rest = jnp.where(row == 2, through - high - middle, 0.0)
    return jnp.where(row == 0, high, jnp.where(row == 1, middle, rest))


def chain_kernel(table, recv, tie, out, turn):
    del tie
    turn[...] = jnp.zeros((128, 128), F32)
    parts = []
    for k in range(SEQ):
        one = recv[k].astype(F32)
        parts.append((one[:SLICE], one[SLICE : 2 * SLICE]))
        turn[k : k + 1, :] = jnp.sum(one[2 * SLICE :], axis=0, keepdims=True)
    turn[...] = turn[...].T
    head = table[32]
    row = lax.broadcasted_iota(jnp.int32, (SLICE, 128), 0)
    cols = jnp.where(row < table[33], turn[pl.ds(head, 1), :], turn[pl.ds(head + 1, 1), :])
    pulled = jnp.zeros((SLICE, STATE), F32)
    pulls = [None] * SEQ
    for k in range(SEQ - 1, -1, -1):
        pulls[k] = pulled
        pulled = cols[:, k : k + 1] * pulled + parts[k][0]
    state = jnp.zeros((SLICE, STATE), F32)
    for k in range(SEQ):
        out[k] = jnp.concatenate([pulls[k], state], axis=0).astype(BF16)
        state = cols[:, k : k + 1] * state + parts[k][1]


def chain(table, recv, tie):
    return pl.pallas_call(
        chain_kernel,
        grid=(1,),
        in_specs=[
            pl.BlockSpec(memory_space=pltpu.SMEM),
            whole(SEQ, MSG, STATE),
            pl.BlockSpec(memory_space=pl.ANY),
        ],
        out_specs=whole(SEQ, 2 * SLICE, STATE),
        out_shape=jax.ShapeDtypeStruct((SEQ, 2 * SLICE, STATE), BF16),
        scratch_shapes=[pltpu.VMEM((128, 128), F32)],
        compiler_params=params(),
        cost_estimate=cost(10**6, 3 * 2**20),
    )(table, recv, tie)


def early_kernel(
    code, before, normed, w_bc, step, grad_y, conv_w, w_x, *refs
):
    bmat, cmat, cum, logd, dyt_out, dywt_out, xgt_out, xlt_out, slope_out, xwt_out, msg = refs[:11]
    pulled, turn, ext, pre, own, held, sems = refs[11:18]
    dyt, dywt, xgt, xlt, slope, xwt, front_sems, out_sems = refs[18:]
    leaving = []
    copies = [
        pltpu.make_async_copy(w_x.at[:, pl.ds(BLK * i, BLK)], held.at[i], sems.at[i])
        for i in range(NBLK)
    ]
    for one in copies:
        one.start()
    ext[:16, :] = before[...]
    ext[16:, :] = normed[...]
    through = front_part(
        normed, w_bc, code, step, grad_y, bmat, cmat, cum, logd, dyt, dywt, pulled, turn
    )
    for at, (source, goal) in enumerate(((dyt, dyt_out), (dywt, dywt_out))):
        leaving.append(pltpu.make_async_copy(source, goal, front_sems.at[at]))
        leaving[-1].start()
    b_high, b_low = split(bmat[...])
    for i in range(NBLK + 1):
        if i < NBLK:
            copies[i].wait()
            pre[i % 2] = nn(ext[...], held[i]).astype(BF16).astype(F32)
        if i == 0:
            continue
        block = i - 1
        past = pre.at[block % 2]
        cols = slice(BLK * block, BLK * (block + 1))
        total = conv_w[0:1, cols] * past[16 : 16 + T, :]
        for tap in range(1, CONV):
            total = total + conv_w[tap : tap + 1, cols] * past[16 - tap : 16 - tap + T, :]
        sig = 0.5 * jnp.tanh(0.5 * total) + 0.5
        xt = (total * sig).T
        slope[:, cols] = sig * (1.0 + total * (1.0 - sig))
        parts = []
        for q in range(BLK // HEAD_DIM):
            h = block * (BLK // HEAD_DIM) + q
            rows = slice(64 * h, 64 * h + 64)
            gain = jnp.sqrt(-2.0 * logd[h : h + 1, :])
            cums = cum[h : h + 1, :]
            tail = jnp.exp(cums[:, T - 1 :] - cums)
            xg = xt[64 * q : 64 * q + 64] * gain
            xgt[rows, :], xlt[rows, :] = split(xg)
            parts.append(xg * tail)
        high, low = split(jnp.concatenate(parts, axis=0))
        xwt[cols, :] = high
        own[cols, :] = nn(high, b_high) + (nn(low, b_high) + nn(high, b_low))
        piece = pl.ds(BLK * block, BLK)
        pairs = [
            (one.at[piece, :], goal.at[piece, :])
            for one, goal in ((xgt, xgt_out), (xlt, xlt_out), (xwt, xwt_out))
        ]
        pairs.append((slope.at[:, piece], slope_out.at[:, piece]))
        for at, (source, goal) in enumerate(pairs):
            leaving.append(pltpu.make_async_copy(source, goal, out_sems.at[block, at]))
            leaving[-1].start()
    for k in range(SEQ):
        rows = slice(SLICE * k, SLICE * (k + 1))
        msg[k] = jnp.concatenate([pulled[rows, :], own[rows, :], through], axis=0).astype(BF16)
    for one in leaving:
        one.wait()


def early(code, before, normed, w_bc, step, grad_y, conv_w, w_x):
    vm = pl.BlockSpec(memory_space=pltpu.VMEM)
    away = pl.BlockSpec(memory_space=pl.ANY)
    return pl.pallas_call(
        early_kernel,
        in_specs=[vm] * 7 + [away],
        out_specs=(vm,) * 4 + (away,) * 6 + (vm,),
        out_shape=(
            jax.ShapeDtypeStruct((T, STATE), F32),
            jax.ShapeDtypeStruct((T, STATE), F32),
            jax.ShapeDtypeStruct((HEADS, T), F32),
            jax.ShapeDtypeStruct((HEADS, T), F32),
            jax.ShapeDtypeStruct((CH, T), BF16),
            jax.ShapeDtypeStruct((CH, T), BF16),
            jax.ShapeDtypeStruct((CH, T), BF16),
            jax.ShapeDtypeStruct((CH, T), BF16),
            jax.ShapeDtypeStruct((T, CH), F32),
            jax.ShapeDtypeStruct((CH, T), BF16),
            jax.ShapeDtypeStruct((SEQ, MSG, STATE), BF16),
        ),
        scratch_shapes=[
            pltpu.VMEM((CH, STATE), F32),
            pltpu.VMEM((128, 128), F32),
            pltpu.VMEM((T + 16, D), BF16),
            pltpu.VMEM((2, T + 16, BLK), F32),
            pltpu.VMEM((CH, STATE), F32),
            pltpu.VMEM((NBLK, D, BLK), BF16),
            pltpu.SemaphoreType.DMA((NBLK,)),
            pltpu.VMEM((CH, T), BF16),
            pltpu.VMEM((CH, T), BF16),
            pltpu.VMEM((CH, T), BF16),
            pltpu.VMEM((CH, T), BF16),
            pltpu.VMEM((T, CH), F32),
            pltpu.VMEM((CH, T), BF16),
            pltpu.SemaphoreType.DMA((2,)),
            pltpu.SemaphoreType.DMA((NBLK, 4)),
        ],
        compiler_params=params(56),
        cost_estimate=cost(2 * T * D * (CH + 256), 16 * 2**20, T * CH),
    )(code, before, normed, w_bc, step, grad_y, conv_w, w_x)


def intra_kernel(grad_y, dyt, xgt, cum, bmat, cmat, tie, dxg, rc, dbc, gram, dgram):
    del tie
    step = pl.program_id(0)

    @pl.when(step == 0)
    def _():
        gram[...] = wide(nt, cmat[...], bmat[...]) * SCALE
        dgram[...] = jnp.zeros((T, T), F32)

    half = T // 2
    row = lax.broadcasted_iota(jnp.int32, (half, half), 0)
    col = lax.broadcasted_iota(jnp.int32, (half, half), 1)
    keep = row >= col
    blank = jnp.zeros((HEAD_DIM, T), BF16)
    corner = jnp.zeros((half, half), BF16)
    for q in range(BLK // HEAD_DIM):
        head = pl.ds(step * (BLK // HEAD_DIM) + q, 1)
        rows = slice(64 * q, 64 * q + 64)
        cums = cum[head, :]
        column = jnp.broadcast_to(cums, (half, T)).T
        l00 = jnp.exp(jnp.where(keep, column[:half] - cums[:, :half], -1e30))
        l10 = jnp.exp(column[half:] - cums[:, :half])
        l11 = jnp.exp(jnp.where(keep, column[half:] - cums[:, half:], -1e30))
        m00 = (l00 * gram[:half, :half]).astype(BF16)
        m10 = (l10 * gram[half:, :half]).astype(BF16)
        m11 = (l11 * gram[half:, half:]).astype(BF16)
        mat = jnp.concatenate(
            [jnp.concatenate([m00, corner], axis=1), jnp.concatenate([m10, m11], axis=1)], axis=0
        )
        dy = dyt[rows, :]
        xg = xgt[rows, :]
        pair = slice(128 * (q // 2), 128 * (q // 2) + 128)
        right = jnp.concatenate([xg, blank] if q % 2 == 0 else [blank, xg], axis=0)
        dm0 = nn(grad_y[:, pair], right[:, :half])
        dm1 = nn(grad_y[half:, pair], right[:, half:])
        dgram[:half, :half] += l00 * dm0[:half]
        dgram[half:, :half] += l10 * dm0[half:]
        dgram[half:, half:] += l11 * dm1
        back = nn(dy, mat)
        yin = nt(xg, mat)
        dxg[rows, :] = back
        rc[head, :] = jnp.sum(dy.astype(F32) * yin - xg.astype(F32) * back, axis=0, keepdims=True)

    @pl.when(step == NBLK - 1)
    def _():
        dg = dgram[...] * SCALE
        dbc[:STATE, :] = wide(nn, cmat[...].T, dg)
        dbc[STATE:, :] = wide(nn, dg, bmat[...]).T


def intra(grad_y, dyt, xgt, cum, bmat, cmat, tie):
    rows = pl.BlockSpec((BLK, T), lambda i: (i, 0))
    return pl.pallas_call(
        intra_kernel,
        grid=(NBLK,),
        in_specs=[
            pl.BlockSpec((T, BLK), lambda i: (0, i)),
            rows,
            rows,
            whole(HEADS, T),
            whole(T, STATE),
            whole(T, STATE),
            pl.BlockSpec(memory_space=pl.ANY),
        ],
        out_specs=(rows, whole(HEADS, T), whole(2 * STATE, T)),
        out_shape=(
            jax.ShapeDtypeStruct((CH, T), F32),
            jax.ShapeDtypeStruct((HEADS, T), F32),
            jax.ShapeDtypeStruct((2 * STATE, T), F32),
        ),
        scratch_shapes=[pltpu.VMEM((T, T), F32), pltpu.VMEM((T, T), F32)],
        compiler_params=params(),
        cost_estimate=cost(HEADS * 2 * T * T * 64 * 8, 4 * 2**20, HEADS * T * T),
    )(grad_y, dyt, xgt, cum, bmat, cmat, tie)


def shared_kernel(back, xwt, dywt, dbc, ds, st, shared, ds_wide, st_wide):
    for k in range(SEQ):
        rows = slice(SLICE * k, SLICE * (k + 1))
        both = back[k].astype(F32)
        ds_wide[rows, :] = both[:SLICE]
        st_wide[rows, :] = both[SLICE:]
    ds[...] = ds_wide[...].astype(BF16)
    st[...] = st_wide[...].astype(BF16)
    for at, (state, tokens) in enumerate(((ds_wide, xwt), (st_wide, dywt))):
        turned = state[...].T.astype(BF16)
        part = nn(turned, tokens[...]) + dbc[STATE * at : STATE * (at + 1), :]
        shared[:, STATE * at : STATE * (at + 1)] = part.T.astype(BF16)


def shared_part(back, xwt, dywt, dbc):
    return pl.pallas_call(
        shared_kernel,
        out_shape=(
            jax.ShapeDtypeStruct((CH, STATE), BF16),
            jax.ShapeDtypeStruct((CH, STATE), BF16),
            jax.ShapeDtypeStruct((T, 2 * STATE), BF16),
        ),
        scratch_shapes=[pltpu.VMEM((CH, STATE), F32), pltpu.VMEM((CH, STATE), F32)],
        compiler_params=params(),
        cost_estimate=cost(4 * CH * T * 128, 4 * 2**20),
    )(back, xwt, dywt, dbc)


def grad_kernel(
    skip, bmat, taps, cum, logd, tie, back, dxg, dyt, xgt, xlt, slope, dpre, halo, halves, cross, *refs
):
    del tie
    ext, sems, *held = refs
    copies = []
    for i in range(NBLK):
        rows = pl.ds(BLK * i, BLK)
        parts = [one.at[rows, :] for one in (back, dxg, dyt, xgt, xlt)] + [slope.at[:, rows]]
        copies.append(
            [
                pltpu.make_async_copy(part, buffer.at[i], sems.at[i, at])
                for at, (part, buffer) in enumerate(zip(parts, held))
            ]
        )
        for one in copies[i]:
            one.start()
    b_high, b_low = split(bmat[...])
    for i in range(NBLK):
        for one in copies[i]:
            one.wait()
        back_i, dxg_i, dyt_i, xgt_i, xlt_i, slope_i = [buffer.at[i] for buffer in held]
        later = nt(back_i[...], b_high) + nt(back_i[...], b_low)
        parts = []
        for q in range(BLK // HEAD_DIM):
            index = i * (BLK // HEAD_DIM) + q
            head = slice(index, index + 1)
            rows = slice(64 * q, 64 * q + 64)
            gain = jnp.sqrt(-2.0 * logd[head, :])
            cums = cum[head, :]
            tail = jnp.exp(cums[:, T - 1 :] - cums)
            inter = later[rows] * tail
            whole_dxg = dxg_i[rows, :] + inter
            xg = xgt_i[rows, :].astype(F32) + xlt_i[rows, :].astype(F32)
            cross[head, :] = jnp.sum(xg * inter, axis=0, keepdims=True)
            halves[head, :] = 0.5 * jnp.sum(xg * whole_dxg, axis=0, keepdims=True)
            parts.append(gain * whole_dxg + skip[index] * dyt_i[rows, :].astype(F32))
        cols = slice(BLK * i, BLK * (i + 1))
        wide_i = ext.at[i % 2]
        wide_i[:8, :] = jnp.zeros((8, BLK), F32)
        wide_i[8 : T + 8, :] = jnp.concatenate(parts, axis=0).T * slope_i[...]
        wide_i[T + 8 :, :] = jnp.zeros((8, BLK), F32)
        total = taps[0:1, cols] * wide_i[8 : T + 8, :]
        edge = taps[0:1, cols] * wide_i[:8, :]
        for tap in range(1, CONV):
            weight = taps[tap : tap + 1, cols]
            total = total + weight * wide_i[8 + tap : T + 8 + tap, :]
            edge = edge + weight * wide_i[tap : 8 + tap, :]
        dpre[:, cols] = total.astype(BF16)
        halo[:, cols] = edge


def gradients(skip, back, bmat, dxg, dyt, xgt, xlt, slope, taps, cum, logd, tie):
    vm = pl.BlockSpec(memory_space=pltpu.VMEM)
    away = pl.BlockSpec(memory_space=pl.ANY)
    return pl.pallas_call(
        grad_kernel,
        in_specs=[pl.BlockSpec(memory_space=pltpu.SMEM)] + [vm] * 4 + [away] * 7,
        out_shape=(
            jax.ShapeDtypeStruct((T, CH), BF16),
            jax.ShapeDtypeStruct((8, CH), F32),
            jax.ShapeDtypeStruct((HEADS, T), F32),
            jax.ShapeDtypeStruct((HEADS, T), F32),
        ),
        scratch_shapes=[
            pltpu.VMEM((2, T + 16, BLK), F32),
            pltpu.SemaphoreType.DMA((NBLK, 6)),
            pltpu.VMEM((NBLK, BLK, STATE), BF16),
            pltpu.VMEM((NBLK, BLK, T), F32),
            pltpu.VMEM((NBLK, BLK, T), BF16),
            pltpu.VMEM((NBLK, BLK, T), BF16),
            pltpu.VMEM((NBLK, BLK, T), BF16),
            pltpu.VMEM((NBLK, T, BLK), F32),
        ],
        compiler_params=params(56),
        cost_estimate=cost(4 * CH * T * 128, 6 * 2**20, T * HEADS),
    )(skip, bmat, taps, cum, logd, tie, back, dxg, dyt, xgt, xlt, slope)


def step_kernel(fore, back, cmat, dyt, cum, logd, rc, halves, cross, tie, gls):
    del tie
    c_high, c_low = split(cmat[...])
    before = nt(fore[...], c_high) + nt(fore[...], c_low)
    cums = cum[...]
    inner = []
    through = []
    for h in range(HEADS):
        rows = slice(64 * h, 64 * h + 64)
        inner.append(jnp.sum(dyt[rows, :].astype(F32) * before[rows], axis=0, keepdims=True))
        both = fore[rows, :].astype(F32) * back[rows, :].astype(F32)
        both = jnp.sum(both, axis=0, keepdims=True)
        through.append(jnp.sum(both, axis=1, keepdims=True))
    arriving = rc[...] + jnp.exp(cums) * SCALE * jnp.concatenate(inner, axis=0)
    later = jnp.dot(arriving, triangle(False), precision=HIGH, preferred_element_type=F32)
    crossing = cross[...]
    earlier = (
        jnp.dot(crossing, triangle(True), precision=HIGH, preferred_element_type=F32) - crossing
    )
    kept = jnp.exp(cums[:, T - 1 :]) * jnp.concatenate(through, axis=0)
    gls[...] = logd[...] * (later + earlier + kept) + halves[...]


def step_part(fore, back, cmat, dyt, cum, logd, rc, halves, cross, tie):
    vm = pl.BlockSpec(memory_space=pltpu.VMEM)
    return pl.pallas_call(
        step_kernel,
        in_specs=[vm] * 9 + [pl.BlockSpec(memory_space=pl.ANY)],
        out_shape=jax.ShapeDtypeStruct((HEADS, T), F32),
        compiler_params=params(),
        cost_estimate=cost(4 * CH * T * 128, 4 * 2**20),
    )(fore, back, cmat, dyt, cum, logd, rc, halves, cross, tie)


def select_kernel(order, normed, tie, mine, other, flip):
    del tie
    for k in range(D // 128):
        cols = slice(128 * k, 128 * k + 128)
        flip[cols, :] = normed[:, cols].astype(F32).T.astype(BF16)
    for k in range(16):
        rows = slice(ROWS * k, ROWS * (k + 1))
        mine[rows, :] = flip[pl.ds(pl.multiple_of(order[k] * ROWS, 16), ROWS), :]
        other[rows, :] = flip[pl.ds(pl.multiple_of(order[16 + k] * ROWS, 16), ROWS), :]


def select(order, normed, tie):
    vm = pl.BlockSpec(memory_space=pltpu.VMEM)
    return pl.pallas_call(
        select_kernel,
        in_specs=[pl.BlockSpec(memory_space=pltpu.SMEM), vm, pl.BlockSpec(memory_space=pl.ANY)],
        out_shape=(jax.ShapeDtypeStruct((CH, T), BF16), jax.ShapeDtypeStruct((CH, T), BF16)),
        scratch_shapes=[pltpu.VMEM((D, T), BF16)],
        compiler_params=params(),
        cost_estimate=cost(10**6, 3 * 2**20),
    )(order, normed, tie)


PART = [slice(320 * r, 320 * (r + 1)) for r in range(4)]
WIDE = 640
FULL = WIDE + STATE
MAIN = [slice(0, WIDE), slice(WIDE, 2 * WIDE)]
EXTRA = [slice(0, STATE), slice(STATE, 2 * STATE)]


def mended(grad, halo, cols):
    edge = jnp.concatenate([jnp.zeros((8, WIDE), F32), halo[:, cols]], axis=0)
    return grad[: T - 16, cols], (grad[T - 16 :, cols].astype(F32) + edge).astype(BF16)


def product(refs, side):
    mine, other, grad, grad_other, halo, halo_other, shared, shared_other = refs
    cols = MAIN[side]
    right = jnp.concatenate(
        mended(grad, halo, cols) + mended(grad_other, halo_other, cols), axis=0
    )
    extra = jnp.concatenate([shared[:, EXTRA[side]], shared_other[:, EXTRA[side]]], axis=0)

    def rows(part):
        left = jnp.concatenate([mine[PART[part], :], other[PART[part], :]], axis=1)
        return nn(left, right), nn(left, extra)

    return rows


def far_kernel(*refs):
    for out, (part, side) in zip(refs[8:], ((2, 0), (2, 1))):
        main, extra = product(refs[:8], side)(part)
        out[:, :WIDE] = main.astype(BF16)
        out[:, WIDE:] = extra.astype(BF16)


def near_kernel(*refs):
    order = ((1, 0), (3, 1), (1, 1), (3, 0), (0, 0), (0, 1))
    for out, (part, side) in zip(refs[9:], order):
        main, extra = product(refs[:8], side)(part)
        out[:, :WIDE] = main.astype(out.dtype)
        out[:, WIDE:] = extra.astype(out.dtype)


def product_part(kernel, args, ties, types):
    vm = pl.BlockSpec(memory_space=pltpu.VMEM)
    return pl.pallas_call(
        kernel,
        in_specs=[vm] * 8 + [pl.BlockSpec(memory_space=pl.ANY)] * len(ties),
        out_shape=tuple(jax.ShapeDtypeStruct((320, FULL), one) for one in types),
        compiler_params=params(),
        cost_estimate=cost(2 * 512 * FULL * 320 * len(types), (3 + len(types)) * 2**20),
    )(*args, *ties)


def join_kernel(count, *refs):
    ins, outs = refs[: 3 * count], refs[3 * count :]
    for i, out in enumerate(outs):
        near, arrived, direct = ins[3 * i : 3 * i + 3]
        size = near.shape[0]
        out[:size, :] = (near[...] + arrived[...].astype(F32)).astype(BF16)
        out[size:, :] = direct[...]


def join(*triples):
    count = len(triples)
    return pl.pallas_call(
        functools.partial(join_kernel, count),
        out_shape=tuple(
            jax.ShapeDtypeStruct((2 * near.shape[0], near.shape[1]), BF16)
            for near, _, _ in triples
        ),
        compiler_params=params(),
        cost_estimate=cost(10**6, 4 * 2**20),
    )(*[one for triple in triples for one in triple])


def pass_kernel(near_up, up, near_down, down, out_up, out_down):
    size = near_up.shape[0]
    out_up[...] = (near_up[...] + up[:size, :].astype(F32)).astype(BF16)
    out_down[...] = (near_down[...] + down[:size, :].astype(F32)).astype(BF16)


def pass_on(near_up, up, near_down, down):
    one = jax.ShapeDtypeStruct(near_up.shape, BF16)
    return pl.pallas_call(
        pass_kernel,
        out_shape=(one, one),
        compiler_params=params(),
        cost_estimate=cost(10**6, 2 * 2**20),
    )(near_up, up, near_down, down)


def turn_kernel(here_a, here_b, up, down, far_up, far_down, near_up, near_down, dir_up, dir_down, a, b):
    size = 4 * ROWS

    def one(r, side):
        rows = slice(ROWS * r, ROWS * (r + 1))
        direct = slice(size + ROWS * r, size + ROWS * (r + 1))
        if side == 0:
            arrived = up[rows, :].astype(F32) + down[direct, :].astype(F32)
            return here_a[rows, :] + arrived
        arrived = down[rows, :].astype(F32) + up[direct, :].astype(F32)
        return here_b[rows, :] + arrived

    far_up[...] = one(2, 0).astype(BF16)
    far_down[...] = one(2, 1).astype(BF16)
    near_up[...] = one(1, 0)
    near_down[...] = one(3, 1)
    dir_up[...] = one(1, 1).astype(BF16)
    dir_down[...] = one(3, 0).astype(BF16)
    a[...] = one(0, 0)
    b[...] = one(0, 1)


def turn_part(here_a, here_b, up, down):
    return pl.pallas_call(
        turn_kernel,
        out_shape=tuple(
            jax.ShapeDtypeStruct((ROWS, FULL), one)
            for one in (BF16, BF16, F32, F32, BF16, BF16, F32, F32)
        ),
        compiler_params=params(),
        cost_estimate=cost(10**6, 4 * 2**20),
    )(here_a, here_b, up, down)


def last_kernel(
    a, b, up, down, here_u, up_u, down_u, near_up, near_down, grad_wx, grad_wbc, grad_u
):
    norm = (T * SEQ) ** (-0.5)
    first = a[...] + (up[:ROWS, :].astype(F32) + down[ROWS:, :].astype(F32))
    second = b[...] + (down[:ROWS, :].astype(F32) + up[ROWS:, :].astype(F32))
    grad_wx[:, :WIDE] = first[:, :WIDE] * norm
    grad_wx[:, WIDE:] = second[:, :WIDE] * norm
    grad_wbc[:, :STATE] = first[:, WIDE:] * norm
    grad_wbc[:, STATE:] = second[:, WIDE:] * norm
    size = here_u.shape[0] // 2
    low = here_u[:size, :] + (near_up[...].astype(F32) + down_u[size:, :].astype(F32))
    high = here_u[size:, :] + (near_down[...].astype(F32) + up_u[size:, :].astype(F32))
    grad_u[:size, :] = low.astype(BF16)
    grad_u[size:, :] = high.astype(BF16)


def last_part(*args):
    return pl.pallas_call(
        last_kernel,
        out_shape=(
            jax.ShapeDtypeStruct((ROWS, CH), F32),
            jax.ShapeDtypeStruct((ROWS, 2 * STATE), F32),
            jax.ShapeDtypeStruct((D // ZS, T), BF16),
        ),
        compiler_params=params(),
        cost_estimate=cost(10**6, 3 * 2**20),
    )(*args)


def input_kernel(order, w_x, w_bc, grad, halo, shared, tie, *refs):
    del tie
    far_up, far_down, near_up, near_down, here, held, small, sems = refs
    size = D // ZS
    half = size // 2
    copies = []
    turn = (2, 1, 3, 0)
    for at, r in enumerate(turn):
        rows = pl.ds(pl.multiple_of(order[r] * size, size), size)
        copies.append(pltpu.make_async_copy(w_x.at[rows, :], held.at[at], sems.at[at]))
        copies[at].start()
    rows = pl.ds(pl.multiple_of(order[0] * size, size), size)
    last_copy = pltpu.make_async_copy(w_bc.at[rows, :], small, sems.at[ZS])
    last_copy.start()
    edge = jnp.concatenate([jnp.zeros((8, CH), F32), halo[...]], axis=0)
    last = (grad[T - 16 :, :].astype(F32) + edge).astype(BF16)
    right = jnp.concatenate([grad[: T - 16, :], last], axis=0)
    for at, r in enumerate(turn):
        copies[at].wait()
        part = nt(held[at], right)
        if r == 2:
            far_up[:half, :] = part[:half].astype(BF16)
            far_down[:half, :] = part[half:].astype(BF16)
        elif r == 0:
            last_copy.wait()
            here[...] = part + nt(small[...], shared[...])
        elif r == 1:
            near_up[...] = part[:half]
            far_up[half:, :] = part[half:].astype(BF16)
        else:
            far_down[half:, :] = part[:half].astype(BF16)
            near_down[...] = part[half:]


def input_part(order, w_x, w_bc, grad, halo, shared, tie):
    rows = D // ZS
    vm = pl.BlockSpec(memory_space=pltpu.VMEM)
    away = pl.BlockSpec(memory_space=pl.ANY)
    sizes = (rows, rows, rows // 2, rows // 2, rows)
    types = (BF16, BF16, F32, F32, F32)
    return pl.pallas_call(
        input_kernel,
        in_specs=[pl.BlockSpec(memory_space=pltpu.SMEM), away, away, vm, vm, vm, away],
        out_shape=tuple(jax.ShapeDtypeStruct((size, T), one) for size, one in zip(sizes, types)),
        scratch_shapes=[
            pltpu.VMEM((ZS, rows, CH), BF16),
            pltpu.VMEM((rows, 2 * STATE), BF16),
            pltpu.SemaphoreType.DMA((ZS + 1,)),
        ],
        compiler_params=params(48),
        cost_estimate=cost(2 * D * (CH + 64) * T, 10 * 2**20),
    )(order, w_x, w_bc, grad, halo, shared, tie)


def device(x, y, core):
    return ((x % 4) * 4 + y % 4) * 2 + core


def ring(first, by):
    pairs = []
    for x in range(4):
        for y in range(4):
            for core in range(2):
                along_x = (core == 0) == first
                goal = device(x + by, y, core) if along_x else device(x, y + by, core)
                pairs.append((device(x, y, core), goal))
    return pairs


def along(first, by):
    return lambda value: lax.ppermute(value, "seq", ring(first, by))


def along_head(by):
    return lambda value: lax.ppermute(value, "head", [(i, (i + by) % ZS) for i in range(ZS)])


def place_table():
    rows = []
    for place in range(SEQ):
        core, y, x = place % 2, place // 2 % 4, place // 8
        blocks = [
            [device(x + a, y + b, 0) for a in range(4) for b in range(4)],
            [device(x + b, y + a, 1) for a in range(4) for b in range(4)],
        ]
        head = SLICE * place // HEAD_DIM
        bound = HEAD_DIM * (head + 1) - SLICE * place
        rows.append(blocks[core] + blocks[1 - core] + [head, bound])
    return np.array(rows, np.int32)


def full_table():
    order = [[(z + r) % ZS for r in range(ZS)] for z in range(ZS)]
    return np.array([[list(one) + o for o in order] for one in place_table()], np.int32)


def body(normed, w_x, w_bc, conv_w, decay_code, step, d_skip, grad_y):
    place = lax.axis_index("seq")
    core = place % 2
    z = lax.axis_index("head")
    table = jnp.asarray(full_table())[place, z]
    order_z = table[34:]
    swap = [(i, i ^ 1) for i in range(SEQ)]

    before = lax.ppermute(normed[T - 16 :], "seq", [(i, i + 1) for i in range(SEQ - 1)])

    bmat, cmat, cum, logd, dyt, dywt, xgt, xlt, slope, xwt, msg = early(
        decay_code[None, :], before, normed, w_bc, step, grad_y, conv_w, w_x
    )
    recv = lax.all_to_all(msg, "seq", 0, 0)
    mine, other = select(table, normed, msg)
    other = lax.ppermute(other, "seq", swap)
    dxg, rc, dbc = intra(grad_y, dyt, xgt, cum, bmat, cmat, mine)
    back = lax.all_to_all(chain(table, recv, rc), "seq", 0, 0)

    ds, st, shared = shared_part(back, xwt, dywt, dbc)
    others = [along_head(by)(shared) for by in (1, 2, 3)]
    dpre, halo, halves, cross = gradients(
        d_skip, ds, bmat, dxg, dyt, xgt, xlt, slope, conv_w, cum, logd, st
    )
    dpre_other = lax.ppermute(dpre, "seq", swap)
    halo_mine = lax.ppermute(halo, "seq", [(i, i - 1) for i in range(1, SEQ)])
    halo_pair = lax.ppermute(halo, "seq", [(i, i - 2) for i in range(2, SEQ, 2)])
    halo_other = jnp.where(core == 0, halo_pair, halo)
    one, two, three, _ = lax.optimization_barrier((*others, halo))
    near_pair = shared.astype(F32) + two.astype(F32)
    far_pair = one.astype(F32) + three.astype(F32)
    shared = (near_pair + far_pair).astype(BF16)
    shared_other = lax.ppermute(shared, "seq", swap)

    args = (mine, other, dpre, dpre_other, halo_mine, halo_other, shared, shared_other)
    move = {by: along(True, by) for by in (1, -1)}
    turn = {by: along(False, by) for by in (1, -1)}
    head = {by: along_head(by) for by in (1, -1)}
    far_up, far_down = product_part(far_kernel, args, (), (BF16, BF16))
    ru, rd = move[1](far_up), move[-1](far_down)
    near_up, near_down, dir_up, dir_down, here_a, here_b = product_part(
        near_kernel, args, (far_up,), (F32, F32, BF16, BF16, F32, F32)
    )
    up, down = join((near_up, ru, dir_up), (near_down, rd, dir_down))
    ru, rd = move[1](up), move[-1](down)
    z_far_up, z_far_down, z_up, z_down, z_here = input_part(
        order_z, w_x, w_bc, dpre, halo_mine, shared, up
    )
    gls = step_part(st, ds, cmat, dyt, cum, logd, rc, halves, cross, z_here)
    far_up, far_down, near_up, near_down, dir_up, dir_down, here_a, here_b = turn_part(
        here_a, here_b, ru, rd
    )
    ru, rd = turn[1](far_up), turn[-1](far_down)
    zu, zd = head[1](z_far_up), head[-1](z_far_down)
    z_up, z_down = pass_on(z_up, zu, z_down, zd)
    z_near_up, z_near_down = head[1](z_up), head[-1](z_down)
    up, down = join((near_up, ru, dir_up), (near_down, rd, dir_down))
    ru, rd = turn[1](up), turn[-1](down)
    grad_wx, grad_wbc, grad_u = last_part(
        here_a, here_b, ru, rd, z_here, zu, zd, z_near_up, z_near_down
    )
    return (grad_u, grad_wx, grad_wbc, gls)


def solution(mesh):
    return jax.shard_map(
        body,
        mesh=mesh,
        in_specs=(
            P("seq", None),
            P(None, "head"),
            P(),
            P(None, "head"),
            P("head"),
            P("head", "seq"),
            P("head"),
            P("seq", "head"),
        ),
        out_specs=(P("head", "seq"), P("seq", "head"), P("seq", None), P("head", "seq")),
        check_vma=False,
    )
```

```python
import functools
import math

import jax
import jax.numpy as jnp
import numpy as np
from jax import lax
from jax.experimental import pallas as pl
from jax.experimental.pallas import tpu as pltpu
from jax.sharding import PartitionSpec as P

D = 2560
HEAD_DIM = 64
STATE = 128
CONV = 4
LEVELS = 256
T = 256
CH = 1280
HEADS = 20
SEQ = 32
ZS = 4
ROWS = 80
SLICE = 40
MSG = 96
BLK = 256
NBLK = CH // BLK
SCALE = STATE ** (-0.5)
F32 = jnp.float32
BF16 = jnp.bfloat16
HIGH = lax.Precision.HIGHEST
NT = (((1,), (1,)), ((), ()))


def nt(a, b):
    return lax.dot_general(a, b, NT, preferred_element_type=F32)


def nn(a, b):
    return jnp.dot(a, b, preferred_element_type=F32)


def split(value):
    high = value.astype(BF16)
    return high, (value - high.astype(F32)).astype(BF16)


def wide(dot, a, b):
    a_high, a_low = split(a)
    b_high, b_low = split(b)
    return dot(a_high, b_high) + (dot(a_low, b_high) + dot(a_high, b_low))


def params(mib=20):
    return pltpu.CompilerParams(vmem_limit_bytes=mib * 2**20)


def cost(flops, nbytes, trans=0):
    return pl.CostEstimate(flops=flops, bytes_accessed=nbytes, transcendentals=trans)


def whole(*shape):
    return pl.BlockSpec(shape, lambda i: (0,) * len(shape))


def triangle(upper):
    row = lax.broadcasted_iota(jnp.int32, (T, T), 0)
    col = lax.broadcasted_iota(jnp.int32, (T, T), 1)
    return jnp.where(row <= col if upper else row >= col, 1.0, 0.0).astype(F32)


def front_part(normed, w_bc, code, step, grad_y, bmat, cmat, cum, logd, dyt, dywt, pulled, turn):
    shared = nn(normed[...], w_bc[...])
    bmat[...] = shared[:, :STATE]
    cmat[...] = shared[:, STATE:]
    c_high, c_low = split(shared[:, STATE:])
    low = math.log(0.995)
    high = math.log(0.9999)
    turn[...] = jnp.zeros((128, 128), F32)
    turn[0:1, :HEADS] = code[...].astype(F32)
    codes = turn[...].T[:HEADS, 0:1]
    logs = (low + codes / (LEVELS - 1) * (high - low)) * step[...]
    logd[...] = logs
    cums = jnp.dot(logs, triangle(True), precision=HIGH, preferred_element_type=F32)
    cum[...] = cums
    grown = jnp.exp(cums)
    weight = grown * SCALE
    for pair in range(HEADS // 2):
        rows = slice(128 * pair, 128 * pair + 128)
        tile = grad_y[:, rows].astype(F32).T
        dyt[rows, :] = tile.astype(BF16)
        tile = jnp.concatenate(
            [
                tile[:64] * weight[2 * pair : 2 * pair + 1],
                tile[64:] * weight[2 * pair + 1 : 2 * pair + 2],
            ],
            axis=0,
        )
        high, low = split(tile)
        dywt[rows, :] = high
        pulled[rows, :] = nn(high, c_high) + (nn(low, c_high) + nn(high, c_low))
    turn[...] = jnp.zeros((128, 128), F32)
    turn[:HEADS, :] = grown[:, 128:]
    through = turn[...].T[127:, :]
    high = through.astype(BF16).astype(F32)
    middle = (through - high).astype(BF16).astype(F32)
    row = lax.broadcasted_iota(jnp.int32, (MSG - 2 * SLICE, STATE), 0)
    rest = jnp.where(row == 2, through - high - middle, 0.0)
    return jnp.where(row == 0, high, jnp.where(row == 1, middle, rest))


def chain_kernel(table, recv, tie, out, turn):
    del tie
    turn[...] = jnp.zeros((128, 128), F32)
    parts = []
    for k in range(SEQ):
        one = recv[k].astype(F32)
        parts.append((one[:SLICE], one[SLICE : 2 * SLICE]))
        turn[k : k + 1, :] = jnp.sum(one[2 * SLICE :], axis=0, keepdims=True)
    turn[...] = turn[...].T
    head = table[32]
    row = lax.broadcasted_iota(jnp.int32, (SLICE, 128), 0)
    cols = jnp.where(row < table[33], turn[pl.ds(head, 1), :], turn[pl.ds(head + 1, 1), :])
    pulled = jnp.zeros((SLICE, STATE), F32)
    pulls = [None] * SEQ
    for k in range(SEQ - 1, -1, -1):
        pulls[k] = pulled
        pulled = cols[:, k : k + 1] * pulled + parts[k][0]
    state = jnp.zeros((SLICE, STATE), F32)
    for k in range(SEQ):
        out[k] = jnp.concatenate([pulls[k], state], axis=0).astype(BF16)
        state = cols[:, k : k + 1] * state + parts[k][1]


def chain(table, recv, tie):
    return pl.pallas_call(
        chain_kernel,
        grid=(1,),
        in_specs=[
            pl.BlockSpec(memory_space=pltpu.SMEM),
            whole(SEQ, MSG, STATE),
            pl.BlockSpec(memory_space=pl.ANY),
        ],
        out_specs=whole(SEQ, 2 * SLICE, STATE),
        out_shape=jax.ShapeDtypeStruct((SEQ, 2 * SLICE, STATE), BF16),
        scratch_shapes=[pltpu.VMEM((128, 128), F32)],
        compiler_params=params(),
        cost_estimate=cost(10**6, 3 * 2**20),
    )(table, recv, tie)


def early_kernel(
    code, before, normed, w_bc, step, grad_y, conv_w, w_x, *refs
):
    bmat, cmat, cum, logd, dyt, dywt, xgt, xlt, slope, xwt, msg = refs[:11]
    pulled, turn, ext, pre, own, held, sems = refs[11:]
    copies = [
        pltpu.make_async_copy(w_x.at[:, pl.ds(BLK * i, BLK)], held.at[i], sems.at[i])
        for i in range(NBLK)
    ]
    for one in copies:
        one.start()
    ext[:16, :] = before[...]
    ext[16:, :] = normed[...]
    through = front_part(
        normed, w_bc, code, step, grad_y, bmat, cmat, cum, logd, dyt, dywt, pulled, turn
    )
    b_high, b_low = split(bmat[...])
    for i in range(NBLK + 1):
        if i < NBLK:
            copies[i].wait()
            pre[i % 2] = nn(ext[...], held[i]).astype(BF16).astype(F32)
        if i == 0:
            continue
        block = i - 1
        past = pre.at[block % 2]
        cols = slice(BLK * block, BLK * (block + 1))
        total = conv_w[0:1, cols] * past[16 : 16 + T, :]
        for tap in range(1, CONV):
            total = total + conv_w[tap : tap + 1, cols] * past[16 - tap : 16 - tap + T, :]
        sig = 0.5 * jnp.tanh(0.5 * total) + 0.5
        xt = (total * sig).T
        slope[:, cols] = sig * (1.0 + total * (1.0 - sig))
        parts = []
        for q in range(BLK // HEAD_DIM):
            h = block * (BLK // HEAD_DIM) + q
            rows = slice(64 * h, 64 * h + 64)
            gain = jnp.sqrt(-2.0 * logd[h : h + 1, :])
            cums = cum[h : h + 1, :]
            tail = jnp.exp(cums[:, T - 1 :] - cums)
            xg = xt[64 * q : 64 * q + 64] * gain
            xgt[rows, :], xlt[rows, :] = split(xg)
            parts.append(xg * tail)
        high, low = split(jnp.concatenate(parts, axis=0))
        xwt[cols, :] = high
        own[cols, :] = nn(high, b_high) + (nn(low, b_high) + nn(high, b_low))
    for k in range(SEQ):
        rows = slice(SLICE * k, SLICE * (k + 1))
        msg[k] = jnp.concatenate([pulled[rows, :], own[rows, :], through], axis=0).astype(BF16)


def early(code, before, normed, w_bc, step, grad_y, conv_w, w_x):
    vm = pl.BlockSpec(memory_space=pltpu.VMEM)
    return pl.pallas_call(
        early_kernel,
        in_specs=[vm] * 7 + [pl.BlockSpec(memory_space=pl.ANY)],
        out_shape=(
            jax.ShapeDtypeStruct((T, STATE), F32),
            jax.ShapeDtypeStruct((T, STATE), F32),
            jax.ShapeDtypeStruct((HEADS, T), F32),
            jax.ShapeDtypeStruct((HEADS, T), F32),
            jax.ShapeDtypeStruct((CH, T), BF16),
            jax.ShapeDtypeStruct((CH, T), BF16),
            jax.ShapeDtypeStruct((CH, T), BF16),
            jax.ShapeDtypeStruct((CH, T), BF16),
            jax.ShapeDtypeStruct((T, CH), F32),
            jax.ShapeDtypeStruct((CH, T), BF16),
            jax.ShapeDtypeStruct((SEQ, MSG, STATE), BF16),
        ),
        scratch_shapes=[
            pltpu.VMEM((CH, STATE), F32),
            pltpu.VMEM((128, 128), F32),
            pltpu.VMEM((T + 16, D), BF16),
            pltpu.VMEM((2, T + 16, BLK), F32),
            pltpu.VMEM((CH, STATE), F32),
            pltpu.VMEM((NBLK, D, BLK), BF16),
            pltpu.SemaphoreType.DMA((NBLK,)),
        ],
        compiler_params=params(56),
        cost_estimate=cost(2 * T * D * (CH + 256), 16 * 2**20, T * CH),
    )(code, before, normed, w_bc, step, grad_y, conv_w, w_x)


def intra_kernel(grad_y, dyt, xgt, cum, bmat, cmat, tie, dxg, rc, dbc, gram, dgram):
    del tie
    step = pl.program_id(0)

    @pl.when(step == 0)
    def _():
        gram[...] = wide(nt, cmat[...], bmat[...]) * SCALE
        dgram[...] = jnp.zeros((T, T), F32)

    half = T // 2
    row = lax.broadcasted_iota(jnp.int32, (half, half), 0)
    col = lax.broadcasted_iota(jnp.int32, (half, half), 1)
    keep = row >= col
    blank = jnp.zeros((HEAD_DIM, T), BF16)
    corner = jnp.zeros((half, half), BF16)
    for q in range(BLK // HEAD_DIM):
        head = pl.ds(step * (BLK // HEAD_DIM) + q, 1)
        rows = slice(64 * q, 64 * q + 64)
        cums = cum[head, :]
        column = jnp.broadcast_to(cums, (half, T)).T
        l00 = jnp.exp(jnp.where(keep, column[:half] - cums[:, :half], -1e30))
        l10 = jnp.exp(column[half:] - cums[:, :half])
        l11 = jnp.exp(jnp.where(keep, column[half:] - cums[:, half:], -1e30))
        m00 = (l00 * gram[:half, :half]).astype(BF16)
        m10 = (l10 * gram[half:, :half]).astype(BF16)
        m11 = (l11 * gram[half:, half:]).astype(BF16)
        mat = jnp.concatenate(
            [jnp.concatenate([m00, corner], axis=1), jnp.concatenate([m10, m11], axis=1)], axis=0
        )
        dy = dyt[rows, :]
        xg = xgt[rows, :]
        pair = slice(128 * (q // 2), 128 * (q // 2) + 128)
        right = jnp.concatenate([xg, blank] if q % 2 == 0 else [blank, xg], axis=0)
        dm0 = nn(grad_y[:, pair], right[:, :half])
        dm1 = nn(grad_y[half:, pair], right[:, half:])
        dgram[:half, :half] += l00 * dm0[:half]
        dgram[half:, :half] += l10 * dm0[half:]
        dgram[half:, half:] += l11 * dm1
        back = nn(dy, mat)
        yin = nt(xg, mat)
        dxg[rows, :] = back
        rc[head, :] = jnp.sum(dy.astype(F32) * yin - xg.astype(F32) * back, axis=0, keepdims=True)

    @pl.when(step == NBLK - 1)
    def _():
        dg = dgram[...] * SCALE
        dbc[:STATE, :] = wide(nn, cmat[...].T, dg)
        dbc[STATE:, :] = wide(nn, dg, bmat[...]).T


def intra(grad_y, dyt, xgt, cum, bmat, cmat, tie):
    rows = pl.BlockSpec((BLK, T), lambda i: (i, 0))
    return pl.pallas_call(
        intra_kernel,
        grid=(NBLK,),
        in_specs=[
            pl.BlockSpec((T, BLK), lambda i: (0, i)),
            rows,
            rows,
            whole(HEADS, T),
            whole(T, STATE),
            whole(T, STATE),
            pl.BlockSpec(memory_space=pl.ANY),
        ],
        out_specs=(rows, whole(HEADS, T), whole(2 * STATE, T)),
        out_shape=(
            jax.ShapeDtypeStruct((CH, T), F32),
            jax.ShapeDtypeStruct((HEADS, T), F32),
            jax.ShapeDtypeStruct((2 * STATE, T), F32),
        ),
        scratch_shapes=[pltpu.VMEM((T, T), F32), pltpu.VMEM((T, T), F32)],
        compiler_params=params(),
        cost_estimate=cost(HEADS * 2 * T * T * 64 * 8, 4 * 2**20, HEADS * T * T),
    )(grad_y, dyt, xgt, cum, bmat, cmat, tie)


def shared_kernel(back, xwt, dywt, dbc, ds, st, shared, ds_wide, st_wide):
    for k in range(SEQ):
        rows = slice(SLICE * k, SLICE * (k + 1))
        both = back[k].astype(F32)
        ds_wide[rows, :] = both[:SLICE]
        st_wide[rows, :] = both[SLICE:]
    ds[...] = ds_wide[...].astype(BF16)
    st[...] = st_wide[...].astype(BF16)
    for at, (state, tokens) in enumerate(((ds_wide, xwt), (st_wide, dywt))):
        turned = state[...].T.astype(BF16)
        part = nn(turned, tokens[...]) + dbc[STATE * at : STATE * (at + 1), :]
        shared[:, STATE * at : STATE * (at + 1)] = part.T.astype(BF16)


def shared_part(back, xwt, dywt, dbc):
    return pl.pallas_call(
        shared_kernel,
        out_shape=(
            jax.ShapeDtypeStruct((CH, STATE), BF16),
            jax.ShapeDtypeStruct((CH, STATE), BF16),
            jax.ShapeDtypeStruct((T, 2 * STATE), BF16),
        ),
        scratch_shapes=[pltpu.VMEM((CH, STATE), F32), pltpu.VMEM((CH, STATE), F32)],
        compiler_params=params(),
        cost_estimate=cost(4 * CH * T * 128, 4 * 2**20),
    )(back, xwt, dywt, dbc)


def grad_kernel(
    skip, bmat, taps, cum, logd, tie, back, dxg, dyt, xgt, xlt, slope, dpre, halo, halves, cross, *refs
):
    del tie
    ext, sems, *held = refs
    copies = []
    for i in range(NBLK):
        rows = pl.ds(BLK * i, BLK)
        parts = [one.at[rows, :] for one in (back, dxg, dyt, xgt, xlt)] + [slope.at[:, rows]]
        copies.append(
            [
                pltpu.make_async_copy(part, buffer.at[i], sems.at[i, at])
                for at, (part, buffer) in enumerate(zip(parts, held))
            ]
        )
        for one in copies[i]:
            one.start()
    b_high, b_low = split(bmat[...])
    for i in range(NBLK):
        for one in copies[i]:
            one.wait()
        back_i, dxg_i, dyt_i, xgt_i, xlt_i, slope_i = [buffer.at[i] for buffer in held]
        later = nt(back_i[...], b_high) + nt(back_i[...], b_low)
        parts = []
        for q in range(BLK // HEAD_DIM):
            index = i * (BLK // HEAD_DIM) + q
            head = slice(index, index + 1)
            rows = slice(64 * q, 64 * q + 64)
            gain = jnp.sqrt(-2.0 * logd[head, :])
            cums = cum[head, :]
            tail = jnp.exp(cums[:, T - 1 :] - cums)
            inter = later[rows] * tail
            whole_dxg = dxg_i[rows, :] + inter
            xg = xgt_i[rows, :].astype(F32) + xlt_i[rows, :].astype(F32)
            cross[head, :] = jnp.sum(xg * inter, axis=0, keepdims=True)
            halves[head, :] = 0.5 * jnp.sum(xg * whole_dxg, axis=0, keepdims=True)
            parts.append(gain * whole_dxg + skip[index] * dyt_i[rows, :].astype(F32))
        cols = slice(BLK * i, BLK * (i + 1))
        wide_i = ext.at[i % 2]
        wide_i[:8, :] = jnp.zeros((8, BLK), F32)
        wide_i[8 : T + 8, :] = jnp.concatenate(parts, axis=0).T * slope_i[...]
        wide_i[T + 8 :, :] = jnp.zeros((8, BLK), F32)
        total = taps[0:1, cols] * wide_i[8 : T + 8, :]
        edge = taps[0:1, cols] * wide_i[:8, :]
        for tap in range(1, CONV):
            weight = taps[tap : tap + 1, cols]
            total = total + weight * wide_i[8 + tap : T + 8 + tap, :]
            edge = edge + weight * wide_i[tap : 8 + tap, :]
        dpre[:, cols] = total.astype(BF16)
        halo[:, cols] = edge


def gradients(skip, back, bmat, dxg, dyt, xgt, xlt, slope, taps, cum, logd, tie):
    vm = pl.BlockSpec(memory_space=pltpu.VMEM)
    away = pl.BlockSpec(memory_space=pl.ANY)
    return pl.pallas_call(
        grad_kernel,
        in_specs=[pl.BlockSpec(memory_space=pltpu.SMEM)] + [vm] * 4 + [away] * 7,
        out_shape=(
            jax.ShapeDtypeStruct((T, CH), BF16),
            jax.ShapeDtypeStruct((8, CH), F32),
            jax.ShapeDtypeStruct((HEADS, T), F32),
            jax.ShapeDtypeStruct((HEADS, T), F32),
        ),
        scratch_shapes=[
            pltpu.VMEM((2, T + 16, BLK), F32),
            pltpu.SemaphoreType.DMA((NBLK, 6)),
            pltpu.VMEM((NBLK, BLK, STATE), BF16),
            pltpu.VMEM((NBLK, BLK, T), F32),
            pltpu.VMEM((NBLK, BLK, T), BF16),
            pltpu.VMEM((NBLK, BLK, T), BF16),
            pltpu.VMEM((NBLK, BLK, T), BF16),
            pltpu.VMEM((NBLK, T, BLK), F32),
        ],
        compiler_params=params(56),
        cost_estimate=cost(4 * CH * T * 128, 6 * 2**20, T * HEADS),
    )(skip, bmat, taps, cum, logd, tie, back, dxg, dyt, xgt, xlt, slope)


def step_kernel(fore, back, cmat, dyt, cum, logd, rc, halves, cross, tie, gls):
    del tie
    c_high, c_low = split(cmat[...])
    before = nt(fore[...], c_high) + nt(fore[...], c_low)
    cums = cum[...]
    inner = []
    through = []
    for h in range(HEADS):
        rows = slice(64 * h, 64 * h + 64)
        inner.append(jnp.sum(dyt[rows, :].astype(F32) * before[rows], axis=0, keepdims=True))
        both = fore[rows, :].astype(F32) * back[rows, :].astype(F32)
        both = jnp.sum(both, axis=0, keepdims=True)
        through.append(jnp.sum(both, axis=1, keepdims=True))
    arriving = rc[...] + jnp.exp(cums) * SCALE * jnp.concatenate(inner, axis=0)
    later = jnp.dot(arriving, triangle(False), precision=HIGH, preferred_element_type=F32)
    crossing = cross[...]
    earlier = (
        jnp.dot(crossing, triangle(True), precision=HIGH, preferred_element_type=F32) - crossing
    )
    kept = jnp.exp(cums[:, T - 1 :]) * jnp.concatenate(through, axis=0)
    gls[...] = logd[...] * (later + earlier + kept) + halves[...]


def step_part(fore, back, cmat, dyt, cum, logd, rc, halves, cross, tie):
    vm = pl.BlockSpec(memory_space=pltpu.VMEM)
    return pl.pallas_call(
        step_kernel,
        in_specs=[vm] * 9 + [pl.BlockSpec(memory_space=pl.ANY)],
        out_shape=jax.ShapeDtypeStruct((HEADS, T), F32),
        compiler_params=params(),
        cost_estimate=cost(4 * CH * T * 128, 4 * 2**20),
    )(fore, back, cmat, dyt, cum, logd, rc, halves, cross, tie)


def select_kernel(order, normed, tie, mine, other, flip):
    del tie
    for k in range(D // 128):
        cols = slice(128 * k, 128 * k + 128)
        flip[cols, :] = normed[:, cols].astype(F32).T.astype(BF16)
    for k in range(16):
        rows = slice(ROWS * k, ROWS * (k + 1))
        mine[rows, :] = flip[pl.ds(pl.multiple_of(order[k] * ROWS, 16), ROWS), :]
        other[rows, :] = flip[pl.ds(pl.multiple_of(order[16 + k] * ROWS, 16), ROWS), :]


def select(order, normed, tie):
    vm = pl.BlockSpec(memory_space=pltpu.VMEM)
    return pl.pallas_call(
        select_kernel,
        in_specs=[pl.BlockSpec(memory_space=pltpu.SMEM), vm, pl.BlockSpec(memory_space=pl.ANY)],
        out_shape=(jax.ShapeDtypeStruct((CH, T), BF16), jax.ShapeDtypeStruct((CH, T), BF16)),
        scratch_shapes=[pltpu.VMEM((D, T), BF16)],
        compiler_params=params(),
        cost_estimate=cost(10**6, 3 * 2**20),
    )(order, normed, tie)


PART = [slice(320 * r, 320 * (r + 1)) for r in range(4)]
WIDE = 640
FULL = WIDE + STATE
MAIN = [slice(0, WIDE), slice(WIDE, 2 * WIDE)]
EXTRA = [slice(0, STATE), slice(STATE, 2 * STATE)]


def mended(grad, halo, cols):
    edge = jnp.concatenate([jnp.zeros((8, WIDE), F32), halo[:, cols]], axis=0)
    return grad[: T - 16, cols], (grad[T - 16 :, cols].astype(F32) + edge).astype(BF16)


def product(refs, side):
    mine, other, grad, grad_other, halo, halo_other, shared, shared_other = refs
    cols = MAIN[side]
    right = jnp.concatenate(
        mended(grad, halo, cols) + mended(grad_other, halo_other, cols), axis=0
    )
    extra = jnp.concatenate([shared[:, EXTRA[side]], shared_other[:, EXTRA[side]]], axis=0)

    def rows(part):
        left = jnp.concatenate([mine[PART[part], :], other[PART[part], :]], axis=1)
        return nn(left, right), nn(left, extra)

    return rows


def far_kernel(*refs):
    for out, (part, side) in zip(refs[8:], ((2, 0), (2, 1))):
        main, extra = product(refs[:8], side)(part)
        out[:, :WIDE] = main.astype(BF16)
        out[:, WIDE:] = extra.astype(BF16)


def near_kernel(*refs):
    order = ((1, 0), (3, 1), (1, 1), (3, 0), (0, 0), (0, 1))
    for out, (part, side) in zip(refs[9:], order):
        main, extra = product(refs[:8], side)(part)
        out[:, :WIDE] = main.astype(out.dtype)
        out[:, WIDE:] = extra.astype(out.dtype)


def product_part(kernel, args, ties, types):
    vm = pl.BlockSpec(memory_space=pltpu.VMEM)
    return pl.pallas_call(
        kernel,
        in_specs=[vm] * 8 + [pl.BlockSpec(memory_space=pl.ANY)] * len(ties),
        out_shape=tuple(jax.ShapeDtypeStruct((320, FULL), one) for one in types),
        compiler_params=params(),
        cost_estimate=cost(2 * 512 * FULL * 320 * len(types), (3 + len(types)) * 2**20),
    )(*args, *ties)


def join_kernel(count, *refs):
    ins, outs = refs[: 3 * count], refs[3 * count :]
    for i, out in enumerate(outs):
        near, arrived, direct = ins[3 * i : 3 * i + 3]
        size = near.shape[0]
        out[:size, :] = (near[...] + arrived[...].astype(F32)).astype(BF16)
        out[size:, :] = direct[...]


def join(*triples):
    count = len(triples)
    return pl.pallas_call(
        functools.partial(join_kernel, count),
        out_shape=tuple(
            jax.ShapeDtypeStruct((2 * near.shape[0], near.shape[1]), BF16)
            for near, _, _ in triples
        ),
        compiler_params=params(),
        cost_estimate=cost(10**6, 4 * 2**20),
    )(*[one for triple in triples for one in triple])


def turn_kernel(here_a, here_b, up, down, far_up, far_down, near_up, near_down, dir_up, dir_down, a, b):
    size = 4 * ROWS

    def one(r, side):
        rows = slice(ROWS * r, ROWS * (r + 1))
        direct = slice(size + ROWS * r, size + ROWS * (r + 1))
        if side == 0:
            arrived = up[rows, :].astype(F32) + down[direct, :].astype(F32)
            return here_a[rows, :] + arrived
        arrived = down[rows, :].astype(F32) + up[direct, :].astype(F32)
        return here_b[rows, :] + arrived

    far_up[...] = one(2, 0).astype(BF16)
    far_down[...] = one(2, 1).astype(BF16)
    near_up[...] = one(1, 0)
    near_down[...] = one(3, 1)
    dir_up[...] = one(1, 1).astype(BF16)
    dir_down[...] = one(3, 0).astype(BF16)
    a[...] = one(0, 0)
    b[...] = one(0, 1)


def turn_part(here_a, here_b, up, down):
    return pl.pallas_call(
        turn_kernel,
        out_shape=tuple(
            jax.ShapeDtypeStruct((ROWS, FULL), one)
            for one in (BF16, BF16, F32, F32, BF16, BF16, F32, F32)
        ),
        compiler_params=params(),
        cost_estimate=cost(10**6, 4 * 2**20),
    )(here_a, here_b, up, down)


def last_kernel(a, b, up, down, here_u, up_u, down_u, grad_wx, grad_wbc, grad_u):
    norm = (T * SEQ) ** (-0.5)
    first = a[...] + (up[:ROWS, :].astype(F32) + down[ROWS:, :].astype(F32))
    second = b[...] + (down[:ROWS, :].astype(F32) + up[ROWS:, :].astype(F32))
    grad_wx[:, :WIDE] = first[:, :WIDE] * norm
    grad_wx[:, WIDE:] = second[:, :WIDE] * norm
    grad_wbc[:, :STATE] = first[:, WIDE:] * norm
    grad_wbc[:, STATE:] = second[:, WIDE:] * norm
    size = here_u.shape[0] // 2
    low = here_u[:size, :] + (up_u[:size, :].astype(F32) + down_u[size:, :].astype(F32))
    high = here_u[size:, :] + (down_u[:size, :].astype(F32) + up_u[size:, :].astype(F32))
    grad_u[:size, :] = low.astype(BF16)
    grad_u[size:, :] = high.astype(BF16)


def last_part(*args):
    return pl.pallas_call(
        last_kernel,
        out_shape=(
            jax.ShapeDtypeStruct((ROWS, CH), F32),
            jax.ShapeDtypeStruct((ROWS, 2 * STATE), F32),
            jax.ShapeDtypeStruct((D // ZS, T), BF16),
        ),
        compiler_params=params(),
        cost_estimate=cost(10**6, 3 * 2**20),
    )(*args)


def input_kernel(order, w_x, w_bc, grad, halo, shared, tie, *refs):
    del tie
    far_up, far_down, near_up, near_down, dir_up, dir_down, here, held, small, sems = refs
    size = D // ZS
    half = size // 2
    copies = []
    turn = (2, 1, 3, 0)
    for at, r in enumerate(turn):
        rows = pl.ds(pl.multiple_of(order[r] * size, size), size)
        copies.append(pltpu.make_async_copy(w_x.at[rows, :], held.at[at], sems.at[at]))
        copies[at].start()
    rows = pl.ds(pl.multiple_of(order[0] * size, size), size)
    last_copy = pltpu.make_async_copy(w_bc.at[rows, :], small, sems.at[ZS])
    last_copy.start()
    edge = jnp.concatenate([jnp.zeros((8, CH), F32), halo[...]], axis=0)
    last = (grad[T - 16 :, :].astype(F32) + edge).astype(BF16)
    right = jnp.concatenate([grad[: T - 16, :], last], axis=0)
    outs = ((far_up, far_down), (near_up, dir_up), (dir_down, near_down))
    for at, r in enumerate(turn):
        copies[at].wait()
        part = nt(held[at], right)
        if r == 0:
            last_copy.wait()
            here[...] = part + nt(small[...], shared[...])
        else:
            low, high = outs[at]
            low[...] = part[:half].astype(low.dtype)
            high[...] = part[half:].astype(high.dtype)


def input_part(order, w_x, w_bc, grad, halo, shared, tie):
    rows = D // ZS
    vm = pl.BlockSpec(memory_space=pltpu.VMEM)
    away = pl.BlockSpec(memory_space=pl.ANY)
    sizes = (rows // 2,) * 6 + (rows,)
    types = (BF16, BF16, F32, F32, BF16, BF16, F32)
    return pl.pallas_call(
        input_kernel,
        in_specs=[pl.BlockSpec(memory_space=pltpu.SMEM), away, away, vm, vm, vm, away],
        out_shape=tuple(jax.ShapeDtypeStruct((size, T), one) for size, one in zip(sizes, types)),
        scratch_shapes=[
            pltpu.VMEM((ZS, rows, CH), BF16),
            pltpu.VMEM((rows, 2 * STATE), BF16),
            pltpu.SemaphoreType.DMA((ZS + 1,)),
        ],
        compiler_params=params(48),
        cost_estimate=cost(2 * D * (CH + 64) * T, 10 * 2**20),
    )(order, w_x, w_bc, grad, halo, shared, tie)


def device(x, y, core):
    return ((x % 4) * 4 + y % 4) * 2 + core


def ring(first, by):
    pairs = []
    for x in range(4):
        for y in range(4):
            for core in range(2):
                along_x = (core == 0) == first
                goal = device(x + by, y, core) if along_x else device(x, y + by, core)
                pairs.append((device(x, y, core), goal))
    return pairs


def along(first, by):
    return lambda value: lax.ppermute(value, "seq", ring(first, by))


def along_head(by):
    return lambda value: lax.ppermute(value, "head", [(i, (i + by) % ZS) for i in range(ZS)])


def place_table():
    rows = []
    for place in range(SEQ):
        core, y, x = place % 2, place // 2 % 4, place // 8
        blocks = [
            [device(x + a, y + b, 0) for a in range(4) for b in range(4)],
            [device(x + b, y + a, 1) for a in range(4) for b in range(4)],
        ]
        head = SLICE * place // HEAD_DIM
        bound = HEAD_DIM * (head + 1) - SLICE * place
        rows.append(blocks[core] + blocks[1 - core] + [head, bound])
    return np.array(rows, np.int32)


def full_table():
    order = [[(z + r) % ZS for r in range(ZS)] for z in range(ZS)]
    return np.array([[list(one) + o for o in order] for one in place_table()], np.int32)


def body(normed, w_x, w_bc, conv_w, decay_code, step, d_skip, grad_y):
    place = lax.axis_index("seq")
    core = place % 2
    z = lax.axis_index("head")
    table = jnp.asarray(full_table())[place, z]
    order_z = table[34:]
    swap = [(i, i ^ 1) for i in range(SEQ)]

    before = lax.ppermute(normed[T - 16 :], "seq", [(i, i + 1) for i in range(SEQ - 1)])

    bmat, cmat, cum, logd, dyt, dywt, xgt, xlt, slope, xwt, msg = early(
        decay_code[None, :], before, normed, w_bc, step, grad_y, conv_w, w_x
    )
    recv = lax.all_to_all(msg, "seq", 0, 0)
    mine, other = select(table, normed, msg)
    other = lax.ppermute(other, "seq", swap)
    dxg, rc, dbc = intra(grad_y, dyt, xgt, cum, bmat, cmat, mine)
    back = lax.all_to_all(chain(table, recv, rc), "seq", 0, 0)

    ds, st, shared = shared_part(back, xwt, dywt, dbc)
    others = [along_head(by)(shared) for by in (1, 2, 3)]
    dpre, halo, halves, cross = gradients(
        d_skip, ds, bmat, dxg, dyt, xgt, xlt, slope, conv_w, cum, logd, st
    )
    dpre_other = lax.ppermute(dpre, "seq", swap)
    halo_mine = lax.ppermute(halo, "seq", [(i, i - 1) for i in range(1, SEQ)])
    halo_pair = lax.ppermute(halo, "seq", [(i, i - 2) for i in range(2, SEQ, 2)])
    halo_other = jnp.where(core == 0, halo_pair, halo)
    one, two, three, _ = lax.optimization_barrier((*others, halo))
    near_pair = shared.astype(F32) + two.astype(F32)
    far_pair = one.astype(F32) + three.astype(F32)
    shared = (near_pair + far_pair).astype(BF16)
    shared_other = lax.ppermute(shared, "seq", swap)

    args = (mine, other, dpre, dpre_other, halo_mine, halo_other, shared, shared_other)
    move = {by: along(True, by) for by in (1, -1)}
    turn = {by: along(False, by) for by in (1, -1)}
    head = {by: along_head(by) for by in (1, -1)}
    far_up, far_down = product_part(far_kernel, args, (), (BF16, BF16))
    ru, rd = move[1](far_up), move[-1](far_down)
    near_up, near_down, dir_up, dir_down, here_a, here_b = product_part(
        near_kernel, args, (far_up,), (F32, F32, BF16, BF16, F32, F32)
    )
    up, down = join((near_up, ru, dir_up), (near_down, rd, dir_down))
    ru, rd = move[1](up), move[-1](down)
    z_far_up, z_far_down, z_up, z_down, z_dir_up, z_dir_down, z_here = input_part(
        order_z, w_x, w_bc, dpre, halo_mine, shared, up
    )
    gls = step_part(st, ds, cmat, dyt, cum, logd, rc, halves, cross, z_here)
    far_up, far_down, near_up, near_down, dir_up, dir_down, here_a, here_b = turn_part(
        here_a, here_b, ru, rd
    )
    ru, rd = turn[1](far_up), turn[-1](far_down)
    zu, zd = head[1](z_far_up), head[-1](z_far_down)
    z_up, z_down = join((z_up, zu, z_dir_up), (z_down, zd, z_dir_down))
    zu, zd = head[1](z_up), head[-1](z_down)
    up, down = join((near_up, ru, dir_up), (near_down, rd, dir_down))
    ru, rd = turn[1](up), turn[-1](down)
    grad_wx, grad_wbc, grad_u = last_part(here_a, here_b, ru, rd, z_here, zu, zd)
    return (grad_u, grad_wx, grad_wbc, gls)


def solution(mesh):
    return jax.shard_map(
        body,
        mesh=mesh,
        in_specs=(
            P("seq", None),
            P(None, "head"),
            P(),
            P(None, "head"),
            P("head"),
            P("head", "seq"),
            P("head"),
            P("seq", "head"),
        ),
        out_specs=(P("head", "seq"), P("seq", "head"), P("seq", None), P("head", "seq")),
        check_vma=False,
    )
```
